128 devices in a mesh: lat: 8 (over x, core), lon: 16 (over y, z).
Axes of the slice: x: 4, y: 4, z: 4, core: 2. Of those that a mesh axis runs over, the one named last changes fastest.
Arguments:
- grid_tokens: bfloat16 [128, 256, 512], P('lat', 'lon'), may hold values from -30 to 30
- obs_tokens: bfloat16 [2048, 128, 512], P(('lat', 'lon')), may hold values from -30 to 30
- destinations: int32 [2048, 1], P(('lat', 'lon')), may hold values from 0 to 15; in each aligned block of 16 rows (0 to 15, 16 to 31, ...) at most 2 rows name the same one
- valid_counts: int32 [128, 16], P(('lat', 'lon')), may hold values from 1 to 128, 1536 in all within a row
- w_query: bfloat16 [512, 512], replicated, may hold values from -0.25 to 0.25
- w_key: bfloat16 [512, 512], replicated, may hold values from -0.25 to 0.25
- w_value: bfloat16 [512, 512], replicated, may hold values from -0.25 to 0.25
- w_out: bfloat16 [512, 512], replicated, may hold values from -0.25 to 0.25
- stencil_taps: float32 [5, 512], replicated, may hold values from -3 to 3
- cotangent: bfloat16 [128, 256, 512], P('lat', 'lon'), may hold values from -6 to 6
Outputs:
- encoded: bfloat16 [128, 256, 512], P('lat', 'lon')
- grad_grid: bfloat16 [128, 256, 512], P('lat', 'lon')
- grad_obs: bfloat16 [2048, 128, 512], P(('lat', 'lon'))
- grad_w_query: float32 [512, 512], replicated
- grad_w_key: float32 [512, 512], replicated
- grad_w_value: float32 [512, 512], replicated
- grad_w_out: float32 [512, 512], replicated
- grad_taps: float32 [5, 512], replicated
The draws below stay inside these ranges and needn't reach their ends.
Inputs may be any that keep to these rules, and one draw needn't show every extreme that they name: `destinations`: within one ingest device's 16 blocks no tile column is named more than 2 times, and some device names one exactly 2 times. `valid_counts`: each ingest device's 16 counts sum to 1536, and one of them is 128.
All inputs are finite; a program needn't handle non-finite values.
Results may differ from the reference program's by a relative error of at most 0.012.
The reference program's roundings to bfloat16 on the way count: a program that leaves them out, or rounds other values in their place, can miss the bound.
Values may be sent and summed in bfloat16 or wider, within the bound.
A program may use at most 192 MiB of HBM per device.

```python
import math
import jax
import jax.numpy as jnp
import numpy as np
from jax import lax

D = 512
HEADS = 8
TLAT = 16
TLON = 16
NB_DEV = 16
BLK = 128
CAP = 2
GT = 256
SLOTS = 32
INGESTS = 128
NLAT_CELLS = 128
NLON_CELLS = 256
OBS_BLOCKS = 2048
FILLED = 1536
N_LAT = 8
N_LON = 16


def draw_grid_tokens(key, part):
    key = jax.random.fold_in(key, 11)
    noise_key = jax.random.fold_in(key, 0)
    extent = (NLAT_CELLS, NLON_CELLS, D)
    values = jnp.clip(jax.random.normal(noise_key, extent, jnp.float32), -6.0, 6.0)
    return values.astype(jnp.bfloat16)


def draw_obs_tokens(key, part):
    key = jax.random.fold_in(key, 12)
    noise_key = jax.random.fold_in(key, 0)
    extent = (OBS_BLOCKS, BLK, D)
    values = jnp.clip(jax.random.normal(noise_key, extent, jnp.float32), -6.0, 6.0)
    return values.astype(jnp.bfloat16)


def steps_of(rng, shape, shards, least, high):
    gain = 1.0
    for axis_at, parts in shards:
        heights = jax.random.uniform(jax.random.fold_in(jax.random.fold_in(rng, 6), axis_at), (parts,), jnp.float32, least / len(shards), high / len(shards))
        gain = gain * jnp.repeat(jnp.exp(heights), shape[axis_at] // parts).reshape((-1,) + (1,) * (len(shape) - 1 - axis_at))
    return gain


def split_up(count, total, most, skew):
    loads = [(1 << 20) // math.isqrt(rank ** skew) + 1 for rank in range(2, count + 1)]
    spare, given = total - most - (count - 1), [1] * (count - 1)
    while spare > 0:
        candidates = [i for i in range(count - 1) if given[i] < most]
        pool, left = sum([loads[i] for i in candidates]), spare
        for i in candidates:
            extra = min(most - given[i], max(1, left * loads[i] // pool), spare)
            given[i] = given[i] + extra
            spare = spare - extra
    return np.array([most] + given)


def uneven(stream_key, amount, total, reach, lean):
    if amount == 2:
        one = jax.random.randint(stream_key, (), max(1, total - reach), min(reach, total - 1) + 1)
        return jnp.stack([one, total - one])
    tallies = jnp.asarray(split_up(amount, total, reach, lean), jnp.int32)
    twos = (amount - 1) // 2
    source_of, taker = tallies[1:1 + 2 * twos:2], tallies[2:2 + 2 * twos:2]
    slack = jnp.minimum(source_of - 1, reach - taker)
    moved = jax.random.randint(jax.random.fold_in(stream_key, 1), (twos,), 0, 1 << 20) % (slack + 1)
    tallies = tallies.at[1:1 + 2 * twos:2].set(source_of - moved).at[2:2 + 2 * twos:2].set(taker + moved)
    return tallies[jax.random.permutation(jax.random.fold_in(stream_key, 2), amount)]


def deal_out(key, own, number, rows, count, top, bound, lean):
    order = jax.random.permutation(key, count)
    crowded, usual = load_shares(count, rows * top, bound, lean, True), load_shares(count, rows * top, bound, lean, False)
    places = jnp.arange(count)

    def named(sizes, offset_by):
        used = int((sizes > 0).sum())
        fixed = max(1, used // 4)
        shifted = fixed + (places - fixed + offset_by * (used - fixed)) % max(1, count - fixed)
        return jnp.zeros((count,), jnp.int32).at[order[jnp.where(places < fixed, places, shifted)]].set(jnp.asarray(sizes, jnp.int32))

    sizes = jnp.where(number % 4 == 0, named(crowded, number // 4), named(usual, number - number // 4 - 1))
    mixed = jax.random.permutation(jax.random.fold_in(own, 3), count)
    giver, receiver = mixed[0:count // 2 * 2:2], mixed[1:count // 2 * 2:2]
    room = jnp.minimum(sizes[giver] - 1, bound - sizes[receiver]) // 2
    room = jnp.where((giver == order[0]) | (receiver == order[0]) | (sizes[receiver] == 0), 0, jnp.maximum(room, 0))
    shifted = jax.random.randint(jax.random.fold_in(own, 4), (count // 2,), 0, 1 << 20) % (room + 1)
    sizes = sizes.at[giver].add(-shifted).at[receiver].add(shifted)
    labels = jnp.searchsorted(jnp.cumsum(sizes), jnp.arange(rows * top), side="right").astype(jnp.int32)
    grid = labels.reshape(top, rows).T
    grid = grid[jax.random.permutation(jax.random.fold_in(own, 1), rows)]
    offset_by = jax.random.randint(jax.random.fold_in(own, 2), (rows, 1), 0, top)
    return jnp.take_along_axis(grid, (jnp.arange(top)[None, :] + offset_by) % top, axis=1)


def load_shares(amount, total, reach, skew, full):
    loads = [(1 << 20) // math.isqrt(rank ** skew) + 1 for rank in range(1, amount + 1)]
    largest = reach if full else min(reach, max(-(-total // amount), total * loads[0] // sum(loads)))
    least = 1 if total - largest >= amount - 1 else 0
    counts, rest = [largest] + [least] * (amount - 1), total - largest - least * (amount - 1)
    while rest > 0:
        free = [i for i in range(1, amount) if counts[i] < largest] or [i for i in range(1, amount) if counts[i] < reach]
        whole, remaining = sum([loads[i] for i in free]), rest
        for i in free:
            more = min(reach - counts[i], max(1, remaining * loads[i] // whole), rest)
            counts[i] = counts[i] + more
            rest = rest - more
    return np.array(counts)


def gaussian(rng, shape, spread, most, cuts=(), kind=jnp.bfloat16):
    result = spread * jax.random.normal(rng, shape, jnp.float32)
    if cuts:
        result = result * steps_of(rng, shape, cuts, -0.22, 0.18)
    return jnp.clip(result, -most, most).astype(kind)


def setup_inputs(seed: int = 0) -> dict:
    arg_keys = jax.random.split(jax.random.key(seed), 11)
    grid_tokens = draw_grid_tokens(jax.random.fold_in(arg_keys[10], 71), 0)
    obs_tokens = draw_obs_tokens(jax.random.fold_in(arg_keys[10], 71), 0)
    destinations_keys = jax.random.split(jax.random.fold_in(arg_keys[2], 1), OBS_BLOCKS // NB_DEV)
    destinations_turns = jax.random.permutation(jax.random.fold_in(arg_keys[2], 3), OBS_BLOCKS // NB_DEV)
    destinations = jax.vmap(lambda own, number: deal_out(jax.random.fold_in(arg_keys[2], 2), own, number, NB_DEV, N_LON, 1, CAP, 2))(destinations_keys, destinations_turns).reshape((OBS_BLOCKS, 1))
    valid_counts = jax.vmap(lambda own: uneven(own, NB_DEV, FILLED, BLK, 1))(jax.random.split(arg_keys[3], INGESTS)).reshape((INGESTS, NB_DEV)).astype(jnp.int32)
    w_query = gaussian(arg_keys[4], (D, D), D ** -0.5, 0.25)
    w_key = gaussian(arg_keys[5], (D, D), D ** -0.5, 0.25)
    w_value = gaussian(arg_keys[6], (D, D), D ** -0.5, 0.25)
    w_out = gaussian(arg_keys[7], (D, D), D ** -0.5, 0.25)
    stencil_taps = gaussian(arg_keys[8], (5, D), 0.3, 3.0, (), jnp.float32)
    cotangent = gaussian(arg_keys[9], (NLAT_CELLS, NLON_CELLS, D), 1.0, 6.0, ((0, 8), (1, 16)))
    return {"grid_tokens": grid_tokens, "obs_tokens": obs_tokens, "destinations": destinations, "valid_counts": valid_counts, "w_query": w_query, "w_key": w_key, "w_value": w_value, "w_out": w_out, "stencil_taps": stencil_taps, "cotangent": cotangent}


def product(former, latter):
    return jnp.dot(former.astype(jnp.float32), latter.astype(jnp.float32), precision=lax.Precision.HIGHEST)


def product_tn(former, latter):
    return lax.dot_general(former.astype(jnp.float32), latter.astype(jnp.float32), (((0,), (0,)), ((), ())), precision=lax.Precision.HIGHEST)


def product_nt(former, latter):
    return lax.dot_general(former.astype(jnp.float32), latter.astype(jnp.float32), (((1,), (1,)), ((), ())), precision=lax.Precision.HIGHEST)


def rounded(values):
    return lax.optimization_barrier(values.astype(jnp.bfloat16)).astype(jnp.float32)


def head_slices(source, number, column_span):
    picked = lax.dynamic_slice_in_dim(source, number * column_span, column_span, 1)
    return picked.reshape(source.shape[0], 2, column_span // 2).astype(jnp.float32)


def pair_weights(query_pair, key_pair, live_keys, scaling):
    scores = jnp.einsum("qhd,khd->hqk", query_pair, key_pair, precision=lax.Precision.HIGHEST) * scaling
    scores = jnp.where(live_keys[None, None, :], scores, -1e30)
    largest = jnp.max(scores, 2, keepdims=True)
    raised = jnp.exp(scores - largest)
    return raised / jnp.sum(raised, 2, keepdims=True)


def rejoin(pieces):
    return pieces.transpose(1, 0, 2).reshape(pieces.shape[1], pieces.shape[0] * pieces.shape[2])


def attend(queries, key_rows, value_rows, live_keys):
    column_span = 2 * (D // HEADS)
    scaling = (D // HEADS) ** -0.5

    def one_pair(number):
        query_pair = head_slices(queries, number, column_span)
        key_pair = head_slices(key_rows, number, column_span)
        value_pair = head_slices(value_rows, number, column_span)
        weights = pair_weights(query_pair, key_pair, live_keys, scaling)
        mixture = jnp.einsum("hqk,khd->qhd", rounded(weights), value_pair, precision=lax.Precision.HIGHEST)
        return mixture.reshape(queries.shape[0], column_span).astype(jnp.bfloat16)

    return rejoin(lax.map(one_pair, jnp.arange(HEADS // 2, dtype=jnp.int32)))


def attend_back(queries, key_rows, value_rows, live_keys, upstream):
    column_span = 2 * (D // HEADS)
    scaling = (D // HEADS) ** -0.5

    def one_pair(number):
        query_pair = head_slices(queries, number, column_span)
        key_pair = head_slices(key_rows, number, column_span)
        value_pair = head_slices(value_rows, number, column_span)
        grad_pair = head_slices(upstream, number, column_span)
        weights = pair_weights(query_pair, key_pair, live_keys, scaling)
        grad_weights = jnp.einsum("qhd,khd->hqk", grad_pair, value_pair, precision=lax.Precision.HIGHEST)
        inner_sum = jnp.sum(weights * grad_weights, 2, keepdims=True)
        grad_scores = rounded(weights * (grad_weights - inner_sum) * scaling)
        grad_query = jnp.einsum("hqk,khd->qhd", grad_scores, key_pair, precision=lax.Precision.HIGHEST)
        grad_key = jnp.einsum("hqk,qhd->khd", grad_scores, query_pair, precision=lax.Precision.HIGHEST)
        grad_value = jnp.einsum("hqk,qhd->khd", rounded(weights), grad_pair, precision=lax.Precision.HIGHEST)
        return (grad_query.reshape(queries.shape[0], column_span).astype(jnp.bfloat16),
                grad_key.reshape(key_rows.shape[0], column_span).astype(jnp.bfloat16),
                grad_value.reshape(key_rows.shape[0], column_span).astype(jnp.bfloat16))

    query_parts, key_parts, value_parts = lax.map(one_pair, jnp.arange(HEADS // 2, dtype=jnp.int32))
    return rejoin(query_parts), rejoin(key_parts), rejoin(value_parts)


def to_tiles(gridded):
    return gridded.reshape(N_LAT, TLAT, N_LON, TLON, gridded.shape[-1]).transpose(0, 2, 1, 3, 4).reshape(INGESTS, TLAT * TLON, gridded.shape[-1])


def from_tiles(tiled):
    return tiled.reshape(N_LAT, N_LON, TLAT, TLON, tiled.shape[-1]).transpose(0, 2, 1, 3, 4).reshape(N_LAT * TLAT, N_LON * TLON, tiled.shape[-1])


def neighbours(gridded):
    zero_row = jnp.zeros_like(gridded[:1])
    northern = jnp.concatenate([zero_row, gridded[:-1]], 0)
    southern = jnp.concatenate([gridded[1:], zero_row], 0)
    western = jnp.roll(gridded, 1, axis=1)
    eastern = jnp.roll(gridded, -1, axis=1)
    return northern, southern, western, eastern


def receive_lists(destinations, valid_counts):
    target = destinations[:, 0].reshape(INGESTS, NB_DEV)
    order_ids = jnp.arange(NB_DEV, dtype=jnp.int32)
    earlier = (target[:, :, None] == target[:, None, :]) & (order_ids[None, None, :] < order_ids[None, :, None])
    rank_ids = jnp.sum(earlier.astype(jnp.int32), 2)
    slot_ids = target * CAP + rank_ids
    chooser = slot_ids[:, None, :] == jnp.arange(N_LON * CAP, dtype=jnp.int32)[None, :, None]
    which_block = jnp.sum(jnp.where(chooser, order_ids[None, None, :], 0), 2)
    present = jnp.any(chooser, 2)
    filled = jnp.sum(jnp.where(chooser, valid_counts[:, None, :], 0), 2)
    sources = jnp.arange(INGESTS, dtype=jnp.int32)[:, None] * NB_DEV + which_block

    def regroup(table):
        return table.reshape(N_LAT, N_LON, N_LON, CAP).transpose(0, 2, 1, 3).reshape(INGESTS, N_LON * CAP)

    return regroup(sources), regroup(present), regroup(filled)


def reference(grid_tokens, obs_tokens, destinations, valid_counts, w_query, w_key, w_value, w_out, stencil_taps, cotangent):
    w_pair = jnp.concatenate([w_key, w_value], 1)
    tiled = to_tiles(grid_tokens)
    flat_grid = tiled.reshape(INGESTS * GT, D)
    queries = product(flat_grid, w_query).astype(jnp.bfloat16).reshape(INGESTS, GT, D)
    own_pairs = product(flat_grid, w_pair).astype(jnp.bfloat16).reshape(INGESTS, GT, 2 * D)
    obs_flat = obs_tokens.reshape(OBS_BLOCKS * BLK, D)
    obs_pairs = product(obs_flat, w_pair).astype(jnp.bfloat16).reshape(OBS_BLOCKS, BLK, 2 * D)
    sources, present, filled = receive_lists(destinations, valid_counts)
    positions = jnp.arange(BLK, dtype=jnp.int32)
    tile_ids = jnp.arange(INGESTS, dtype=jnp.int32)

    def tile_keys(tile_id):
        picked = obs_pairs[sources[tile_id]] * present[tile_id][:, None, None].astype(jnp.bfloat16)
        live_obs = (positions[None, :] < filled[tile_id][:, None]).reshape(SLOTS * BLK)
        paired = jnp.concatenate([own_pairs[tile_id], picked.reshape(SLOTS * BLK, 2 * D)], 0)
        live_keys = jnp.concatenate([jnp.ones((GT,), jnp.bool_), live_obs])
        return paired[:, :D], paired[:, D:], live_keys

    def forward_tile(tile_id):
        key_rows, value_rows, live_keys = tile_keys(tile_id)
        return attend(queries[tile_id], key_rows, value_rows, live_keys)

    attended = lax.map(forward_tile, tile_ids)
    flat_att = attended.reshape(INGESTS * GT, D)
    middle = (flat_grid.astype(jnp.float32) + product(flat_att, w_out)).astype(jnp.bfloat16)
    mid_grid = from_tiles(middle.reshape(INGESTS, GT, D)).astype(jnp.float32)
    northern, southern, western, eastern = neighbours(mid_grid)
    encoded = ((1.0 + stencil_taps[0]) * mid_grid + stencil_taps[1] * northern + stencil_taps[2] * southern
               + stencil_taps[3] * western + stencil_taps[4] * eastern).astype(jnp.bfloat16)
    upstream = cotangent.astype(jnp.float32)
    up_north, up_south, up_west, up_east = neighbours(upstream)
    grad_middle = ((1.0 + stencil_taps[0]) * upstream + stencil_taps[1] * up_south + stencil_taps[2] * up_north
                   + stencil_taps[3] * up_east + stencil_taps[4] * up_west).astype(jnp.bfloat16)
    grad_taps = jnp.stack([jnp.sum(upstream * mid_grid, (0, 1)), jnp.sum(upstream * northern, (0, 1)),
                           jnp.sum(upstream * southern, (0, 1)), jnp.sum(upstream * western, (0, 1)),
                           jnp.sum(upstream * eastern, (0, 1))])
    grad_tiles = to_tiles(grad_middle).reshape(INGESTS * GT, D)
    grad_w_out = product_tn(flat_att, grad_tiles)
    grad_attended = product_nt(grad_tiles, w_out).astype(jnp.bfloat16).reshape(INGESTS, GT, D)

    def backward_tile(carried, tile_id):
        key_rows, value_rows, live_keys = tile_keys(tile_id)
        grad_query, grad_key, grad_value = attend_back(queries[tile_id], key_rows, value_rows, live_keys, grad_attended[tile_id])
        grad_pairs = jnp.concatenate([grad_key, grad_value], 1)
        obs_part = grad_pairs[GT:].reshape(SLOTS, BLK, 2 * D) * present[tile_id][:, None, None].astype(jnp.bfloat16)
        carried = carried.at[sources[tile_id]].add(obs_part)
        return carried, (grad_query, grad_pairs[:GT])

    start_grads = jnp.zeros((OBS_BLOCKS, BLK, 2 * D), jnp.bfloat16)
    obs_grads, (grad_queries, own_grads) = lax.scan(backward_tile, start_grads, tile_ids)
    grad_queries = grad_queries.reshape(INGESTS * GT, D)
    own_grads = own_grads.reshape(INGESTS * GT, 2 * D)
    grad_flat = grad_tiles.astype(jnp.float32) + product_nt(grad_queries, w_query) + product_nt(own_grads, w_pair)
    grad_grid = from_tiles(grad_flat.astype(jnp.bfloat16).reshape(INGESTS, GT, D))
    flat_obs_grads = obs_grads.reshape(OBS_BLOCKS * BLK, 2 * D)
    grad_obs = product_nt(flat_obs_grads, w_pair).astype(jnp.bfloat16).reshape(OBS_BLOCKS, BLK, D)
    grad_w_query = product_tn(flat_grid, grad_queries)
    grad_w_pair = product_tn(flat_grid, own_grads) + product_tn(obs_flat, flat_obs_grads)
    return (encoded, grad_grid, grad_obs, grad_w_query, grad_w_pair[:, :D], grad_w_pair[:, D:], grad_w_out, grad_taps)
```

```python
import functools

import jax
import jax.numpy as jnp
from jax import lax
from jax.experimental import pallas as pl
from jax.experimental.pallas import tpu as pltpu
from jax.sharding import PartitionSpec as P

D = 512
HEADS = 8
HD = D // HEADS
BLK = 128
CAP = 2
ROWS = CAP * BLK
CELLS = 256
SCALING = HD ** (-0.5)
MESH = pl.DeviceIdType.MESH
BF = jnp.bfloat16
F32 = jnp.float32


def padded(cells, sides, width, closed):
    for axis, dim in sides:
        count = lax.axis_size(axis)
        ends = count if closed else count - 1
        head = lax.slice_in_dim(cells, 0, width, axis=dim)
        tail = lax.slice_in_dim(cells, cells.shape[dim] - width, cells.shape[dim], axis=dim)
        cells = jnp.concatenate(
            [
                lax.ppermute(tail, axis, [(i, (i + 1) % count) for i in range(ends)]),
                cells,
                lax.ppermute(head, axis, [((i + 1) % count, i) for i in range(ends)]),
            ],
            axis=dim,
        )
    return cells


def dot(a, b):
    return jnp.dot(a, b, preferred_element_type=F32)


def dot_nt(a, b):
    return lax.dot_general(a, b, (((1,), (1,)), ((), ())), preferred_element_type=F32)


def attention_kernel(
    n, blk_ref, cnt_ref, slot_ref, obs_ref, grid_ref, gm_ref, wq_ref, wk_ref, wv_ref, wo_ref,
    mid_ref, gobs_ref, ggrid_ref, dwq_ref, dwkv_ref, dwo_ref,
    send, xs, ret, cnt_send, cnt_recv, kv, kt, vt, xt, bias, wkv, wkvt, qz, qzt, doz, dozt, dot_t,
    acc_o, acc_q, m_ref, l_ref, d_ref, dkv, dxo, own,
    x_ssem, x_rsem, c_ssem, c_rsem, g_ssem, g_rsem,
):
    me = lax.axis_index("lon")
    chunks = n + 1

    def peer(d):
        return {"lon": lax.rem(me + d, n)}

    barrier = pltpu.get_barrier_semaphore()

    def greet(d, carry):
        pl.semaphore_signal(barrier, inc=1, device_id=peer(d), device_id_type=MESH)
        return carry

    lax.fori_loop(1, n, greet, 0)

    row_ids = lax.broadcasted_iota(jnp.int32, (8, CELLS), 0)

    def pack(d, carry):
        s = 2 * d
        send[d, 0] = obs_ref[blk_ref[s]]
        send[d, 1] = obs_ref[blk_ref[s + 1]]
        cnt_send[d] = jnp.where(row_ids == 0, cnt_ref[s], cnt_ref[s + 1]).astype(F32)
        return carry

    lax.fori_loop(0, n, pack, 0)
    pl.semaphore_wait(barrier, n - 1)

    def x_copy(d):
        return pltpu.make_async_remote_copy(
            src_ref=send.at[d], dst_ref=xs.at[d + 1], send_sem=x_ssem.at[d], recv_sem=x_rsem.at[d],
            device_id=peer(d), device_id_type=MESH,
        )

    def c_copy(d):
        return pltpu.make_async_remote_copy(
            src_ref=cnt_send.at[d], dst_ref=cnt_recv.at[d], send_sem=c_ssem.at[d], recv_sem=c_rsem.at[d],
            device_id=peer(d), device_id_type=MESH,
        )

    def g_copy(d):
        return pltpu.make_async_remote_copy(
            src_ref=send.at[d], dst_ref=ret.at[pl.ds(CAP * d, CAP)], send_sem=g_ssem.at[d], recv_sem=g_rsem.at[d],
            device_id=peer(n - d), device_id_type=MESH,
        )

    def ship(d, carry):
        c_copy(d).start()
        x_copy(d).start()
        return carry

    lax.fori_loop(1, n, ship, 0)

    xs[0] = grid_ref[...].reshape(CAP, BLK, D)
    xs[1] = send[0]
    cnt_recv[0] = cnt_send[0]
    wkv[:, :D] = wk_ref[...]
    wkv[:, D:] = wv_ref[...]
    wkvt[:D, :] = wk_ref[...].astype(F32).T.astype(BF)
    wkvt[D:, :] = wv_ref[...].astype(F32).T.astype(BF)
    lanes = lax.broadcasted_iota(jnp.int32, (CELLS, 2 * HD), 1)
    queries = dot(grid_ref[...], wq_ref[...]).astype(BF).astype(F32) * SCALING
    ups = dot_nt(gm_ref[...], wo_ref[...]).astype(BF).astype(F32)
    dot_t[...] = ups.T
    for h in range(HEADS):
        p, e = h // 2, h % 2
        mine = (lanes >= HD) if e else (lanes < HD)
        picked = jnp.where(mine, queries[:, p * 2 * HD : (p + 1) * 2 * HD], 0.0)
        qz[h] = picked.astype(BF)
        qzt[h] = picked.T.astype(BF)
        picked = jnp.where(mine, ups[:, p * 2 * HD : (p + 1) * 2 * HD], 0.0)
        doz[h] = picked.astype(BF)
        dozt[h] = picked.T.astype(BF)
    bias[0] = jnp.zeros((ROWS, CELLS), F32)
    acc_o[...] = jnp.zeros_like(acc_o)
    acc_q[...] = jnp.zeros_like(acc_q)
    dwkv_ref[...] = jnp.zeros_like(dwkv_ref)
    m_ref[...] = jnp.full(m_ref.shape, -1e30, F32)
    l_ref[...] = jnp.zeros_like(l_ref)
    key_ids = lax.broadcasted_iota(jnp.int32, (BLK, CELLS), 0).astype(F32)

    def forward(c, carry):
        @pl.when(c >= 2)
        def _():
            c_copy(c - 1).wait_recv()
            x_copy(c - 1).wait_recv()

        @pl.when(c >= 1)
        def _():
            tile = cnt_recv[c - 1]
            bias[c, 0:BLK, :] = jnp.where(key_ids < tile[0:1, :], 0.0, -1e30)
            bias[c, BLK:ROWS, :] = jnp.where(key_ids < tile[1:2, :], 0.0, -1e30)

        for j in range(4):
            cols = slice(j * 256, (j + 1) * 256)
            part = dot(xs[c].reshape(ROWS, D), wkv[:, cols]).astype(BF)
            kv[c, :, cols] = part
            if j < 2:
                kt[c, cols, :] = part.T
            else:
                vt[j * 256 - D : (j + 1) * 256 - D, :] = part.T

        def pair(p, inner):
            keys = kv[c, :, pl.ds(pl.multiple_of(p * 128, 128), 128)]
            for e in range(2):
                h = 2 * p + e
                rows = pl.ds(pl.multiple_of(h * HD, HD), HD)
                scores = dot(keys, qzt[h]) + bias[c]
                old = m_ref[h]
                new = jnp.maximum(old, jnp.max(scores, 0, keepdims=True))
                raised = jnp.exp(scores - new)
                shrink = jnp.exp(old - new)
                l_ref[h] = l_ref[h] * shrink + jnp.sum(raised, 0, keepdims=True)
                m_ref[h] = new
                acc_o[rows, :] = acc_o[rows, :] * shrink + dot(vt[rows, :], raised.astype(BF))
            return inner

        lax.fori_loop(0, HEADS // 2, pair, 0)
        return carry

    lax.fori_loop(0, chunks, forward, 0)

    def finish(h, carry):
        rows = pl.ds(pl.multiple_of(h * HD, HD), HD)
        total = l_ref[h]
        mixed = acc_o[rows, :] / total
        acc_o[rows, :] = mixed
        m_ref[h] = m_ref[h] + jnp.log(total)
        d_ref[h] = jnp.sum(mixed * dot_t[rows, :], 0, keepdims=True)
        return carry

    lax.fori_loop(0, HEADS, finish, 0)
    attended = acc_o[...].astype(BF)
    mid_ref[...] = (
        grid_ref[...].astype(F32) + dot(acc_o[...].T.astype(BF), wo_ref[...])
    ).astype(BF)
    dwo_ref[...] = dot(attended, gm_ref[...])

    def sent(d, carry):
        c_copy(d).wait_send()
        x_copy(d).wait_send()
        return carry

    lax.fori_loop(1, n, sent, 0)

    def backward(step, carry):
        c = lax.rem(step + 2, chunks)

        def pair(p, inner):
            here = pl.ds(pl.multiple_of(p * 128, 128), 128)
            there = pl.ds(pl.multiple_of(D + p * 128, 128), 128)
            keys = kv[c, :, here]
            values = kv[c, :, there]
            grad_k = jnp.zeros((ROWS, 128), F32)
            grad_v = jnp.zeros((ROWS, 128), F32)
            for e in range(2):
                h = 2 * p + e
                rows = pl.ds(pl.multiple_of(h * HD, HD), HD)
                weights = jnp.exp(dot(keys, qzt[h]) + bias[c] - m_ref[h])
                grads = (weights * (dot(values, dozt[h]) - d_ref[h])).astype(BF)
                grad_k = grad_k + dot(grads, qz[h])
                grad_v = grad_v + dot(weights.astype(BF), doz[h])
                acc_q[rows, :] += dot(kt[c, rows, :], grads)
            dkv[:, here] = grad_k.astype(BF)
            dkv[:, there] = grad_v.astype(BF)
            return inner

        lax.fori_loop(0, HEADS // 2, pair, 0)
        xt[...] = xs[c].reshape(ROWS, D).T
        for j in range(4):
            cols = slice(j * 256, (j + 1) * 256)
            dwkv_ref[:, cols] += dot(xt[...], dkv[:, cols])
        for j in range(2):
            cols = slice(j * 256, (j + 1) * 256)
            dxo[:, cols] = dot(dkv[...], wkvt[:, cols])

        @pl.when(c == 0)
        def _():
            own[...] = dxo[...]

        @pl.when(c == 1)
        def _():
            ret[0:CAP] = dxo[...].astype(BF).reshape(CAP, BLK, D)

        @pl.when(c >= 2)
        def _():
            send[c - 1] = dxo[...].astype(BF).reshape(CAP, BLK, D)
            g_copy(c - 1).start()

        return carry

    lax.fori_loop(0, chunks, backward, 0)

    grad_q = (acc_q[...].T * SCALING).astype(BF)
    ggrid_ref[...] = (
        gm_ref[...].astype(F32) + dot_nt(grad_q, wq_ref[...]) + own[...]
    ).astype(BF)
    dwq_ref[...] = dot(grid_ref[...].T, grad_q)

    def returned(d, carry):
        g_copy(d).wait_recv()
        g_copy(d).wait_send()
        return carry

    lax.fori_loop(1, n, returned, 0)

    def unpack(b, carry):
        gobs_ref[b] = ret[slot_ref[b]]
        return carry

    lax.fori_loop(0, gobs_ref.shape[0], unpack, 0)


def attention(n, tables, obs, grid, grad_mid, weights):
    vmem = pl.BlockSpec(memory_space=pltpu.VMEM)
    smem = pl.BlockSpec(memory_space=pltpu.SMEM)
    blocks = obs.shape[0]
    dma = pltpu.SemaphoreType.DMA((n,))
    return pl.pallas_call(
        functools.partial(attention_kernel, n),
        out_shape=(
            jax.ShapeDtypeStruct((CELLS, D), BF),
            jax.ShapeDtypeStruct((blocks, BLK, D), BF),
            jax.ShapeDtypeStruct((CELLS, D), BF),
            jax.ShapeDtypeStruct((D, D), F32),
            jax.ShapeDtypeStruct((D, 2 * D), F32),
            jax.ShapeDtypeStruct((D, D), F32),
        ),
        in_specs=[smem] * 3 + [vmem] * 7,
        out_specs=(vmem,) * 6,
        scratch_shapes=[
            pltpu.VMEM((n, CAP, BLK, D), BF),
            pltpu.VMEM((n + 1, CAP, BLK, D), BF),
            pltpu.VMEM((n * CAP, BLK, D), BF),
            pltpu.VMEM((n, 8, CELLS), F32),
            pltpu.VMEM((n, 8, CELLS), F32),
            pltpu.VMEM((n + 1, ROWS, 2 * D), BF),
            pltpu.VMEM((n + 1, D, ROWS), BF),
            pltpu.VMEM((D, ROWS), BF),
            pltpu.VMEM((D, ROWS), BF),
            pltpu.VMEM((n + 1, ROWS, CELLS), F32),
            pltpu.VMEM((D, 2 * D), BF),
            pltpu.VMEM((2 * D, D), BF),
            pltpu.VMEM((HEADS, CELLS, 2 * HD), BF),
            pltpu.VMEM((HEADS, 2 * HD, CELLS), BF),
            pltpu.VMEM((HEADS, CELLS, 2 * HD), BF),
            pltpu.VMEM((HEADS, 2 * HD, CELLS), BF),
            pltpu.VMEM((D, CELLS), F32),
            pltpu.VMEM((D, CELLS), F32),
            pltpu.VMEM((D, CELLS), F32),
            pltpu.VMEM((HEADS, 1, CELLS), F32),
            pltpu.VMEM((HEADS, 1, CELLS), F32),
            pltpu.VMEM((HEADS, 1, CELLS), F32),
            pltpu.VMEM((ROWS, 2 * D), BF),
            pltpu.VMEM((ROWS, D), F32),
            pltpu.VMEM((ROWS, D), F32),
            dma, dma, dma, dma, dma, dma,
        ],
        compiler_params=pltpu.CompilerParams(
            collective_id=0, has_side_effects=True, vmem_limit_bytes=60 * 2**20
        ),
        name="attention",
    )(*tables, obs, grid, grad_mid, *weights)


def sum_kernel(
    nlat, nlon, dwq_ref, dwkv_ref, dwo_ref, taps_ref, wq_out, wk_out, wv_out, wo_out, taps_out,
    a0, b0, a1, b1, a2, b2, a3, b3, a4, b4, t0, t1,
    a1s, a1r, b1s, b1r, a2s, a2r, b2s, b2r, a3s, a3r, b3s, b3r, a4s, a4r, b4s, b4r,
    t1s, t1r, t2s, t2r,
):
    sizes = {"lat": nlat, "lon": nlon}
    place = {axis: lax.axis_index(axis) for axis in sizes}
    barrier = pltpu.get_barrier_semaphore()

    def every(axis, body):
        count, me = sizes[axis], place[axis]

        def step(o, carry):
            body(lax.rem(me + o, count))
            return carry

        lax.fori_loop(1, count, step, 0)

    for axis in sizes:
        every(axis, lambda at, axis=axis: pl.semaphore_signal(
            barrier, inc=1, device_id={axis: at}, device_id_type=MESH))

    def piece(j):
        rows = pl.ds(pl.multiple_of((j // 2) * 16, 16), 16)
        cols = pl.ds(pl.multiple_of(lax.rem(j, 2) * 256, 256), 256)
        return rows, cols

    def cut(j, carry):
        rows, cols = piece(j)
        right = pl.ds(pl.multiple_of(D + lax.rem(j, 2) * 256, 256), 256)
        low, high = j, j + 64
        a0[low // nlon, lax.rem(low, nlon)] = dwq_ref[rows, cols].astype(BF)
        a0[high // nlon, lax.rem(high, nlon)] = dwkv_ref[rows, cols].astype(BF)
        b0[low // nlat, lax.rem(low, nlat)] = dwkv_ref[rows, right].astype(BF)
        b0[high // nlat, lax.rem(high, nlat)] = dwo_ref[rows, cols].astype(BF)
        return carry

    lax.fori_loop(0, 64, cut, 0)
    t0[place["lat"]] = taps_ref[...]
    pl.semaphore_wait(barrier, nlat + nlon - 2)

    def scatter(axis, src, dst, ssem, rsem):
        me = place[axis]

        def copy(to, frm):
            return pltpu.make_async_remote_copy(
                src_ref=src.at[to], dst_ref=dst.at[frm], send_sem=ssem.at[to], recv_sem=rsem.at[frm],
                device_id={axis: to}, device_id_type=MESH,
            )

        return (
            lambda: every(axis, lambda at: copy(at, me).start()),
            lambda: every(axis, lambda at: copy(at, at).wait_recv()),
            lambda: every(axis, lambda at: copy(at, me).wait_send()),
        )

    def gather(axis, buf, ssem, rsem):
        me = place[axis]

        def copy(to, frm):
            return pltpu.make_async_remote_copy(
                src_ref=buf.at[me], dst_ref=buf.at[frm], send_sem=ssem.at[to], recv_sem=rsem.at[frm],
                device_id={axis: to}, device_id_type=MESH,
            )

        return (
            lambda: every(axis, lambda at: copy(at, me).start()),
            lambda: every(axis, lambda at: copy(at, at).wait_recv()),
            lambda: every(axis, lambda at: copy(at, me).wait_send()),
        )

    def total(axis, src, dst):
        value = src[place[axis]].astype(F32)
        count, me = sizes[axis], place[axis]
        return lax.fori_loop(
            1, count, lambda o, held: held + dst[lax.rem(me + o, count)].astype(F32), value
        )

    sa1 = scatter("lat", a0, a1, a1s, a1r)
    sb1 = scatter("lon", b0, b1, b1s, b1r)
    gt1 = gather("lat", t0, t1s, t1r)
    gt1[0]()
    sa1[0]()
    sb1[0]()
    gt1[1]()
    summed = t0[0]
    for i in range(1, nlat):
        summed = summed + t0[i]
    t1[place["lon"]] = summed
    gt2 = gather("lon", t1, t2s, t2r)
    gt2[0]()

    sa1[1]()
    sa2 = scatter("lon", a2, a3, a2s, a2r)

    def add_a(k, carry):
        held = a0[place["lat"], k].astype(F32)
        for o in range(1, nlat):
            held = held + a1[lax.rem(place["lat"] + o, nlat), k].astype(F32)
        a2[k] = held.astype(BF)
        return carry

    lax.fori_loop(0, nlon, add_a, 0)
    sa2[0]()
    sb1[1]()
    sb2 = scatter("lat", b2, b3, b2s, b2r)

    def add_b(k, carry):
        held = b0[place["lon"], k].astype(F32)
        for o in range(1, nlon):
            held = held + b1[lax.rem(place["lon"] + o, nlon), k].astype(F32)
        b2[k] = held.astype(BF)
        return carry

    lax.fori_loop(0, nlat, add_b, 0)
    sb2[0]()
    sa2[1]()
    la, lo = place["lat"], place["lon"]
    a4[la, lo] = total("lon", a2, a3).astype(BF)
    ga3 = gather("lon", a4.at[la], a3s, a3r)
    ga3[0]()
    sb2[1]()
    b4[lo, la] = total("lat", b2, b3).astype(BF)
    gb3 = gather("lat", b4.at[lo], b3s, b3r)
    gb3[0]()
    ga3[1]()
    ga4 = gather("lat", a4, a4s, a4r)
    ga4[0]()
    gb3[1]()
    gb4 = gather("lon", b4, b4s, b4r)
    gb4[0]()
    gt2[1]()
    summed = t1[0]
    for i in range(1, nlon):
        summed = summed + t1[i]
    taps_out[...] = summed
    ga4[1]()

    def join_a(j, carry):
        rows, cols = piece(j)
        low, high = j, j + 64
        wq_out[rows, cols] = a4[low // nlon, lax.rem(low, nlon)].astype(F32)
        wk_out[rows, cols] = a4[high // nlon, lax.rem(high, nlon)].astype(F32)
        return carry

    lax.fori_loop(0, 64, join_a, 0)
    gb4[1]()

    def join_b(j, carry):
        rows, cols = piece(j)
        low, high = j, j + 64
        wv_out[rows, cols] = b4[low // nlat, lax.rem(low, nlat)].astype(F32)
        wo_out[rows, cols] = b4[high // nlat, lax.rem(high, nlat)].astype(F32)
        return carry

    lax.fori_loop(0, 64, join_b, 0)
    for done in (gt1, sa1, sb1, gt2, sa2, sb2, ga3, gb3, ga4, gb4):
        done[2]()


def sum_gradients(nlat, nlon, dwq, dwkv, dwo, taps):
    vmem = pl.BlockSpec(memory_space=pltpu.VMEM)
    matrix = jax.ShapeDtypeStruct((D, D), F32)
    lat, lon = pltpu.SemaphoreType.DMA((nlat,)), pltpu.SemaphoreType.DMA((nlon,))

    def buf(*lead):
        return pltpu.VMEM((*lead, 16, 256), BF)

    return pl.pallas_call(
        functools.partial(sum_kernel, nlat, nlon),
        out_shape=(matrix, matrix, matrix, matrix, jax.ShapeDtypeStruct(taps.shape, F32)),
        in_specs=[vmem] * 4,
        out_specs=(vmem,) * 5,
        scratch_shapes=[
            buf(nlat, nlon), buf(nlon, nlat), buf(nlat, nlon), buf(nlon, nlat),
            buf(nlon), buf(nlat), buf(nlon), buf(nlat), buf(nlat, nlon), buf(nlon, nlat),
            pltpu.VMEM((nlat, *taps.shape), F32), pltpu.VMEM((nlon, *taps.shape), F32),
            lat, lat, lon, lon, lon, lon, lat, lat, lon, lon, lat, lat, lat, lat, lon, lon,
            lat, lat, lon, lon,
        ],
        compiler_params=pltpu.CompilerParams(
            collective_id=1, has_side_effects=True, vmem_limit_bytes=40 * 2**20
        ),
        name="sum_gradients",
    )(dwq, dwkv, dwo, taps)


def on_device(
    grid_tokens, obs_tokens, destinations, valid_counts, w_query, w_key, w_value, w_out,
    stencil_taps, cotangent,
):
    tile_rows, tile_columns = (grid_tokens.shape[0], grid_tokens.shape[1])
    cell_count = tile_rows * tile_columns
    block_count = obs_tokens.shape[0]
    nlat, nlon = lax.axis_size("lat"), lax.axis_size("lon")
    flat_grid = grid_tokens.reshape(cell_count, D)
    target = lax.rem(destinations[:, 0] - lax.axis_index("lon") + nlon, nlon)
    order_ids = jnp.arange(block_count, dtype=jnp.int32)
    earlier = (target[:, None] == target[None, :]) & (order_ids[None, :] < order_ids[:, None])
    slot_ids = target * CAP + jnp.sum(earlier.astype(jnp.int32), 1)
    chooser = slot_ids[None, :] == jnp.arange(nlon * CAP, dtype=jnp.int32)[:, None]
    block_ids = jnp.sum(jnp.where(chooser, order_ids[None, :], 0), 1)
    counts = jnp.sum(jnp.where(chooser, valid_counts[0][None, :], 0), 1)

    taps = stencil_taps[:, None, None, :]
    lat_ext = padded(cotangent, (("lat", 0),), 1, False).astype(F32)
    lon_ext = padded(cotangent, (("lon", 1),), 1, True).astype(F32)
    up = cotangent.astype(F32)
    up_north, up_south, up_west, up_east = lat_ext[:-2], lat_ext[2:], lon_ext[:, :-2], lon_ext[:, 2:]
    grad_middle = (
        (1.0 + taps[0]) * up + taps[1] * up_south + taps[2] * up_north
        + taps[3] * up_east + taps[4] * up_west
    ).astype(BF)

    middle, grad_obs, grad_grid, dwq, dwkv, dwo = attention(
        nlon, (block_ids, counts, slot_ids), obs_tokens, flat_grid,
        grad_middle.reshape(cell_count, D), (w_query, w_key, w_value, w_out),
    )
    middle = middle.reshape(tile_rows, tile_columns, D)
    centre = middle.astype(F32)
    terms = [jnp.sum(centre * side, (0, 1)) for side in (up, up_south, up_north, up_east, up_west)]
    terms = jnp.concatenate([jnp.stack(terms), jnp.zeros((3, D), F32)])
    lat_mid = padded(middle, (("lat", 0),), 1, False).astype(F32)
    lon_mid = padded(middle, (("lon", 1),), 1, True).astype(F32)
    sums = sum_gradients(nlat, nlon, dwq, dwkv, dwo, terms)
    encoded = (
        (1.0 + taps[0]) * centre + taps[1] * lat_mid[:-2] + taps[2] * lat_mid[2:]
        + taps[3] * lon_mid[:, :-2] + taps[4] * lon_mid[:, 2:]
    ).astype(BF)
    return (
        encoded, grad_grid.reshape(tile_rows, tile_columns, D), grad_obs,
        *sums[:4], sums[4][:5],
    )


def solution(mesh):
    in_specs = (
        P("lat", "lon", None),
        P(("lat", "lon"), None, None),
        P(("lat", "lon"), None),
        P(("lat", "lon"), None),
        P(),
        P(),
        P(),
        P(),
        P(),
        P("lat", "lon", None),
    )
    out_specs = (
        P("lat", "lon", None),
        P("lat", "lon", None),
        P(("lat", "lon"), None, None),
        P(),
        P(),
        P(),
        P(),
        P(),
    )
    return jax.shard_map(
        on_device, mesh=mesh, in_specs=in_specs, out_specs=out_specs, check_vma=False
    )
```

```python
import functools

import jax
import jax.numpy as jnp
from jax import lax
from jax.experimental import pallas as pl
from jax.experimental.pallas import tpu as pltpu
from jax.sharding import PartitionSpec as P

D = 512
HEADS = 8
HD = D // HEADS
BLK = 128
CAP = 2
ROWS = CAP * BLK
CELLS = 256
TILE = 16
SCALING = HD ** (-0.5)
MESH = pl.DeviceIdType.MESH
BF = jnp.bfloat16
F32 = jnp.float32


def dot(a, b):
    return jnp.dot(a, b, preferred_element_type=F32)


def dot_nt(a, b):
    return lax.dot_general(a, b, (((1,), (1,)), ((), ())), preferred_element_type=F32)


def onehot(rows, cols, hit):
    at = [lax.broadcasted_iota(jnp.int32, (rows, cols), k) for k in range(2)]
    return jnp.where(hit(*at), 1.0, 0.0).astype(BF)


def around(cells, halo, first, last):
    top = jnp.where(first, 0.0, halo[0].astype(F32)).astype(BF)
    bottom = jnp.where(last, 0.0, halo[1].astype(F32)).astype(BF)
    side = TILE
    west = dot(onehot(CELLS, CELLS, lambda q, k: (k == q - 1) & (lax.rem(q, side) != 0)), cells)
    west = west + dot(onehot(CELLS, side, lambda q, k: q == k * side), halo[2])
    east = dot(onehot(CELLS, CELLS, lambda q, k: (k == q + 1) & (lax.rem(q, side) != side - 1)), cells)
    east = east + dot(onehot(CELLS, side, lambda q, k: q == k * side + side - 1), halo[3])
    return (
        jnp.concatenate([top, cells[:-side]], 0).astype(F32),
        jnp.concatenate([cells[side:], bottom], 0).astype(F32),
        west,
        east,
    )


def edges(cells, out):
    out[0] = cells[CELLS - TILE :]
    out[1] = cells[:TILE]
    out[2] = dot(onehot(TILE, CELLS, lambda k, q: q == k * TILE + TILE - 1), cells).astype(BF)
    out[3] = dot(onehot(TILE, CELLS, lambda k, q: q == k * TILE), cells).astype(BF)


class Exchange:
    def __init__(self, axis, count, copy):
        self.axis, self.count, self.copy = axis, count, copy
        self.me = lax.axis_index(axis)

    def each(self, body):
        def step(o, carry):
            body(lax.rem(self.me + o, self.count))
            return carry

        lax.fori_loop(1, self.count, step, 0)

    def start(self):
        self.each(lambda at: self.copy(at, self.me).start())

    def wait(self):
        self.each(lambda at: self.copy(at, at).wait_recv())

    def sent(self):
        self.each(lambda at: self.copy(at, self.me).wait_send())


def scatter(axis, count, src, dst, ssem, rsem):
    return Exchange(axis, count, lambda to, frm: pltpu.make_async_remote_copy(
        src_ref=src.at[to], dst_ref=dst.at[frm], send_sem=ssem.at[to], recv_sem=rsem.at[frm],
        device_id={axis: to}, device_id_type=MESH))


def gather(axis, count, buf, ssem, rsem):
    me = lax.axis_index(axis)
    return Exchange(axis, count, lambda to, frm: pltpu.make_async_remote_copy(
        src_ref=buf.at[me], dst_ref=buf.at[frm], send_sem=ssem.at[to], recv_sem=rsem.at[frm],
        device_id={axis: to}, device_id_type=MESH))


class MatrixSum:
    def __init__(self, sizes, first, second, scratch, out):
        self.nf, self.ns = sizes[first], sizes[second]
        self.mf, self.ms = lax.axis_index(first), lax.axis_index(second)
        self.whole, self.got, self.part, self.got2 = scratch[:4]
        self.out = out
        s1, r1, s2, r2, s3, r3, s4, r4 = scratch[4:]
        self.first = scatter(first, self.nf, self.whole, self.got, s1, r1)
        self.second = scatter(second, self.ns, self.part, self.got2, s2, r2)
        self.third = gather(second, self.ns, out.at[self.mf], s3, r3)
        self.fourth = gather(first, self.nf, out, s4, r4)

    def begin(self, source):
        span = self.ns * 16
        per = D // span
        for f in range(self.nf):
            rows = slice((f % per) * span, (f % per + 1) * span)
            cols = slice((f // per) * 128, (f // per + 1) * 128)
            self.whole[f] = source(rows, cols).astype(BF).reshape(self.ns, 16, 128)
        self.first.start()

    def step2(self):
        self.first.wait()
        held = self.whole[self.mf].astype(F32)
        for o in range(1, self.nf):
            held = held + self.got[lax.rem(self.mf + o, self.nf)].astype(F32)
        self.part[...] = held.astype(BF)
        self.second.start()

    def step3(self):
        self.second.wait()
        held = self.part[self.ms].astype(F32)
        for o in range(1, self.ns):
            held = held + self.got2[lax.rem(self.ms + o, self.ns)].astype(F32)
        self.out[self.mf, self.ms] = held.astype(BF)
        self.third.start()

    def step4(self):
        self.third.wait()
        self.fourth.start()

    def step5(self):
        self.fourth.wait()

    def close(self):
        for part in (self.first, self.second, self.third, self.fourth):
            part.sent()


def kernel(
    nlat, n, dest_ref, count_ref, obs_ref, grid_ref, cot_ref, wq_ref, wk_ref, wv_ref, wo_ref, sten_ref,
    enc_ref, gobs_ref, ggrid_ref, sq_ref, sk_ref, sv_ref, so_ref, taps_ref,
    send, xs, ret, cnt_send, cnt_recv, kv, kt, vt, xt, bias, wkv, wkvt, qz, qzt, doz, dozt, dot_t,
    acc_o, acc_q, m_ref, l_ref, d_ref, dkv, dwkv, gm_ref, mid_ref, sides, edge, halo, t0, t1,
    x_ssem, x_rsem, c_ssem, c_rsem, g_ssem, g_rsem, h_ssem, h_rsem, t1s, t1r, t2s, t2r,
    *sum_scratch,
):
    sizes = {"lat": nlat, "lon": n}
    lat, me = lax.axis_index("lat"), lax.axis_index("lon")
    groups = n // 2
    blocks = obs_ref.shape[0]
    sum_q, sum_k, sum_v, sum_o = (
        MatrixSum(sizes, *axes, sum_scratch[12 * i : 12 * (i + 1)], out)
        for i, (axes, out) in enumerate((
            (("lat", "lon"), sq_ref), (("lon", "lat"), sk_ref), (("lat", "lon"), sv_ref),
            (("lat", "lon"), so_ref)))
    )
    tap1 = gather("lat", nlat, t0, t1s, t1r)
    tap2 = gather("lon", n, t1, t2s, t2r)

    def peer(d):
        return {"lon": lax.rem(me + d, n)}

    barrier = pltpu.get_barrier_semaphore()
    for whom in (tap1, tap2):
        whom.each(lambda at, axis=whom.axis: pl.semaphore_signal(
            barrier, inc=1, device_id={axis: at}, device_id_type=MESH))

    row_ids = lax.broadcasted_iota(jnp.int32, (8, CELLS), 0)

    def pack(d, carry):
        tile = lax.rem(me + d, n)

        def look(b, found):
            number, b0, b1, c0, c1 = found
            hit = dest_ref[b, 0] == tile
            one, two = hit & (number == 0), hit & (number == 1)
            return (
                number + hit.astype(jnp.int32),
                jnp.where(one, b, b0), jnp.where(two, b, b1),
                jnp.where(one, count_ref[0, b], c0), jnp.where(two, count_ref[0, b], c1),
            )

        zero = jnp.int32(0)
        found = (zero,) * 5
        for b in range(blocks):
            found = look(b, found)
        _, b0, b1, c0, c1 = found
        send[d, 0] = obs_ref[b0]
        send[d, 1] = obs_ref[b1]
        cnt_send[d] = jnp.where(row_ids == 0, c0, c1).astype(F32)
        return carry

    edges(cot_ref[...], edge.at[0])
    lax.fori_loop(0, n, pack, 0)
    pl.semaphore_wait(barrier, nlat + n - 2)

    def x_copy(d):
        return pltpu.make_async_remote_copy(
            src_ref=send.at[d], dst_ref=xs.at[d + 1], send_sem=x_ssem.at[d], recv_sem=x_rsem.at[d],
            device_id=peer(d), device_id_type=MESH,
        )

    def c_copy(d):
        return pltpu.make_async_remote_copy(
            src_ref=cnt_send.at[d], dst_ref=cnt_recv.at[d], send_sem=c_ssem.at[d], recv_sem=c_rsem.at[d],
            device_id=peer(d), device_id_type=MESH,
        )

    def g_copy(d):
        return pltpu.make_async_remote_copy(
            src_ref=send.at[d], dst_ref=ret.at[pl.ds(CAP * d, CAP)], send_sem=g_ssem.at[d],
            recv_sem=g_rsem.at[d], device_id=peer(n - d), device_id_type=MESH,
        )

    def h_copies(which):
        whom = (
            {"lat": lax.rem(lat + 1, nlat)}, {"lat": lax.rem(lat + nlat - 1, nlat)}, peer(1), peer(n - 1),
        )
        return [
            pltpu.make_async_remote_copy(
                src_ref=edge.at[which, k], dst_ref=halo.at[which, k], send_sem=h_ssem.at[which, k],
                recv_sem=h_rsem.at[which, k], device_id=whom[k], device_id_type=MESH,
            )
            for k in range(4)
        ]

    for copy in h_copies(0):
        copy.start()

    def ship(d, carry):
        c_copy(d).start()
        x_copy(d).start()
        return carry

    lax.fori_loop(1, n, ship, 0)

    xs[0] = grid_ref[...].reshape(CAP, BLK, D)
    xs[1] = send[0]
    cnt_recv[0] = cnt_send[0]
    wkv[:, :D] = wk_ref[...]
    wkv[:, D:] = wv_ref[...]
    wkvt[:D, :] = wk_ref[...].astype(F32).T.astype(BF)
    wkvt[D:, :] = wv_ref[...].astype(F32).T.astype(BF)
    lanes = lax.broadcasted_iota(jnp.int32, (CELLS, 2 * HD), 1)
    queries = dot(grid_ref[...], wq_ref[...]).astype(BF).astype(F32) * SCALING
    for copy in h_copies(0):
        copy.wait_recv()
    up = cot_ref[...].astype(F32)
    around_up = around(cot_ref[...], halo.at[0], lat == 0, lat == nlat - 1)
    for k in range(4):
        sides[k] = around_up[k].astype(BF)
    up_north, up_south, up_west, up_east = around_up
    gm_ref[...] = (
        (1.0 + sten_ref[0:1, :]) * up + sten_ref[1:2, :] * up_south + sten_ref[2:3, :] * up_north
        + sten_ref[3:4, :] * up_east + sten_ref[4:5, :] * up_west
    ).astype(BF)
    ups = dot_nt(gm_ref[...], wo_ref[...]).astype(BF).astype(F32)
    dot_t[...] = ups.T
    for h in range(HEADS):
        p, e = h // 2, h % 2
        mine = (lanes >= HD) if e else (lanes < HD)
        picked = jnp.where(mine, queries[:, p * 2 * HD : (p + 1) * 2 * HD], 0.0)
        qz[h] = picked.astype(BF)
        qzt[h] = picked.T.astype(BF)
        picked = jnp.where(mine, ups[:, p * 2 * HD : (p + 1) * 2 * HD], 0.0)
        doz[h] = picked.astype(BF)
        dozt[h] = picked.T.astype(BF)
    bias[0:ROWS, :] = jnp.zeros((ROWS, 128), F32)
    acc_o[...] = jnp.zeros_like(acc_o)
    acc_q[...] = jnp.zeros_like(acc_q)
    dwkv[...] = jnp.zeros_like(dwkv)
    m_ref[...] = jnp.full(m_ref.shape, -1e30, F32)
    l_ref[...] = jnp.zeros_like(l_ref)
    key_ids = lax.broadcasted_iota(jnp.int32, (BLK, 128), 0).astype(F32)

    def masked(rows):
        part = bias[rows, :]
        return jnp.concatenate([part, part], 1)


    def project(c, w, g):
        width = w * ROWS
        rows = pl.ds(pl.multiple_of(c * ROWS, ROWS), width)
        tokens = xs[pl.ds(c, w)].reshape(width, D)
        for j in range(4):
            cols = slice(j * 256, (j + 1) * 256)
            part = dot(tokens, wkv[:, cols]).astype(BF)
            kv[rows, cols] = part
            if j < 2:
                kt[g, cols, :width] = part.T
            else:
                vt[j * 256 - D : (j + 1) * 256 - D, :width] = part.T

    def attend(c, w):
        width = w * ROWS
        rows = pl.ds(pl.multiple_of(c * ROWS, ROWS), width)
        for h in range(HEADS):
            p = h // 2
            mine = slice(h * HD, (h + 1) * HD)
            scores = dot(kv[rows, p * 128 : (p + 1) * 128], qzt[h]) + masked(rows)
            old = m_ref[h]
            new = jnp.maximum(old, jnp.max(scores, 0, keepdims=True))
            raised = jnp.exp(scores - new)
            shrink = jnp.exp(old - new)
            l_ref[h] = l_ref[h] * shrink + jnp.sum(raised, 0, keepdims=True)
            m_ref[h] = new
            acc_o[mine, :] = acc_o[mine, :] * shrink + dot(vt[mine, :width], raised.astype(BF))

    project(0, 1, 0)
    attend(0, 1)

    def forward(g, carry):
        c = CAP * g - 1

        @pl.when(g >= 2)
        def _():
            c_copy(c - 1).wait_recv()
            x_copy(c - 1).wait_recv()

        c_copy(c).wait_recv()
        x_copy(c).wait_recv()
        for k in range(2):
            tile = cnt_recv[c - 1 + k]
            for r in range(CAP):
                rows = pl.ds(pl.multiple_of((c + k) * ROWS + r * BLK, BLK), BLK)
                bias[rows, :] = jnp.where(key_ids < tile[r : r + 1, :128], 0.0, -1e30)
        project(c, 2, g)
        attend(c, 2)
        return carry

    lax.fori_loop(1, groups + 1, forward, 0)

    def up_of():
        return cot_ref[...].astype(F32)

    def finish(h, carry):
        rows = pl.ds(pl.multiple_of(h * HD, HD), HD)
        total = l_ref[h]
        mixed = acc_o[rows, :] / total
        acc_o[rows, :] = mixed
        m_ref[h] = m_ref[h] + jnp.log(total)
        d_ref[h] = jnp.sum(mixed * dot_t[rows, :], 0, keepdims=True)
        return carry

    lax.fori_loop(0, HEADS, finish, 0)
    mid_ref[...] = (
        grid_ref[...].astype(F32) + dot(acc_o[...].T.astype(BF), wo_ref[...])
    ).astype(BF)
    edges(mid_ref[...], edge.at[1])
    for copy in h_copies(1):
        copy.start()
    centre = mid_ref[...].astype(F32)
    t0[lat] = jnp.zeros((8, D), F32)
    for row, side in enumerate((up_of(), *(sides[k].astype(F32) for k in (1, 0, 3, 2)))):
        t0[lat, row : row + 1, :] = jnp.sum(centre * side, 0, keepdims=True)
    tap1.start()
    attended = acc_o[...].astype(BF)
    sum_o.begin(lambda rows, cols: dot(attended[rows, :], gm_ref[:, cols]))

    def sent(d, carry):
        c_copy(d).wait_send()
        x_copy(d).wait_send()
        return carry

    lax.fori_loop(1, n, sent, 0)

    def differentiate(c, w, g):
        width = w * ROWS
        rows = pl.ds(pl.multiple_of(c * ROWS, ROWS), width)
        for p in range(HEADS // 2):
            here = slice(p * 128, (p + 1) * 128)
            there = slice(D + p * 128, D + (p + 1) * 128)
            grad_k = jnp.zeros((width, 128), F32)
            grad_v = jnp.zeros((width, 128), F32)
            for e in range(2):
                h = 2 * p + e
                mine = slice(h * HD, (h + 1) * HD)
                weights = jnp.exp(dot(kv[rows, here], qzt[h]) + masked(rows) - m_ref[h])
                grads = (weights * (dot(kv[rows, there], dozt[h]) - d_ref[h])).astype(BF)
                grad_k = grad_k + dot(grads, qz[h])
                grad_v = grad_v + dot(weights.astype(BF), doz[h])
                acc_q[mine, :] += dot(kt[g, mine, :width], grads)
            dkv[:width, here] = grad_k.astype(BF)
            dkv[:width, there] = grad_v.astype(BF)
        xt[:, :width] = xs[pl.ds(c, w)].reshape(width, D).T
        for j in range(4):
            cols = slice(j * 256, (j + 1) * 256)
            dwkv[:, cols] += dot(xt[:, :width], dkv[:width, cols])

    def backward(step, carry):
        g = 1 + lax.rem(step + 1, groups)
        d = CAP * g - 2
        differentiate(d + 1, 2, g)
        for j in range(2):
            cols = slice(j * 256, (j + 1) * 256)
            part = dot(dkv[...], wkvt[:, cols]).astype(BF)
            send[pl.ds(d, 2), :, :, cols] = part.reshape(2, CAP, BLK, 256)
        g_copy(d + 1).start()

        @pl.when(g >= 2)
        def _():
            g_copy(d).start()

        @pl.when(g == 1)
        def _():
            ret[0:CAP] = send[0]

        @pl.when(step == 2)
        def _():
            tap1.wait()
            total = t0[0]
            for i in range(1, nlat):
                total = total + t0[i]
            t1[me] = total
            tap2.start()
            sum_o.step2()

        @pl.when(step == 4)
        def _():
            sum_o.step3()

        @pl.when(step == 6)
        def _():
            sum_o.step4()

        return carry

    lax.fori_loop(0, groups, backward, 0)
    differentiate(0, 1, 0)

    grad_q = (acc_q[...].T * SCALING).astype(BF)
    sum_k.begin(lambda rows, cols: dwkv[rows, cols])
    sum_v.begin(lambda rows, cols: dwkv[rows, D + cols.start : D + cols.stop])
    dwq = dot(grid_ref[...].T, grad_q)
    sum_q.begin(lambda rows, cols: dwq[rows, cols])
    ggrid_ref[...] = (
        gm_ref[...].astype(F32) + dot_nt(grad_q, wq_ref[...]) + dot(dkv[:CELLS, :], wkvt[...])
    ).astype(BF)
    for copy in h_copies(1):
        copy.wait_recv()
    north, south, west, east = around(mid_ref[...], halo.at[1], lat == 0, lat == nlat - 1)
    enc_ref[...] = (
        (1.0 + sten_ref[0:1, :]) * mid_ref[...].astype(F32) + sten_ref[1:2, :] * north
        + sten_ref[2:3, :] * south + sten_ref[3:4, :] * west + sten_ref[4:5, :] * east
    ).astype(BF)
    late = (sum_k, sum_v, sum_q)
    for part in late:
        part.step2()

    def returned(d, carry):
        g_copy(d).wait_recv()
        g_copy(d).wait_send()
        return carry

    lax.fori_loop(1, n, returned, 0)

    for part in late:
        part.step3()

    def unpack(b, carry):
        tile = dest_ref[b, 0]
        rank = jnp.int32(0)
        for other in range(blocks):
            rank = rank + ((dest_ref[other, 0] == tile) & (other < b)).astype(jnp.int32)
        gobs_ref[b] = ret[CAP * lax.rem(tile - me + n, n) + jnp.minimum(rank, CAP - 1)]
        return carry

    lax.fori_loop(0, blocks, unpack, 0)
    for part in late:
        part.step4()
    tap2.wait()
    total = t1[0]
    for i in range(1, n):
        total = total + t1[i]
    taps_ref[...] = total
    for part in (sum_o, *late):
        part.step5()
    for part in (tap1, tap2):
        part.sent()
    for part in (sum_o, *late):
        part.close()
    for which in range(2):
        for copy in h_copies(which):
            copy.wait_send()


def on_device(
    grid_tokens, obs_tokens, destinations, valid_counts, w_query, w_key, w_value, w_out,
    stencil_taps, cotangent,
):
    tile_shape = grid_tokens.shape
    blocks = obs_tokens.shape[0]
    nlat, n = lax.axis_size("lat"), lax.axis_size("lon")
    vmem = pl.BlockSpec(memory_space=pltpu.VMEM)
    smem = pl.BlockSpec(memory_space=pltpu.SMEM)
    lat_sem, lon_sem = pltpu.SemaphoreType.DMA((nlat,)), pltpu.SemaphoreType.DMA((n,))
    halo_sem = pltpu.SemaphoreType.DMA((2, 4))
    sums = []
    for nf, ns, f_sem, s_sem in (
        (nlat, n, lat_sem, lon_sem), (n, nlat, lon_sem, lat_sem), (nlat, n, lat_sem, lon_sem),
        (nlat, n, lat_sem, lon_sem),
    ):
        sums += [
            pltpu.VMEM((nf, ns, 16, 128), BF), pltpu.VMEM((nf, ns, 16, 128), BF),
            pltpu.VMEM((ns, 16, 128), BF), pltpu.VMEM((ns, 16, 128), BF),
            f_sem, f_sem, s_sem, s_sem, s_sem, s_sem, f_sem, f_sem,
        ]
    tile = jax.ShapeDtypeStruct((CELLS, D), BF)
    lat_first = jax.ShapeDtypeStruct((nlat, n, 16, 128), BF)
    lon_first = jax.ShapeDtypeStruct((n, nlat, 16, 128), BF)
    encoded, grad_obs, grad_grid, *summed, taps = pl.pallas_call(
        functools.partial(kernel, nlat, n),
        out_shape=(
            tile, jax.ShapeDtypeStruct((blocks, BLK, D), BF), tile,
            lat_first, lon_first, lat_first, lat_first, jax.ShapeDtypeStruct((8, D), F32),
        ),
        in_specs=[smem] * 2 + [vmem] * 8,
        out_specs=(vmem,) * 8,
        scratch_shapes=[
            pltpu.VMEM((n, CAP, BLK, D), BF),
            pltpu.VMEM((n + 1, CAP, BLK, D), BF),
            pltpu.VMEM((n * CAP, BLK, D), BF),
            pltpu.VMEM((n, 8, CELLS), F32),
            pltpu.VMEM((n, 8, CELLS), F32),
            pltpu.VMEM(((n + 1) * ROWS, 2 * D), BF),
            pltpu.VMEM((n // 2 + 1, D, 2 * ROWS), BF),
            pltpu.VMEM((D, 2 * ROWS), BF),
            pltpu.VMEM((D, 2 * ROWS), BF),
            pltpu.VMEM(((n + 1) * ROWS, 128), F32),
            pltpu.VMEM((D, 2 * D), BF),
            pltpu.VMEM((2 * D, D), BF),
            pltpu.VMEM((HEADS, CELLS, 2 * HD), BF),
            pltpu.VMEM((HEADS, 2 * HD, CELLS), BF),
            pltpu.VMEM((HEADS, CELLS, 2 * HD), BF),
            pltpu.VMEM((HEADS, 2 * HD, CELLS), BF),
            pltpu.VMEM((D, CELLS), F32),
            pltpu.VMEM((D, CELLS), F32),
            pltpu.VMEM((D, CELLS), F32),
            pltpu.VMEM((HEADS, 1, CELLS), F32),
            pltpu.VMEM((HEADS, 1, CELLS), F32),
            pltpu.VMEM((HEADS, 1, CELLS), F32),
            pltpu.VMEM((2 * ROWS, 2 * D), BF),
            pltpu.VMEM((D, 2 * D), F32),
            pltpu.VMEM((CELLS, D), BF),
            pltpu.VMEM((CELLS, D), BF),
            pltpu.VMEM((4, CELLS, D), BF),
            pltpu.VMEM((2, 4, TILE, D), BF),
            pltpu.VMEM((2, 4, TILE, D), BF),
            pltpu.VMEM((nlat, 8, D), F32),
            pltpu.VMEM((n, 8, D), F32),
            lon_sem, lon_sem, lon_sem, lon_sem, lon_sem, lon_sem, halo_sem, halo_sem,
            lat_sem, lat_sem, lon_sem, lon_sem,
            *sums,
        ],
        compiler_params=pltpu.CompilerParams(
            collective_id=0, has_side_effects=True, vmem_limit_bytes=62 * 2**20
        ),
        name="encoder_step",
    )(
        destinations, valid_counts, obs_tokens, grid_tokens.reshape(CELLS, D),
        cotangent.reshape(CELLS, D), w_query, w_key, w_value, w_out, stencil_taps,
    )
    matrices = [
        part.reshape(4, D, 128).transpose(1, 0, 2).reshape(D, D).astype(F32) for part in summed
    ]
    return (
        encoded.reshape(tile_shape), grad_grid.reshape(tile_shape), grad_obs, *matrices, taps[:5],
    )


def solution(mesh):
    in_specs = (
        P("lat", "lon", None),
        P(("lat", "lon"), None, None),
        P(("lat", "lon"), None),
        P(("lat", "lon"), None),
        P(),
        P(),
        P(),
        P(),
        P(),
        P("lat", "lon", None),
    )
    out_specs = (
        P("lat", "lon", None),
        P("lat", "lon", None),
        P(("lat", "lon"), None, None),
        P(),
        P(),
        P(),
        P(),
        P(),
    )
    return jax.shard_map(
        on_device, mesh=mesh, in_specs=in_specs, out_specs=out_specs, check_vma=False
    )
```

```python
import functools

import jax
import jax.numpy as jnp
from jax import lax
from jax.experimental import pallas as pl
from jax.experimental.pallas import tpu as pltpu
from jax.sharding import PartitionSpec as P

D = 512
HEADS = 8
HD = D // HEADS
BLK = 128
CAP = 2
ROWS = CAP * BLK
CELLS = 256
TILE = 16
SCALING = HD ** (-0.5)
MESH = pl.DeviceIdType.MESH
SIDE = 4
STEPS = (
    (0, 0), (0, 1), (0, 3), (1, 0), (3, 0), (1, 1), (1, 3), (3, 1), (3, 3),
    (0, 2), (2, 0), (1, 2), (3, 2), (2, 1), (2, 3), (2, 2),
)
NEAR = 9
EXTRA = 16
BF = jnp.bfloat16
F32 = jnp.float32


def dot(a, b):
    return jnp.dot(a, b, preferred_element_type=F32)


def dot_nt(a, b):
    return lax.dot_general(a, b, (((1,), (1,)), ((), ())), preferred_element_type=F32)


def onehot(rows, cols, hit):
    at = [lax.broadcasted_iota(jnp.int32, (rows, cols), k) for k in range(2)]
    return jnp.where(hit(*at), 1.0, 0.0).astype(BF)


def around(cells, halo, first, last):
    top = jnp.where(first, 0.0, halo[0].astype(F32)).astype(BF)
    bottom = jnp.where(last, 0.0, halo[1].astype(F32)).astype(BF)
    side = TILE
    west = dot(onehot(CELLS, CELLS, lambda q, k: (k == q - 1) & (lax.rem(q, side) != 0)), cells)
    west = west + dot(onehot(CELLS, side, lambda q, k: q == k * side), halo[2])
    east = dot(onehot(CELLS, CELLS, lambda q, k: (k == q + 1) & (lax.rem(q, side) != side - 1)), cells)
    east = east + dot(onehot(CELLS, side, lambda q, k: q == k * side + side - 1), halo[3])
    return (
        jnp.concatenate([top, cells[:-side]], 0).astype(F32),
        jnp.concatenate([cells[side:], bottom], 0).astype(F32),
        west,
        east,
    )


def edges(cells, out):
    out[0] = cells[CELLS - TILE :]
    out[1] = cells[:TILE]
    out[2] = dot(onehot(TILE, CELLS, lambda k, q: q == k * TILE + TILE - 1), cells).astype(BF)
    out[3] = dot(onehot(TILE, CELLS, lambda k, q: q == k * TILE), cells).astype(BF)


class Exchange:
    def __init__(self, count, me, whom, copy):
        self.count, self.me, self.whom, self.copy = count, me, whom, copy

    def each(self, body):
        def step(o, carry):
            body(lax.rem(self.me + o, self.count))
            return carry

        if self.count == 2:
            body(1 - self.me)
        else:
            lax.fori_loop(1, self.count, step, 0)

    def greet(self, barrier):
        self.each(lambda at: pl.semaphore_signal(
            barrier, inc=1, device_id=self.whom(at), device_id_type=MESH))

    def start(self):
        self.each(lambda at: self.copy(at, self.me).start())

    def wait(self):
        self.each(lambda at: self.copy(at, at).wait_recv())

    def sent(self):
        self.each(lambda at: self.copy(at, self.me).wait_send())


def scatter(group, src, dst, ssem, rsem):
    count, me, whom = group
    return Exchange(count, me, whom, lambda to, frm: pltpu.make_async_remote_copy(
        src_ref=src.at[to], dst_ref=dst.at[frm], send_sem=ssem.at[to], recv_sem=rsem.at[frm],
        device_id=whom(to), device_id_type=MESH))


def gather(group, buf, ssem, rsem):
    count, me, whom = group
    return Exchange(count, me, whom, lambda to, frm: pltpu.make_async_remote_copy(
        src_ref=buf.at[me], dst_ref=buf.at[frm], send_sem=ssem.at[to], recv_sem=rsem.at[frm],
        device_id=whom(to), device_id_type=MESH))


class MatrixSum:
    def __init__(self, groups, scratch, out):
        self.core, self.x, self.lon = (group[1] for group in groups)
        self.counts = [group[0] for group in groups]
        self.whole, self.got, self.half, self.got_half, self.piece, self.got_piece = scratch[:6]
        self.out = out
        sems = scratch[6:]
        self.stages = [
            scatter(groups[0], self.whole, self.got, *sems[0:2]),
            scatter(groups[1], self.half, self.got_half, *sems[2:4]),
            scatter(groups[2], self.piece, self.got_piece, *sems[4:6]),
            gather(groups[2], out.at[self.core, self.x], *sems[6:8]),
            gather(groups[1], out.at[self.core], *sems[8:10]),
            gather(groups[0], out, *sems[10:12]),
        ]

    def load(self, number, source):
        per = D // 256
        for c in range(2):
            for x in range(4):
                f = 4 * c + x
                rows = slice((f % per) * 256, (f % per + 1) * 256)
                cols = slice((f // per) * 128, (f // per + 1) * 128)
                self.whole[c, x, :, number] = source(rows, cols).astype(BF).reshape(16, 16, 128)

    def total(self, stage, own, got):
        group = self.stages[stage]
        held = own[group.me].astype(F32)
        for o in range(1, group.count):
            held = held + got[lax.rem(group.me + o, group.count)].astype(F32)
        return held.astype(BF)

    def begin(self):
        self.stages[0].start()

    def step(self, stage):
        self.stages[stage].wait()
        if stage == 0:
            for x in range(4):
                self.half[x] = (
                    self.whole[self.core, x].astype(F32) + self.got[1 - self.core, x].astype(F32)
                ).astype(BF)
        elif stage == 1:
            self.piece[...] = self.total(1, self.half, self.got_half)
        elif stage == 2:
            self.out[self.core, self.x, self.lon] = self.total(2, self.piece, self.got_piece)
        if stage < 5:
            self.stages[stage + 1].start()

    def close(self):
        for stage in self.stages:
            stage.sent()


def kernel(
    nlat, n, dest_ref, count_ref, obs_ref, grid_ref, cot_ref, wq_ref, wk_ref, wv_ref, wo_ref, sten_ref,
    enc_ref, gobs_ref, ggrid_ref, late_ref, early_ref, taps_ref,
    send, xs, ret, relay, relay_back, kv, kt, vt, xt, bias, wkv, wkvt, qz, qzt, doz, dozt, dot_t,
    acc_o, acc_q, m_ref, l_ref, d_ref, dkv, dwkv, gm_ref, mid_ref, sides, edge, halo, t0, t1,
    x_ssem, x_rsem, r_ssem, r_rsem, g_ssem, g_rsem, b_ssem, b_rsem, h_ssem, h_rsem, t1s, t1r, t2s, t2r,
    *sum_scratch,
):
    lat, me = lax.axis_index("lat"), lax.axis_index("lon")
    groups = n // 2
    blocks = obs_ref.shape[0]
    x_at, core = lat // 2, lax.rem(lat, 2)
    rings = (
        (2, core, lambda at: {"lat": 2 * x_at + at}),
        (nlat // 2, x_at, lambda at: {"lat": 2 * at + core}),
        (n, me, lambda at: {"lon": at}),
    )
    half = len(sum_scratch) // 2
    late = MatrixSum(rings, sum_scratch[:half], late_ref)
    early = MatrixSum(rings, sum_scratch[half:], early_ref)
    tap1 = gather((nlat, lat, lambda at: {"lat": at}), t0, t1s, t1r)
    tap2 = gather(rings[2], t1, t2s, t2r)

    y, z = me // SIDE, lax.rem(me, SIDE)
    way_y, way_z = 1 - 2 * lax.rem(y, 2), 1 - 2 * lax.rem(z, 2)

    def place(dy, dz):
        return lax.rem(y + dy + 2 * SIDE, SIDE) * SIDE + lax.rem(z + dz + 2 * SIDE, SIDE)

    def leg(i, sign):
        dy, dz = STEPS[i]
        return {"lon": place(
            way_y if dy == 2 else sign * dy, way_z if dz == 2 else sign * dz)}

    def onward(i):
        dy, dz = STEPS[i]
        return {"lon": place(-way_y if dy == 2 else 0, -way_z if dz == 2 else 0)}

    barrier = pltpu.get_barrier_semaphore()
    for group in (tap1, tap2):
        group.greet(barrier)

    row_ids = lax.broadcasted_iota(jnp.int32, (EXTRA, D), 0)

    def pack(i):
        tile = place(*STEPS[i])
        number = b0 = b1 = c0 = c1 = jnp.int32(0)
        for b in range(blocks):
            hit = dest_ref[0, b] == tile
            one, two = hit & (number == 0), hit & (number == 1)
            number = number + hit.astype(jnp.int32)
            b0, b1 = jnp.where(one, b, b0), jnp.where(two, b, b1)
            c0, c1 = jnp.where(one, count_ref[0, b], c0), jnp.where(two, count_ref[0, b], c1)
        send[i, 0:BLK, :] = obs_ref[b0]
        send[i, BLK:ROWS, :] = obs_ref[b1]
        send[i, ROWS:, :] = jnp.where(row_ids == 0, c0, c1).astype(F32).astype(BF)

    edges(cot_ref[...], edge.at[0])
    pl.semaphore_wait(barrier, nlat + n - 2)

    def remote(src, dst, ssem, rsem, whom):
        return pltpu.make_async_remote_copy(
            src_ref=src, dst_ref=dst, send_sem=ssem, recv_sem=rsem, device_id=whom, device_id_type=MESH)

    def x_copy(i):
        if i < NEAR:
            return remote(send.at[i], xs.at[i + 1], x_ssem.at[i], x_rsem.at[i], leg(i, 1))
        j = i - NEAR
        return remote(send.at[i], relay.at[j], x_ssem.at[i], r_rsem.at[j], leg(i, 1))

    def x_onward(i):
        j = i - NEAR
        return remote(relay.at[j], xs.at[i + 1], r_ssem.at[j], x_rsem.at[i], onward(i))

    def g_copy(i):
        tokens = send.at[i, pl.ds(0, ROWS)]
        if i < NEAR:
            return remote(tokens, ret.at[i], g_ssem.at[i], g_rsem.at[i], leg(i, -1))
        j = i - NEAR
        return remote(tokens, relay_back.at[j], g_ssem.at[i], b_rsem.at[j], leg(i, -1))

    def g_onward(i):
        j = i - NEAR
        return remote(relay_back.at[j], ret.at[i], b_ssem.at[j], g_rsem.at[i], onward(i))

    def x_arrived(i):
        remote(send.at[0], xs.at[i + 1], x_ssem.at[0], x_rsem.at[i], {"lon": me}).wait_recv()

    def h_copies(which):
        whom = (
            {"lat": lax.rem(lat + 1, nlat)}, {"lat": lax.rem(lat + nlat - 1, nlat)},
            {"lon": lax.rem(me + 1, n)}, {"lon": lax.rem(me + n - 1, n)},
        )
        return [
            remote(edge.at[which, k], halo.at[which, k], h_ssem.at[which, k], h_rsem.at[which, k], whom[k])
            for k in range(4)
        ]

    for copy in h_copies(0):
        copy.start()

    for i in (*range(NEAR, n), *range(1, NEAR)):
        pack(i)
        x_copy(i).start()
    pack(0)

    xs[0, 0:ROWS, :] = grid_ref[...]
    xs[1] = send[0]
    wkv[:, :D] = wk_ref[...]
    wkv[:, D:] = wv_ref[...]
    wkvt[:D, :] = wk_ref[...].astype(F32).T.astype(BF)
    wkvt[D:, :] = wv_ref[...].astype(F32).T.astype(BF)
    lanes = lax.broadcasted_iota(jnp.int32, (CELLS, 2 * HD), 1)
    queries = dot(grid_ref[...], wq_ref[...]).astype(BF).astype(F32) * SCALING
    for copy in h_copies(0):
        copy.wait_recv()
    up = cot_ref[...].astype(F32)
    around_up = around(cot_ref[...], halo.at[0], lat == 0, lat == nlat - 1)
    for k in range(4):
        sides[k] = around_up[k].astype(BF)
    up_north, up_south, up_west, up_east = around_up
    gm_ref[...] = (
        (1.0 + sten_ref[0:1, :]) * up + sten_ref[1:2, :] * up_south + sten_ref[2:3, :] * up_north
        + sten_ref[3:4, :] * up_east + sten_ref[4:5, :] * up_west
    ).astype(BF)
    ups = dot_nt(gm_ref[...], wo_ref[...]).astype(BF).astype(F32)
    dot_t[...] = ups.T
    for h in range(HEADS):
        p, e = h // 2, h % 2
        mine = (lanes >= HD) if e else (lanes < HD)
        picked = jnp.where(mine, queries[:, p * 2 * HD : (p + 1) * 2 * HD], 0.0)
        qz[h] = picked.astype(BF)
        qzt[h] = picked.T.astype(BF)
        picked = jnp.where(mine, ups[:, p * 2 * HD : (p + 1) * 2 * HD], 0.0)
        doz[h] = picked.astype(BF)
        dozt[h] = picked.T.astype(BF)
    acc_o[...] = jnp.zeros_like(acc_o)
    acc_q[...] = jnp.zeros_like(acc_q)
    dwkv[...] = jnp.zeros_like(dwkv)
    m_ref[...] = jnp.full(m_ref.shape, -1e30, F32)
    l_ref[...] = jnp.zeros_like(l_ref)
    key_ids = lax.broadcasted_iota(jnp.int32, (BLK, 128), 0).astype(F32)

    def masked(width):
        part = bias[0:width, :]
        return jnp.concatenate([part, part], 1)

    def mark(c, w):
        if w == 1:
            bias[0:ROWS, :] = jnp.zeros((ROWS, 128), F32)
            return
        for k in range(w):
            tile = xs[c + k, ROWS:, 0:128].astype(F32)
            for r in range(CAP):
                at = k * ROWS + r * BLK
                bias[at : at + BLK, :] = jnp.where(key_ids < tile[r : r + 1, :], 0.0, -1e30)

    def project(c, w, g):
        width = w * ROWS
        rows = pl.ds(pl.multiple_of(c * ROWS, ROWS), width)
        tokens = xs[pl.ds(c, w), 0:ROWS, :].reshape(width, D)
        for j in range(4):
            cols = slice(j * 256, (j + 1) * 256)
            part = dot(tokens, wkv[:, cols]).astype(BF)
            kv[rows, cols] = part
            if j < 2:
                kt[g, cols, :width] = part.T
            else:
                vt[j * 256 - D : (j + 1) * 256 - D, :width] = part.T

    def attend(c, w):
        width = w * ROWS
        mark(c, w)
        rows = pl.ds(pl.multiple_of(c * ROWS, ROWS), width)

        def pair(p, carry):
            keys = kv[rows, pl.ds(pl.multiple_of(p * 128, 128), 128)]
            for e in range(2):
                h = 2 * p + e
                mine = pl.ds(pl.multiple_of(h * HD, HD), HD)
                scores = dot(keys, qzt[h]) + masked(width)
                old = m_ref[h]
                new = jnp.maximum(old, jnp.max(scores, 0, keepdims=True))
                raised = jnp.exp(scores - new)
                shrink = jnp.exp(old - new)
                l_ref[h] = l_ref[h] * shrink + jnp.sum(raised, 0, keepdims=True)
                m_ref[h] = new
                acc_o[mine, :] = acc_o[mine, :] * shrink + dot(vt[mine, :width], raised.astype(BF))
            return carry

        lax.fori_loop(0, HEADS // 2, pair, 0)

    project(0, 1, 0)
    attend(0, 1)

    for i in range(NEAR, n):
        x_copy(i).wait_recv()
        x_onward(i).start()

    def forward(g, carry):
        c = CAP * g - 1

        @pl.when(g >= 2)
        def _():
            x_arrived(c - 1)

        x_arrived(c)
        project(c, 2, g)
        attend(c, 2)
        return carry

    lax.fori_loop(1, groups + 1, forward, 0)

    def up_of():
        return cot_ref[...].astype(F32)

    def finish(h, carry):
        rows = pl.ds(pl.multiple_of(h * HD, HD), HD)
        total = l_ref[h]
        mixed = acc_o[rows, :] / total
        acc_o[rows, :] = mixed
        m_ref[h] = m_ref[h] + jnp.log(total)
        d_ref[h] = jnp.sum(mixed * dot_t[rows, :], 0, keepdims=True)
        return carry

    lax.fori_loop(0, HEADS, finish, 0)
    mid_ref[...] = (
        grid_ref[...].astype(F32) + dot(acc_o[...].T.astype(BF), wo_ref[...])
    ).astype(BF)
    edges(mid_ref[...], edge.at[1])
    for copy in h_copies(1):
        copy.start()
    centre = mid_ref[...].astype(F32)
    t0[lat] = jnp.zeros((8, D), F32)
    for row, side in enumerate((up_of(), *(sides[k].astype(F32) for k in (1, 0, 3, 2)))):
        t0[lat, row : row + 1, :] = jnp.sum(centre * side, 0, keepdims=True)
    tap1.start()
    attended = acc_o[...].astype(BF)
    early.load(0, lambda rows, cols: dot(attended[rows, :], gm_ref[:, cols]))
    early.begin()

    for i in range(1, n):
        x_copy(i).wait_send()

    def differentiate(c, w, parts):
        width = w * ROWS
        mark(c, w)
        rows = pl.ds(pl.multiple_of(c * ROWS, ROWS), width)

        def pair(p, carry):
            here = pl.ds(pl.multiple_of(p * 128, 128), 128)
            there = pl.ds(pl.multiple_of(D + p * 128, 128), 128)
            keys, values = kv[rows, here], kv[rows, there]
            grad_k = grad_v = None
            for e in range(2):
                h = 2 * p + e
                mine = pl.ds(pl.multiple_of(h * HD, HD), HD)
                weights = jnp.exp(dot(keys, qzt[h]) + masked(width) - m_ref[h])
                grads = (weights * (dot(values, dozt[h]) - d_ref[h])).astype(BF)
                part_k, part_v = dot(grads, qz[h]), dot(weights.astype(BF), doz[h])
                grad_k = part_k if e == 0 else grad_k + part_k
                grad_v = part_v if e == 0 else grad_v + part_v
                total = acc_q[mine, :]
                for k, g in enumerate(parts):
                    span = min(width, 2 * ROWS)
                    total = total + dot(kt[g, mine, :span], grads[k * span : (k + 1) * span, :])
                acc_q[mine, :] = total
            dkv[:width, here] = grad_k.astype(BF)
            dkv[:width, there] = grad_v.astype(BF)
            return carry

        lax.fori_loop(0, HEADS // 2, pair, 0)
        xt[:, :width] = xs[pl.ds(c, w), 0:ROWS, :].reshape(width, D).T

        def weigh(j, carry):
            cols = pl.ds(pl.multiple_of(j * 256, 256), 256)
            dwkv[:, cols] += dot(xt[:, :width], dkv[:width, cols])
            return carry

        lax.fori_loop(0, 4, weigh, 0)

    def backward(step, carry):
        g = groups - step
        differentiate(CAP * g - 1, 2, (g,))

        def turn(j, inner):
            cols = pl.ds(pl.multiple_of(j * 256, 256), 256)
            part = dot(dkv[...], wkvt[:, cols]).astype(BF)
            send[pl.ds(CAP * g - 2, 2), 0:ROWS, cols] = part.reshape(2, ROWS, 256)
            return inner

        lax.fori_loop(0, 2, turn, 0)
        for k in range(groups):
            @pl.when(step == k)
            def _(k=k):
                first = CAP * (groups - k) - 2
                if first:
                    g_copy(first).start()
                else:
                    ret[0] = send[0, 0:ROWS, :]
                g_copy(first + 1).start()
                if k >= 2:
                    for i in (first + 4, first + 5):
                        if i >= NEAR:
                            g_copy(i).wait_recv()
                            g_onward(i).start()

        @pl.when(step == 2)
        def _():
            tap1.wait()
            total = t0[0]
            for i in range(1, nlat):
                total = total + t0[i]
            t1[me] = total
            tap2.start()

        for stage in range(5):
            pl.when(step == stage + 2)(functools.partial(early.step, stage))

        return carry

    lax.fori_loop(0, groups, backward, 0)
    differentiate(0, 1, (0,))

    grad_q = (acc_q[...].T * SCALING).astype(BF)
    dwq = dot(grid_ref[...].T, grad_q)
    late.load(0, lambda rows, cols: dwq[rows, cols])
    late.load(1, lambda rows, cols: dwkv[rows, cols])
    late.load(2, lambda rows, cols: dwkv[rows, D + cols.start : D + cols.stop])
    late.begin()
    ggrid_ref[...] = (
        gm_ref[...].astype(F32) + dot_nt(grad_q, wq_ref[...]) + dot(dkv[:CELLS, :], wkvt[...])
    ).astype(BF)
    for copy in h_copies(1):
        copy.wait_recv()
    north, south, west, east = around(mid_ref[...], halo.at[1], lat == 0, lat == nlat - 1)
    enc_ref[...] = (
        (1.0 + sten_ref[0:1, :]) * mid_ref[...].astype(F32) + sten_ref[1:2, :] * north
        + sten_ref[2:3, :] * south + sten_ref[3:4, :] * west + sten_ref[4:5, :] * east
    ).astype(BF)
    late.step(0)

    for i in range(1, n):
        if i < NEAR:
            g_copy(i).wait_recv()
        else:
            g_onward(i).wait_recv()
        g_copy(i).wait_send()
        if i >= NEAR:
            x_onward(i).wait_send()
            g_onward(i).wait_send()

    late.step(1)

    def unpack(b, carry):
        tile = dest_ref[0, b]
        rank = jnp.int32(0)
        for other in range(blocks):
            rank = rank + ((dest_ref[0, other] == tile) & (other < b)).astype(jnp.int32)
        dy = lax.rem(tile // SIDE - y + SIDE, SIDE)
        dz = lax.rem(lax.rem(tile, SIDE) - z + SIDE, SIDE)
        at = jnp.int32(0)
        for i, (sy, sz) in enumerate(STEPS):
            at = jnp.where((dy == sy) & (dz == sz), i, at)
        both = ret[at]
        gobs_ref[b] = jnp.where(rank == 0, both[:BLK], both[BLK:])
        return carry

    lax.fori_loop(0, blocks, unpack, 0)
    late.step(2)
    tap2.wait()
    total = t1[0]
    for i in range(1, n):
        total = total + t1[i]
    taps_ref[...] = total
    late.step(3)
    early.step(5)
    late.step(4)
    late.step(5)
    for part in (tap1, tap2):
        part.sent()
    for part in (early, late):
        part.close()
    for which in range(2):
        for copy in h_copies(which):
            copy.wait_send()


def write_kernel(
    enc, gobs, ggrid, late, early, taps, enc_o, gobs_o, ggrid_o, wq, wk, wv, wo, taps_o,
    enc_v, gobs_v, ggrid_v, late_v, early_v, sums_v, in_sems, out_sems,
):
    pairs = ((late, late_v, None), (early, early_v, None), (gobs, gobs_v, gobs_o), (enc, enc_v, enc_o),
             (ggrid, ggrid_v, ggrid_o))
    loads = [pltpu.make_async_copy(a, b, in_sems.at[k]) for k, (a, b, _) in enumerate(pairs)]
    stores = []

    def store(source, out):
        stores.append(pltpu.make_async_copy(source, out, out_sems.at[len(stores)]))
        stores[-1].start()

    for load in loads:
        load.start()
    taps_o[...] = taps[0:5, :]
    loads[0].wait()
    for k, (out, source, number) in enumerate(
            ((wq, late_v, 0), (wk, late_v, 1), (wv, late_v, 2), (wo, early_v, 0))):
        if k == 3:
            loads[1].wait()
        for f in range(8):
            rows, cols = slice((f % 2) * 256, (f % 2 + 1) * 256), slice((f // 2) * 128, (f // 2 + 1) * 128)
            sums_v[k, rows, cols] = source[f // 4, f % 4, :, number].reshape(256, 128).astype(F32)
        store(sums_v.at[k], out)
        if k < 3:
            loads[2 + k].wait()
            store(pairs[2 + k][1], pairs[2 + k][2])
    for copy in stores:
        copy.wait()


def on_device(
    grid_tokens, obs_tokens, destinations, valid_counts, w_query, w_key, w_value, w_out,
    stencil_taps, cotangent,
):
    tile_shape = grid_tokens.shape
    blocks = obs_tokens.shape[0]
    nlat, n = lax.axis_size("lat"), lax.axis_size("lon")
    vmem = pl.BlockSpec(memory_space=pltpu.VMEM)
    smem = pl.BlockSpec(memory_space=pltpu.SMEM)
    lat_sem, lon_sem = pltpu.SemaphoreType.DMA((nlat,)), pltpu.SemaphoreType.DMA((n,))
    far_sem = pltpu.SemaphoreType.DMA((n - NEAR,))
    halo_sem = pltpu.SemaphoreType.DMA((2, 4))
    x_sem, core_sem = pltpu.SemaphoreType.DMA((nlat // 2,)), pltpu.SemaphoreType.DMA((2,))
    sums = []
    for number in (3, 1):
        whole, part, piece = (
            pltpu.VMEM((*lead, number, 16, 128), BF) for lead in ((2, nlat // 2, n), (nlat // 2, n), (n,))
        )
        sums += [whole, whole, part, part, piece, piece]
        sums += [core_sem, core_sem, x_sem, x_sem, lon_sem, lon_sem]
        sums += [lon_sem, lon_sem, x_sem, x_sem, core_sem, core_sem]
    tile = jax.ShapeDtypeStruct((CELLS, D), BF)
    results = pl.pallas_call(
        functools.partial(kernel, nlat, n),
        out_shape=(
            tile, jax.ShapeDtypeStruct((blocks, BLK, D), BF), tile,
            jax.ShapeDtypeStruct((2, nlat // 2, n, 3, 16, 128), BF),
            jax.ShapeDtypeStruct((2, nlat // 2, n, 1, 16, 128), BF),
            jax.ShapeDtypeStruct((8, D), F32),
        ),
        in_specs=[smem] * 2 + [vmem] * 8,
        out_specs=(vmem,) * 6,
        scratch_shapes=[
            pltpu.VMEM((n, ROWS + EXTRA, D), BF),
            pltpu.VMEM((n + 1, ROWS + EXTRA, D), BF),
            pltpu.VMEM((n, ROWS, D), BF),
            pltpu.VMEM((n - NEAR, ROWS + EXTRA, D), BF),
            pltpu.VMEM((n - NEAR, ROWS, D), BF),
            pltpu.VMEM(((n + 1) * ROWS, 2 * D), BF),
            pltpu.VMEM((n // 2 + 1, D, 2 * ROWS), BF),
            pltpu.VMEM((D, 2 * ROWS), BF),
            pltpu.VMEM((D, 2 * ROWS), BF),
            pltpu.VMEM((2 * ROWS, 128), F32),
            pltpu.VMEM((D, 2 * D), BF),
            pltpu.VMEM((2 * D, D), BF),
            pltpu.VMEM((HEADS, CELLS, 2 * HD), BF),
            pltpu.VMEM((HEADS, 2 * HD, CELLS), BF),
            pltpu.VMEM((HEADS, CELLS, 2 * HD), BF),
            pltpu.VMEM((HEADS, 2 * HD, CELLS), BF),
            pltpu.VMEM((D, CELLS), F32),
            pltpu.VMEM((D, CELLS), F32),
            pltpu.VMEM((D, CELLS), F32),
            pltpu.VMEM((HEADS, 1, CELLS), F32),
            pltpu.VMEM((HEADS, 1, CELLS), F32),
            pltpu.VMEM((HEADS, 1, CELLS), F32),
            pltpu.VMEM((2 * ROWS, 2 * D), BF),
            pltpu.VMEM((D, 2 * D), F32),
            pltpu.VMEM((CELLS, D), BF),
            pltpu.VMEM((CELLS, D), BF),
            pltpu.VMEM((4, CELLS, D), BF),
            pltpu.VMEM((2, 4, TILE, D), BF),
            pltpu.VMEM((2, 4, TILE, D), BF),
            pltpu.VMEM((nlat, 8, D), F32),
            pltpu.VMEM((n, 8, D), F32),
            lon_sem, lon_sem, far_sem, far_sem, lon_sem, lon_sem, far_sem, far_sem, halo_sem, halo_sem,
            lat_sem, lat_sem, lon_sem, lon_sem,
            *sums,
        ],
        compiler_params=pltpu.CompilerParams(
            collective_id=0, has_side_effects=True, vmem_limit_bytes=62 * 2**20
        ),
        name="encoder_step",
    )(
        destinations.reshape(1, blocks), valid_counts, obs_tokens, grid_tokens.reshape(CELLS, D),
        cotangent.reshape(CELLS, D), w_query, w_key, w_value, w_out, stencil_taps,
    )
    anywhere = pl.BlockSpec(memory_space=pl.ANY)
    matrix = jax.ShapeDtypeStruct((D, D), F32)
    encoded, grad_obs, grad_grid, *sums = pl.pallas_call(
        write_kernel,
        out_shape=(
            tile, jax.ShapeDtypeStruct((blocks, BLK, D), BF), tile, matrix, matrix, matrix, matrix,
            jax.ShapeDtypeStruct((5, D), F32),
        ),
        in_specs=[anywhere] * 5 + [vmem],
        out_specs=(anywhere,) * 7 + (vmem,),
        scratch_shapes=[
            pltpu.VMEM((CELLS, D), BF), pltpu.VMEM((blocks, BLK, D), BF), pltpu.VMEM((CELLS, D), BF),
            pltpu.VMEM((2, nlat // 2, n, 3, 16, 128), BF), pltpu.VMEM((2, nlat // 2, n, 1, 16, 128), BF),
            pltpu.VMEM((4, D, D), F32), pltpu.SemaphoreType.DMA((5,)), pltpu.SemaphoreType.DMA((7,)),
        ],
        compiler_params=pltpu.CompilerParams(vmem_limit_bytes=62 * 2**20),
        name="write_results",
    )(*results)
    return (encoded.reshape(tile_shape), grad_grid.reshape(tile_shape), grad_obs, *sums)


def solution(mesh):
    in_specs = (
        P("lat", "lon", None),
        P(("lat", "lon"), None, None),
        P(("lat", "lon"), None),
        P(("lat", "lon"), None),
        P(),
        P(),
        P(),
        P(),
        P(),
        P("lat", "lon", None),
    )
    out_specs = (
        P("lat", "lon", None),
        P("lat", "lon", None),
        P(("lat", "lon"), None, None),
        P(),
        P(),
        P(),
        P(),
        P(),
    )
    return jax.shard_map(
        on_device, mesh=mesh, in_specs=in_specs, out_specs=out_specs, check_vma=False
    )
```

```python
import functools

import jax
import jax.numpy as jnp
from jax import lax
from jax.experimental import pallas as pl
from jax.experimental.pallas import tpu as pltpu
from jax.sharding import PartitionSpec as P

D = 512
HEADS = 8
HD = D // HEADS
BLK = 128
CAP = 2
ROWS = CAP * BLK
CELLS = 256
TILE = 16
SCALING = HD ** (-0.5)
MESH = pl.DeviceIdType.MESH
SIDE = 4
STEPS = (
    (0, 0), (0, 1), (0, 3), (1, 0), (3, 0), (1, 1), (1, 3), (3, 1), (3, 3),
    (0, 2), (2, 0), (1, 2), (3, 2), (2, 1), (2, 3), (2, 2),
)
NEXT, NEAR = 5, 9
EXTRA = 16
BF = jnp.bfloat16
F32 = jnp.float32


def dot(a, b):
    return jnp.dot(a, b, preferred_element_type=F32)


def dot_nt(a, b):
    return lax.dot_general(a, b, (((1,), (1,)), ((), ())), preferred_element_type=F32)


def onehot(rows, cols, hit):
    at = [lax.broadcasted_iota(jnp.int32, (rows, cols), k) for k in range(2)]
    return jnp.where(hit(*at), 1.0, 0.0).astype(BF)


def around(cells, halo, first, last):
    top = jnp.where(first, 0.0, halo[0].astype(F32)).astype(BF)
    bottom = jnp.where(last, 0.0, halo[1].astype(F32)).astype(BF)
    side = TILE
    west = dot(onehot(CELLS, CELLS, lambda q, k: (k == q - 1) & (lax.rem(q, side) != 0)), cells)
    west = west + dot(onehot(CELLS, side, lambda q, k: q == k * side), halo[2])
    east = dot(onehot(CELLS, CELLS, lambda q, k: (k == q + 1) & (lax.rem(q, side) != side - 1)), cells)
    east = east + dot(onehot(CELLS, side, lambda q, k: q == k * side + side - 1), halo[3])
    return (
        jnp.concatenate([top, cells[:-side]], 0).astype(F32),
        jnp.concatenate([cells[side:], bottom], 0).astype(F32),
        west,
        east,
    )


def edges(cells, out):
    out[0] = cells[CELLS - TILE :]
    out[1] = cells[:TILE]
    out[2] = dot(onehot(TILE, CELLS, lambda k, q: q == k * TILE + TILE - 1), cells).astype(BF)
    out[3] = dot(onehot(TILE, CELLS, lambda k, q: q == k * TILE), cells).astype(BF)


class Exchange:
    def __init__(self, count, me, whom, copy):
        self.count, self.me, self.whom, self.copy = count, me, whom, copy

    def each(self, body):
        def step(o, carry):
            body(lax.rem(self.me + o, self.count))
            return carry

        if self.count == 2:
            body(1 - self.me)
        else:
            lax.fori_loop(1, self.count, step, 0)

    def greet(self, barrier):
        self.each(lambda at: pl.semaphore_signal(
            barrier, inc=1, device_id=self.whom(at), device_id_type=MESH))

    def start(self):
        self.each(lambda at: self.copy(at, self.me).start())

    def wait(self):
        self.each(lambda at: self.copy(at, at).wait_recv())

    def sent(self):
        self.each(lambda at: self.copy(at, self.me).wait_send())


def scatter(group, src, dst, ssem, rsem):
    count, me, whom = group
    return Exchange(count, me, whom, lambda to, frm: pltpu.make_async_remote_copy(
        src_ref=src.at[to], dst_ref=dst.at[frm], send_sem=ssem.at[to], recv_sem=rsem.at[frm],
        device_id=whom(to), device_id_type=MESH))


def gather(group, buf, ssem, rsem):
    count, me, whom = group
    return Exchange(count, me, whom, lambda to, frm: pltpu.make_async_remote_copy(
        src_ref=buf.at[me], dst_ref=buf.at[frm], send_sem=ssem.at[to], recv_sem=rsem.at[frm],
        device_id=whom(to), device_id_type=MESH))


class MatrixSum:
    def __init__(self, groups, scratch, out):
        self.core, self.x, self.lon = (group[1] for group in groups)
        self.counts = [group[0] for group in groups]
        self.whole, self.got, self.half, self.got_half, self.piece, self.got_piece = scratch[:6]
        self.out = out
        sems = scratch[6:]
        self.stages = [
            scatter(groups[0], self.whole, self.got, *sems[0:2]),
            scatter(groups[1], self.half, self.got_half, *sems[2:4]),
            scatter(groups[2], self.piece, self.got_piece, *sems[4:6]),
            gather(groups[2], out.at[self.core, self.x], *sems[6:8]),
            gather(groups[1], out.at[self.core], *sems[8:10]),
            gather(groups[0], out, *sems[10:12]),
        ]

    def load(self, number, source):
        per = D // 256
        for c in range(2):
            for x in range(4):
                f = 4 * c + x
                rows = slice((f % per) * 256, (f % per + 1) * 256)
                cols = slice((f // per) * 128, (f // per + 1) * 128)
                self.whole[c, x, :, number] = source(rows, cols).astype(BF).reshape(16, 16, 128)

    def total(self, stage, own, got):
        group = self.stages[stage]
        held = own[group.me].astype(F32)
        for o in range(1, group.count):
            held = held + got[lax.rem(group.me + o, group.count)].astype(F32)
        return held.astype(BF)

    def begin(self):
        self.stages[0].start()

    def step(self, stage):
        self.stages[stage].wait()
        if stage == 0:
            for x in range(4):
                self.half[x] = (
                    self.whole[self.core, x].astype(F32) + self.got[1 - self.core, x].astype(F32)
                ).astype(BF)
        elif stage == 1:
            self.piece[...] = self.total(1, self.half, self.got_half)
        elif stage == 2:
            self.out[self.core, self.x, self.lon] = self.total(2, self.piece, self.got_piece)
        if stage < 5:
            self.stages[stage + 1].start()

    def close(self):
        for stage in self.stages:
            stage.sent()


def kernel(
    nlat, n, dest_ref, count_ref, obs_ref, grid_ref, cot_ref, wq_ref, wk_ref, wv_ref, wo_ref, sten_ref,
    enc_ref, gobs_ref, ggrid_ref, late_ref, early_ref, taps_ref,
    send, xs, ret, relay, relay_back, kv, kt, vt, bias, wkv, qt, qzt, dozt, dot_t,
    acc_o, acc_q, m_ref, l_ref, d_ref, dkvt, dwt, gm_ref, mid_ref, sides, edge, halo, t0, t1,
    x_ssem, x_rsem, r_ssem, r_rsem, g_ssem, g_rsem, b_ssem, b_rsem, h_ssem, h_rsem, t1s, t1r, t2s, t2r,
    *sum_scratch,
):
    lat, me = lax.axis_index("lat"), lax.axis_index("lon")
    groups = n // 2
    blocks = obs_ref.shape[0]
    x_at, core = lat // 2, lax.rem(lat, 2)
    rings = (
        (2, core, lambda at: {"lat": 2 * x_at + at}),
        (nlat // 2, x_at, lambda at: {"lat": 2 * at + core}),
        (n, me, lambda at: {"lon": at}),
    )
    half = len(sum_scratch) // 2
    late = MatrixSum(rings, sum_scratch[:half], late_ref)
    early = MatrixSum(rings, sum_scratch[half:], early_ref)
    tap1 = gather((nlat, lat, lambda at: {"lat": at}), t0, t1s, t1r)
    tap2 = gather(rings[2], t1, t2s, t2r)

    y, z = me // SIDE, lax.rem(me, SIDE)
    way_y, way_z = 1 - 2 * lax.rem(y, 2), 1 - 2 * lax.rem(z, 2)

    def place(dy, dz):
        return lax.rem(y + dy + 2 * SIDE, SIDE) * SIDE + lax.rem(z + dz + 2 * SIDE, SIDE)

    def turned(i):
        return 1 if STEPS[i] in ((0, 2), (2, 0), (2, 2)) else -1

    def leg(i, sign):
        dy, dz = STEPS[i]
        return {"lon": place(
            turned(i) * way_y if dy == 2 else sign * dy, turned(i) * way_z if dz == 2 else sign * dz)}

    def onward(i):
        dy, dz = STEPS[i]
        return {"lon": place(
            -turned(i) * way_y if dy == 2 else 0, -turned(i) * way_z if dz == 2 else 0)}

    barrier = pltpu.get_barrier_semaphore()
    for group in (tap1, tap2):
        group.greet(barrier)

    row_ids = lax.broadcasted_iota(jnp.int32, (EXTRA, D), 0)

    def pack(i):
        tile = place(*STEPS[i])
        number = b0 = b1 = c0 = c1 = jnp.int32(0)
        for b in range(blocks):
            hit = dest_ref[0, b] == tile
            one, two = hit & (number == 0), hit & (number == 1)
            number = number + hit.astype(jnp.int32)
            b0, b1 = jnp.where(one, b, b0), jnp.where(two, b, b1)
            c0, c1 = jnp.where(one, count_ref[0, b], c0), jnp.where(two, count_ref[0, b], c1)
        send[i, 0:BLK, :] = obs_ref[b0]
        send[i, BLK:ROWS, :] = obs_ref[b1]
        send[i, ROWS:, :] = jnp.where(row_ids == 0, c0, c1).astype(F32).astype(BF)

    edges(cot_ref[...], edge.at[0])
    pl.semaphore_wait(barrier, nlat + n - 2)

    def remote(src, dst, ssem, rsem, whom):
        return pltpu.make_async_remote_copy(
            src_ref=src, dst_ref=dst, send_sem=ssem, recv_sem=rsem, device_id=whom, device_id_type=MESH)

    def x_copy(i):
        if i < NEAR:
            return remote(send.at[i], xs.at[i + 1], x_ssem.at[i], x_rsem.at[i], leg(i, 1))
        j = i - NEAR
        return remote(send.at[i], relay.at[j], x_ssem.at[i], r_rsem.at[j], leg(i, 1))

    def x_onward(i):
        j = i - NEAR
        return remote(relay.at[j], xs.at[i + 1], r_ssem.at[j], x_rsem.at[i], onward(i))

    def g_copy(i):
        tokens = send.at[i, pl.ds(0, ROWS)]
        if i < NEAR:
            return remote(tokens, ret.at[i], g_ssem.at[i], g_rsem.at[i], leg(i, -1))
        j = i - NEAR
        return remote(tokens, relay_back.at[j], g_ssem.at[i], b_rsem.at[j], leg(i, -1))

    def g_onward(i):
        j = i - NEAR
        return remote(relay_back.at[j], ret.at[i], b_ssem.at[j], g_rsem.at[i], onward(i))

    def x_arrived(i):
        remote(send.at[0], xs.at[i + 1], x_ssem.at[0], x_rsem.at[i], {"lon": me}).wait_recv()

    def h_copies(which):
        whom = (
            {"lat": lax.rem(lat + 1, nlat)}, {"lat": lax.rem(lat + nlat - 1, nlat)},
            {"lon": lax.rem(me + 1, n)}, {"lon": lax.rem(me + n - 1, n)},
        )
        return [
            remote(edge.at[which, k], halo.at[which, k], h_ssem.at[which, k], h_rsem.at[which, k], whom[k])
            for k in range(4)
        ]

    for copy in h_copies(0):
        copy.start()

    for i in (*range(NEAR, n), *range(1, NEXT)):
        pack(i)
        x_copy(i).start()
    pack(0)

    xs[0, 0:ROWS, :] = grid_ref[...]
    xs[1] = send[0]
    wkv[:, :D] = wk_ref[...]
    wkv[:, D:] = wv_ref[...]
    lanes = lax.broadcasted_iota(jnp.int32, (CELLS, 2 * HD), 1)
    queries = dot(grid_ref[...], wq_ref[...]).astype(BF).astype(F32) * SCALING
    for copy in h_copies(0):
        copy.wait_recv()
    up = cot_ref[...].astype(F32)
    around_up = around(cot_ref[...], halo.at[0], lat == 0, lat == nlat - 1)
    for k in range(4):
        sides[k] = around_up[k].astype(BF)
    up_north, up_south, up_west, up_east = around_up
    gm_ref[...] = (
        (1.0 + sten_ref[0:1, :]) * up + sten_ref[1:2, :] * up_south + sten_ref[2:3, :] * up_north
        + sten_ref[3:4, :] * up_east + sten_ref[4:5, :] * up_west
    ).astype(BF)
    ups = dot_nt(gm_ref[...], wo_ref[...]).astype(BF).astype(F32)
    dot_t[...] = ups.T.astype(BF)
    qt[...] = queries.T.astype(BF)
    for h in range(HEADS):
        p, e = h // 2, h % 2
        mine = (lanes >= HD) if e else (lanes < HD)
        picked = jnp.where(mine, queries[:, p * 2 * HD : (p + 1) * 2 * HD], 0.0)
        qzt[h] = picked.T.astype(BF)
        picked = jnp.where(mine, ups[:, p * 2 * HD : (p + 1) * 2 * HD], 0.0)
        dozt[h] = picked.T.astype(BF)
    acc_o[...] = jnp.zeros_like(acc_o)
    acc_q[...] = jnp.zeros_like(acc_q)
    dwt[...] = jnp.zeros_like(dwt)
    m_ref[...] = jnp.full(m_ref.shape, -1e30, F32)
    l_ref[...] = jnp.zeros_like(l_ref)
    key_ids = lax.broadcasted_iota(jnp.int32, (BLK, 128), 0).astype(F32)

    def masked(width):
        part = bias[0:width, :]
        return jnp.concatenate([part, part], 1)

    def mark(c, w):
        if w == 1:
            bias[0:ROWS, :] = jnp.zeros((ROWS, 128), F32)
            return
        for k in range(w):
            tile = xs[c + k, ROWS:, 0:128].astype(F32)
            for r in range(CAP):
                at = k * ROWS + r * BLK
                bias[at : at + BLK, :] = jnp.where(key_ids < tile[r : r + 1, :], 0.0, -1e30)

    def project(c, w, g):
        width = w * ROWS
        rows = pl.ds(pl.multiple_of(c * ROWS, ROWS), width)
        tokens = xs[pl.ds(c, w), 0:ROWS, :].reshape(width, D)
        for j in range(4):
            cols = slice(j * 256, (j + 1) * 256)
            part = dot(tokens, wkv[:, cols]).astype(BF)
            kv[rows, cols] = part
            if j < 2:
                kt[g, cols, :width] = part.T
            else:
                vt[j * 256 - D : (j + 1) * 256 - D, :width] = part.T

    def attend(c, w):
        width = w * ROWS
        mark(c, w)
        rows = pl.ds(pl.multiple_of(c * ROWS, ROWS), width)

        def four(q, carry):
            for e in range(4):
                h = 4 * q + e
                mine = pl.ds(pl.multiple_of(h * HD, HD), HD)
                here = pl.ds(pl.multiple_of((2 * q + e // 2) * 128, 128), 128)
                scores = dot(kv[rows, here], qzt[h]) + masked(width)
                old = m_ref[h]
                new = jnp.maximum(old, jnp.max(scores, 0, keepdims=True))
                raised = jnp.exp(scores - new)
                shrink = jnp.exp(old - new)
                l_ref[h] = l_ref[h] * shrink + jnp.sum(raised, 0, keepdims=True)
                m_ref[h] = new
                acc_o[mine, :] = acc_o[mine, :] * shrink + dot(vt[mine, :width], raised.astype(BF))
            return carry

        lax.fori_loop(0, HEADS // 4, four, 0)

    project(0, 1, 0)
    attend(0, 1)

    for i in range(NEAR, n):
        x_copy(i).wait_recv()
        x_onward(i).start()

    for i in range(NEXT, NEAR):
        pack(i)

    def forward(step, carry):
        second, third = (step + 6) // 8, (step + 3) // 8
        g = step + 1 + 3 * second + third * (6 - 2 * step)
        c = CAP * g - 1

        @pl.when(step == 2)
        def _():
            for i in range(NEAR, n):
                x_onward(i).wait_send()
            for i in range(NEXT, NEAR):
                x_copy(i).start()

        @pl.when(step >= 1)
        def _():
            x_arrived(c - 1)

        x_arrived(c)
        project(c, 2, g)
        attend(c, 2)
        return carry

    lax.fori_loop(0, groups, forward, 0)

    def up_of():
        return cot_ref[...].astype(F32)

    def finish(h, carry):
        rows = pl.ds(pl.multiple_of(h * HD, HD), HD)
        total = l_ref[h]
        mixed = acc_o[rows, :] / total
        acc_o[rows, :] = mixed
        m_ref[h] = m_ref[h] + jnp.log(total)
        d_ref[h] = jnp.sum(mixed * dot_t[rows, :].astype(F32), 0, keepdims=True)
        return carry

    lax.fori_loop(0, HEADS, finish, 0)
    def middle():
        mid_ref[...] = (
            grid_ref[...].astype(F32) + dot(acc_o[...].T.astype(BF), wo_ref[...])
        ).astype(BF)
        edges(mid_ref[...], edge.at[1])
        for copy in h_copies(1):
            copy.start()
        centre = mid_ref[...].astype(F32)
        t0[lat] = jnp.zeros((8, D), F32)
        for row, side in enumerate((up_of(), *(sides[k].astype(F32) for k in (1, 0, 3, 2)))):
            t0[lat, row : row + 1, :] = jnp.sum(centre * side, 0, keepdims=True)
        tap1.start()
        attended = acc_o[...].astype(BF)
        early.load(0, lambda rows, cols: dot(attended[rows, :], gm_ref[:, cols]))
        early.begin()

    for i in range(1, n):
        x_copy(i).wait_send()

    def differentiate(c, w, g):
        width = w * ROWS
        mark(c, w)
        rows = pl.ds(pl.multiple_of(c * ROWS, ROWS), width)

        def four(q, carry):
            for e in range(4):
                h = 4 * q + e
                pair = (2 * q + e // 2) * 128
                mine = pl.ds(pl.multiple_of(h * HD, HD), HD)
                also = pl.ds(pl.multiple_of(D + h * HD, HD), HD)
                keys = kv[rows, pl.ds(pl.multiple_of(pair, 128), 128)]
                values = kv[rows, pl.ds(pl.multiple_of(D + pair, 128), 128)]
                weights = jnp.exp(dot(keys, qzt[h]) + masked(width) - m_ref[h])
                grads = (weights * (dot(values, dozt[h]) - d_ref[h])).astype(BF)
                dkvt[mine, :width] = dot_nt(qt[mine, :], grads).astype(BF)
                dkvt[also, :width] = dot_nt(dot_t[mine, :], weights.astype(BF)).astype(BF)
                acc_q[mine, :] += dot(kt[g, mine, :width], grads)
            return carry

        lax.fori_loop(0, HEADS // 4, four, 0)

        def weigh(j, carry):
            part = pl.ds(pl.multiple_of(j * 256, 256), 256)
            tokens = xs[pl.ds(c, w), 0:ROWS, :].reshape(width, D)
            dwt[part, :] += dot(dkvt[part, :width], tokens)
            return carry

        lax.fori_loop(0, 4, weigh, 0)

    def backward(step, carry):
        g = groups - step
        differentiate(CAP * g - 1, 2, g)

        def turn(j, inner):
            cols = pl.ds(pl.multiple_of(j * 256, 256), 256)
            part = dot(wkv[cols, :], dkvt[...]).astype(BF).T
            send[pl.ds(CAP * g - 2, 2), 0:ROWS, cols] = part.reshape(2, ROWS, 256)
            return inner

        lax.fori_loop(0, 2, turn, 0)
        for k in range(groups):
            @pl.when(step == k)
            def _(k=k):
                first = CAP * (groups - k) - 2
                if first:
                    g_copy(first).start()
                else:
                    ret[0] = send[0, 0:ROWS, :]
                g_copy(first + 1).start()
                if k >= 2:
                    for i in (first + 4, first + 5):
                        if i >= NEAR:
                            g_copy(i).wait_recv()
                            g_onward(i).start()

        pl.when(step == 0)(middle)

        @pl.when(step == 2)
        def _():
            tap1.wait()
            total = t0[0]
            for i in range(1, nlat):
                total = total + t0[i]
            t1[me] = total
            tap2.start()

        for stage in range(5):
            pl.when(step == stage + 2)(functools.partial(early.step, stage))

        return carry

    lax.fori_loop(0, groups, backward, 0)
    differentiate(0, 1, 0)

    grad_q = (acc_q[...].T * SCALING).astype(BF)
    dwq = dot(grid_ref[...].T, grad_q)
    late.load(0, lambda rows, cols: dwq[rows, cols])
    late.load(1, lambda rows, cols: dwt[cols, rows].astype(BF).T)
    late.load(2, lambda rows, cols: dwt[D + cols.start : D + cols.stop, rows].astype(BF).T)
    late.begin()
    ggrid_ref[...] = (
        gm_ref[...].astype(F32) + dot_nt(grad_q, wq_ref[...])
        + dot(wkv[...], dkvt[:, :CELLS]).T
    ).astype(BF)
    late.step(0)
    for copy in h_copies(1):
        copy.wait_recv()
    north, south, west, east = around(mid_ref[...], halo.at[1], lat == 0, lat == nlat - 1)
    enc_ref[...] = (
        (1.0 + sten_ref[0:1, :]) * mid_ref[...].astype(F32) + sten_ref[1:2, :] * north
        + sten_ref[2:3, :] * south + sten_ref[3:4, :] * west + sten_ref[4:5, :] * east
    ).astype(BF)
    late.step(1)
    for i in range(1, n):
        if i < NEAR:
            g_copy(i).wait_recv()
        else:
            g_onward(i).wait_recv()
        g_copy(i).wait_send()
        if i >= NEAR:
            g_onward(i).wait_send()


    def unpack(b, carry):
        tile = dest_ref[0, b]
        rank = jnp.int32(0)
        for other in range(blocks):
            rank = rank + ((dest_ref[0, other] == tile) & (other < b)).astype(jnp.int32)
        dy = lax.rem(tile // SIDE - y + SIDE, SIDE)
        dz = lax.rem(lax.rem(tile, SIDE) - z + SIDE, SIDE)
        at = jnp.int32(0)
        for i, (sy, sz) in enumerate(STEPS):
            at = jnp.where((dy == sy) & (dz == sz), i, at)
        both = ret[at]
        gobs_ref[b] = jnp.where(rank == 0, both[:BLK], both[BLK:])
        return carry

    lax.fori_loop(0, blocks, unpack, 0)
    late.step(2)
    tap2.wait()
    total = t1[0]
    for i in range(1, n):
        total = total + t1[i]
    taps_ref[...] = total
    late.step(3)
    early.step(5)
    late.step(4)
    late.step(5)
    for part in (tap1, tap2):
        part.sent()
    for part in (early, late):
        part.close()
    for which in range(2):
        for copy in h_copies(which):
            copy.wait_send()


def write_kernel(
    enc, gobs, ggrid, late, early, taps, enc_o, gobs_o, ggrid_o, wq, wk, wv, wo, taps_o,
    enc_v, gobs_v, ggrid_v, late_v, early_v, sums_v, in_sems, out_sems,
):
    pairs = ((late, late_v, None), (early, early_v, None), (gobs, gobs_v, gobs_o), (enc, enc_v, enc_o),
             (ggrid, ggrid_v, ggrid_o))
    loads = [pltpu.make_async_copy(a, b, in_sems.at[k]) for k, (a, b, _) in enumerate(pairs)]
    stores = []

    def store(source, out):
        stores.append(pltpu.make_async_copy(source, out, out_sems.at[len(stores)]))
        stores[-1].start()

    for load in loads:
        load.start()
    taps_o[...] = taps[0:5, :]
    loads[0].wait()
    for k, (out, source, number) in enumerate(
            ((wq, late_v, 0), (wk, late_v, 1), (wv, late_v, 2), (wo, early_v, 0))):
        if k == 3:
            loads[1].wait()
        for f in range(8):
            rows, cols = slice((f % 2) * 256, (f % 2 + 1) * 256), slice((f // 2) * 128, (f // 2 + 1) * 128)
            sums_v[k, rows, cols] = source[f // 4, f % 4, :, number].reshape(256, 128).astype(F32)
        store(sums_v.at[k], out)
        if k < 3:
            loads[2 + k].wait()
            store(pairs[2 + k][1], pairs[2 + k][2])
    for copy in stores:
        copy.wait()


def on_device(
    grid_tokens, obs_tokens, destinations, valid_counts, w_query, w_key, w_value, w_out,
    stencil_taps, cotangent,
):
    tile_shape = grid_tokens.shape
    blocks = obs_tokens.shape[0]
    nlat, n = lax.axis_size("lat"), lax.axis_size("lon")
    vmem = pl.BlockSpec(memory_space=pltpu.VMEM)
    smem = pl.BlockSpec(memory_space=pltpu.SMEM)
    lat_sem, lon_sem = pltpu.SemaphoreType.DMA((nlat,)), pltpu.SemaphoreType.DMA((n,))
    far_sem = pltpu.SemaphoreType.DMA((n - NEAR,))
    halo_sem = pltpu.SemaphoreType.DMA((2, 4))
    x_sem, core_sem = pltpu.SemaphoreType.DMA((nlat // 2,)), pltpu.SemaphoreType.DMA((2,))
    sums = []
    for number in (3, 1):
        whole, part, piece = (
            pltpu.VMEM((*lead, number, 16, 128), BF) for lead in ((2, nlat // 2, n), (nlat // 2, n), (n,))
        )
        sums += [whole, whole, part, part, piece, piece]
        sums += [core_sem, core_sem, x_sem, x_sem, lon_sem, lon_sem]
        sums += [lon_sem, lon_sem, x_sem, x_sem, core_sem, core_sem]
    tile = jax.ShapeDtypeStruct((CELLS, D), BF)
    results = pl.pallas_call(
        functools.partial(kernel, nlat, n),
        out_shape=(
            tile, jax.ShapeDtypeStruct((blocks, BLK, D), BF), tile,
            jax.ShapeDtypeStruct((2, nlat // 2, n, 3, 16, 128), BF),
            jax.ShapeDtypeStruct((2, nlat // 2, n, 1, 16, 128), BF),
            jax.ShapeDtypeStruct((8, D), F32),
        ),
        in_specs=[smem] * 2 + [vmem] * 8,
        out_specs=(vmem,) * 6,
        scratch_shapes=[
            pltpu.VMEM((n, ROWS + EXTRA, D), BF),
            pltpu.VMEM((n + 1, ROWS + EXTRA, D), BF),
            pltpu.VMEM((n, ROWS, D), BF),
            pltpu.VMEM((n - NEAR, ROWS + EXTRA, D), BF),
            pltpu.VMEM((n - NEAR, ROWS, D), BF),
            pltpu.VMEM(((n + 1) * ROWS, 2 * D), BF),
            pltpu.VMEM((n // 2 + 1, D, 2 * ROWS), BF),
            pltpu.VMEM((D, 2 * ROWS), BF),
            pltpu.VMEM((2 * ROWS, 128), F32),
            pltpu.VMEM((D, 2 * D), BF),
            pltpu.VMEM((D, CELLS), BF),
            pltpu.VMEM((HEADS, 2 * HD, CELLS), BF),
            pltpu.VMEM((HEADS, 2 * HD, CELLS), BF),
            pltpu.VMEM((D, CELLS), BF),
            pltpu.VMEM((D, CELLS), F32),
            pltpu.VMEM((D, CELLS), F32),
            pltpu.VMEM((HEADS, 1, CELLS), F32),
            pltpu.VMEM((HEADS, 1, CELLS), F32),
            pltpu.VMEM((HEADS, 1, CELLS), F32),
            pltpu.VMEM((2 * D, 2 * ROWS), BF),
            pltpu.VMEM((2 * D, D), F32),
            pltpu.VMEM((CELLS, D), BF),
            pltpu.VMEM((CELLS, D), BF),
            pltpu.VMEM((4, CELLS, D), BF),
            pltpu.VMEM((2, 4, TILE, D), BF),
            pltpu.VMEM((2, 4, TILE, D), BF),
            pltpu.VMEM((nlat, 8, D), F32),
            pltpu.VMEM((n, 8, D), F32),
            lon_sem, lon_sem, far_sem, far_sem, lon_sem, lon_sem, far_sem, far_sem, halo_sem, halo_sem,
            lat_sem, lat_sem, lon_sem, lon_sem,
            *sums,
        ],
        compiler_params=pltpu.CompilerParams(
            collective_id=0, has_side_effects=True, vmem_limit_bytes=62 * 2**20
        ),
        name="encoder_step",
    )(
        destinations.reshape(1, blocks), valid_counts, obs_tokens, grid_tokens.reshape(CELLS, D),
        cotangent.reshape(CELLS, D), w_query, w_key, w_value, w_out, stencil_taps,
    )
    anywhere = pl.BlockSpec(memory_space=pl.ANY)
    matrix = jax.ShapeDtypeStruct((D, D), F32)
    encoded, grad_obs, grad_grid, *sums = pl.pallas_call(
        write_kernel,
        out_shape=(
            tile, jax.ShapeDtypeStruct((blocks, BLK, D), BF), tile, matrix, matrix, matrix, matrix,
            jax.ShapeDtypeStruct((5, D), F32),
        ),
        in_specs=[anywhere] * 5 + [vmem],
        out_specs=(anywhere,) * 7 + (vmem,),
        scratch_shapes=[
            pltpu.VMEM((CELLS, D), BF), pltpu.VMEM((blocks, BLK, D), BF), pltpu.VMEM((CELLS, D), BF),
            pltpu.VMEM((2, nlat // 2, n, 3, 16, 128), BF), pltpu.VMEM((2, nlat // 2, n, 1, 16, 128), BF),
            pltpu.VMEM((4, D, D), F32), pltpu.SemaphoreType.DMA((5,)), pltpu.SemaphoreType.DMA((7,)),
        ],
        compiler_params=pltpu.CompilerParams(vmem_limit_bytes=62 * 2**20),
        name="write_results",
    )(*results)
    return (encoded.reshape(tile_shape), grad_grid.reshape(tile_shape), grad_obs, *sums)


def solution(mesh):
    in_specs = (
        P("lat", "lon", None),
        P(("lat", "lon"), None, None),
        P(("lat", "lon"), None),
        P(("lat", "lon"), None),
        P(),
        P(),
        P(),
        P(),
        P(),
        P("lat", "lon", None),
    )
    out_specs = (
        P("lat", "lon", None),
        P("lat", "lon", None),
        P(("lat", "lon"), None, None),
        P(),
        P(),
        P(),
        P(),
        P(),
    )
    return jax.shard_map(
        on_device, mesh=mesh, in_specs=in_specs, out_specs=out_specs, check_vma=False
    )
```

```python
import functools

import jax
import jax.numpy as jnp
from jax import lax
from jax.experimental import pallas as pl
from jax.experimental.pallas import tpu as pltpu
from jax.sharding import PartitionSpec as P

D = 512
HEADS = 8
HD = D // HEADS
BLK = 128
CAP = 2
ROWS = CAP * BLK
CELLS = 256
TILE = 16
SCALING = HD ** (-0.5)
MESH = pl.DeviceIdType.MESH
SIDE = 4
STEPS = (
    (0, 0), (0, 1), (0, 3), (1, 0), (3, 0), (1, 1), (1, 3), (3, 1), (3, 3),
    (0, 2), (2, 0), (1, 2), (3, 2), (2, 1), (2, 3), (2, 2),
)
NEXT, NEAR = 5, 9
EXTRA = 16
BF = jnp.bfloat16
F32 = jnp.float32


def dot(a, b):
    return jnp.dot(a, b, preferred_element_type=F32)


def dot_nt(a, b):
    return lax.dot_general(a, b, (((1,), (1,)), ((), ())), preferred_element_type=F32)


def onehot(rows, cols, hit):
    at = [lax.broadcasted_iota(jnp.int32, (rows, cols), k) for k in range(2)]
    return jnp.where(hit(*at), 1.0, 0.0).astype(BF)


def around(cells, halo, first, last):
    top = jnp.where(first, 0.0, halo[0].astype(F32)).astype(BF)
    bottom = jnp.where(last, 0.0, halo[1].astype(F32)).astype(BF)
    side = TILE
    west = dot(onehot(CELLS, CELLS, lambda q, k: (k == q - 1) & (lax.rem(q, side) != 0)), cells)
    west = west + dot(onehot(CELLS, side, lambda q, k: q == k * side), halo[2])
    east = dot(onehot(CELLS, CELLS, lambda q, k: (k == q + 1) & (lax.rem(q, side) != side - 1)), cells)
    east = east + dot(onehot(CELLS, side, lambda q, k: q == k * side + side - 1), halo[3])
    return (
        jnp.concatenate([top, cells[:-side]], 0).astype(F32),
        jnp.concatenate([cells[side:], bottom], 0).astype(F32),
        west,
        east,
    )


def edges(cells, out):
    out[0] = cells[CELLS - TILE :]
    out[1] = cells[:TILE]
    out[2] = dot(onehot(TILE, CELLS, lambda k, q: q == k * TILE + TILE - 1), cells).astype(BF)
    out[3] = dot(onehot(TILE, CELLS, lambda k, q: q == k * TILE), cells).astype(BF)


class Exchange:
    def __init__(self, count, me, whom, copy):
        self.count, self.me, self.whom, self.copy = count, me, whom, copy

    def each(self, body):
        def step(o, carry):
            body(lax.rem(self.me + o, self.count))
            return carry

        if self.count == 2:
            body(1 - self.me)
        else:
            lax.fori_loop(1, self.count, step, 0)

    def start(self):
        self.each(lambda at: self.copy(at, self.me).start())

    def wait(self):
        self.each(lambda at: self.copy(at, at).wait_recv())

    def sent(self):
        self.each(lambda at: self.copy(at, self.me).wait_send())


def scatter(group, src, dst, ssem, rsem):
    count, me, whom = group
    return Exchange(count, me, whom, lambda to, frm: pltpu.make_async_remote_copy(
        src_ref=src.at[to], dst_ref=dst.at[frm], send_sem=ssem.at[to], recv_sem=rsem.at[frm],
        device_id=whom(to), device_id_type=MESH))


def gather(group, buf, ssem, rsem):
    count, me, whom = group
    return Exchange(count, me, whom, lambda to, frm: pltpu.make_async_remote_copy(
        src_ref=buf.at[me], dst_ref=buf.at[frm], send_sem=ssem.at[to], recv_sem=rsem.at[frm],
        device_id=whom(to), device_id_type=MESH))


class MatrixSum:
    def __init__(self, groups, buffers, sems, out):
        self.me = [group[1] for group in groups]
        self.bufs = buffers
        self.out = out
        at, self.stages = out, []
        for k, group in enumerate(groups):
            self.stages.append(scatter(group, buffers[2 * k], buffers[2 * k + 1], *sems[2 * k : 2 * k + 2]))
        for k, group in enumerate(groups):
            self.stages.insert(4, gather(group, at, *sems[8 + 2 * k : 10 + 2 * k]))
            at = at.at[group[1]]
        self.place = at

    def load(self, source):
        per = D // 256
        for c in range(2):
            for x in range(4):
                f = 4 * c + x
                rows = slice((f % per) * 256, (f % per + 1) * 256)
                cols = slice((f // per) * 128, (f // per + 1) * 128)
                self.bufs[0][c, x] = source(rows, cols).astype(BF).reshape(4, 4, 16, 128)

    def begin(self):
        self.stages[0].start()

    def step(self, stage):
        self.stages[stage].wait()
        if stage < 4:
            me, count = self.me[stage], self.stages[stage].count
            own, got = self.bufs[2 * stage], self.bufs[2 * stage + 1]
            held = own[me].astype(F32)
            for o in range(1, count):
                held = held + got[lax.rem(me + o, count)].astype(F32)
            target = self.place if stage == 3 else self.bufs[2 * stage + 2]
            target[...] = held.astype(BF)
        if stage < 7:
            self.stages[stage + 1].start()

    def close(self):
        for stage in self.stages:
            stage.sent()


class TapSum:
    def __init__(self, groups, buffers, sems):
        self.bufs = buffers
        self.stages = [
            gather(group, buffers[k], *sems[2 * k : 2 * k + 2]) for k, group in enumerate(groups)
        ]

    def begin(self):
        self.stages[0].start()

    def step(self, stage, out=None):
        self.stages[stage].wait()
        total = self.bufs[stage][0]
        for k in range(1, self.stages[stage].count):
            total = total + self.bufs[stage][k]
        if stage == 3:
            out[...] = total
        else:
            self.bufs[stage + 1][self.stages[stage + 1].me] = total
            self.stages[stage + 1].start()

    def close(self):
        for stage in self.stages:
            stage.sent()


def kernel(
    nlat, n, dest_ref, count_ref, obs_ref, grid_ref, cot_ref, wq_ref, wk_ref, wv_ref, wo_ref, sten_ref,
    enc_ref, gobs_ref, ggrid_ref, late_ref, early_ref, taps_ref,
    send, xs, ret, relay, relay_back, kv, kt, vt, bias, wkv, qt, qzt, dozt, dot_t,
    acc_o, acc_q, m_ref, l_ref, d_ref, dkvt, dwt, gm_ref, mid_ref, sides, edge, halo,
    x_ssem, x_rsem, r_ssem, r_rsem, g_ssem, g_rsem, b_ssem, b_rsem, h_ssem, h_rsem,
    *sum_scratch,
):
    lat, me = lax.axis_index("lat"), lax.axis_index("lon")
    groups = n // 2
    blocks = obs_ref.shape[0]
    x_at, core = lat // 2, lax.rem(lat, 2)
    y, z = me // SIDE, lax.rem(me, SIDE)
    on_core = (2, core, lambda at: {"lat": 2 * x_at + at})
    on_x = (SIDE, x_at, lambda at: {"lat": 2 * at + core})
    on_y = (SIDE, y, lambda at: {"lon": at * SIDE + z})
    on_z = (SIDE, z, lambda at: {"lon": y * SIDE + at})
    orders = ((on_x, on_y, on_z), (on_y, on_z, on_x), (on_z, on_x, on_y), (on_x, on_y, on_z))
    *late, early = (
        MatrixSum(
            (on_core, *order), sum_scratch[24 * k : 24 * k + 8], sum_scratch[24 * k + 8 : 24 * k + 24],
            late_ref.at[k] if k < 3 else early_ref)
        for k, order in enumerate(orders)
    )
    tap_sum = TapSum((on_core, on_x, on_y, on_z), sum_scratch[96:100], sum_scratch[100:108])

    way_y, way_z = 1 - 2 * lax.rem(y, 2), 1 - 2 * lax.rem(z, 2)

    def place(dy, dz):
        return lax.rem(y + dy + 2 * SIDE, SIDE) * SIDE + lax.rem(z + dz + 2 * SIDE, SIDE)

    def turned(i):
        return 1 if STEPS[i] in ((0, 2), (2, 0), (2, 2)) else -1

    def leg(i, sign):
        dy, dz = STEPS[i]
        return {"lon": place(
            turned(i) * way_y if dy == 2 else sign * dy, turned(i) * way_z if dz == 2 else sign * dz)}

    def onward(i):
        dy, dz = STEPS[i]
        return {"lon": place(
            -turned(i) * way_y if dy == 2 else 0, -turned(i) * way_z if dz == 2 else 0)}

    barrier = pltpu.get_barrier_semaphore()
    def greet(o, carry, axis, count, at):
        pl.semaphore_signal(
            barrier, inc=1, device_id={axis: lax.rem(at + o, count)}, device_id_type=MESH)
        return carry

    lax.fori_loop(1, nlat, functools.partial(greet, axis="lat", count=nlat, at=lat), 0)
    lax.fori_loop(1, n, functools.partial(greet, axis="lon", count=n, at=me), 0)

    row_ids = lax.broadcasted_iota(jnp.int32, (EXTRA, D), 0)

    def pack(i):
        tile = place(*STEPS[i])
        number = b0 = b1 = c0 = c1 = jnp.int32(0)
        for b in range(blocks):
            hit = dest_ref[0, b] == tile
            one, two = hit & (number == 0), hit & (number == 1)
            number = number + hit.astype(jnp.int32)
            b0, b1 = jnp.where(one, b, b0), jnp.where(two, b, b1)
            c0, c1 = jnp.where(one, count_ref[0, b], c0), jnp.where(two, count_ref[0, b], c1)
        send[i, 0:BLK, :] = obs_ref[b0]
        send[i, BLK:ROWS, :] = obs_ref[b1]
        send[i, ROWS:, :] = jnp.where(row_ids == 0, c0, c1).astype(F32).astype(BF)

    edges(cot_ref[...], edge.at[0])
    pl.semaphore_wait(barrier, nlat + n - 2)

    def remote(src, dst, ssem, rsem, whom):
        return pltpu.make_async_remote_copy(
            src_ref=src, dst_ref=dst, send_sem=ssem, recv_sem=rsem, device_id=whom, device_id_type=MESH)

    def x_copy(i):
        if i < NEAR:
            return remote(send.at[i], xs.at[i + 1], x_ssem.at[i], x_rsem.at[i], leg(i, 1))
        j = i - NEAR
        return remote(send.at[i], relay.at[j], x_ssem.at[i], r_rsem.at[j], leg(i, 1))

    def x_onward(i):
        j = i - NEAR
        return remote(relay.at[j], xs.at[i + 1], r_ssem.at[j], x_rsem.at[i], onward(i))

    def g_copy(i):
        tokens = send.at[i, pl.ds(0, ROWS)]
        if i < NEAR:
            return remote(tokens, ret.at[i], g_ssem.at[i], g_rsem.at[i], leg(i, -1))
        j = i - NEAR
        return remote(tokens, relay_back.at[j], g_ssem.at[i], b_rsem.at[j], leg(i, -1))

    def g_onward(i):
        j = i - NEAR
        return remote(relay_back.at[j], ret.at[i], b_ssem.at[j], g_rsem.at[i], onward(i))

    def x_arrived(i):
        remote(send.at[0], xs.at[i + 1], x_ssem.at[0], x_rsem.at[i], {"lon": me}).wait_recv()

    def h_copies(which):
        whom = (
            {"lat": lax.rem(lat + 1, nlat)}, {"lat": lax.rem(lat + nlat - 1, nlat)},
            {"lon": lax.rem(me + 1, n)}, {"lon": lax.rem(me + n - 1, n)},
        )
        return [
            remote(edge.at[which, k], halo.at[which, k], h_ssem.at[which, k], h_rsem.at[which, k], whom[k])
            for k in range(4)
        ]

    for copy in h_copies(0):
        copy.start()

    for i in (*range(NEAR, n), *range(1, NEXT)):
        pack(i)
        x_copy(i).start()
    pack(0)

    xs[0, 0:ROWS, :] = grid_ref[...]
    xs[1] = send[0]
    wkv[:, :D] = wk_ref[...]
    wkv[:, D:] = wv_ref[...]
    lanes = lax.broadcasted_iota(jnp.int32, (CELLS, 2 * HD), 1)
    queries = dot(grid_ref[...], wq_ref[...]).astype(BF).astype(F32) * SCALING
    for copy in h_copies(0):
        copy.wait_recv()
    up = cot_ref[...].astype(F32)
    around_up = around(cot_ref[...], halo.at[0], lat == 0, lat == nlat - 1)
    for k in range(4):
        sides[k] = around_up[k].astype(BF)
    up_north, up_south, up_west, up_east = around_up
    gm_ref[...] = (
        (1.0 + sten_ref[0:1, :]) * up + sten_ref[1:2, :] * up_south + sten_ref[2:3, :] * up_north
        + sten_ref[3:4, :] * up_east + sten_ref[4:5, :] * up_west
    ).astype(BF)
    ups = dot_nt(gm_ref[...], wo_ref[...]).astype(BF).astype(F32)
    dot_t[...] = ups.T.astype(BF)
    qt[...] = queries.T.astype(BF)
    for h in range(HEADS):
        p, e = h // 2, h % 2
        mine = (lanes >= HD) if e else (lanes < HD)
        picked = jnp.where(mine, queries[:, p * 2 * HD : (p + 1) * 2 * HD], 0.0)
        qzt[h] = picked.T.astype(BF)
        picked = jnp.where(mine, ups[:, p * 2 * HD : (p + 1) * 2 * HD], 0.0)
        dozt[h] = picked.T.astype(BF)
    acc_o[...] = jnp.zeros_like(acc_o)
    acc_q[...] = jnp.zeros_like(acc_q)
    dwt[...] = jnp.zeros_like(dwt)
    m_ref[...] = jnp.full(m_ref.shape, -1e30, F32)
    l_ref[...] = jnp.zeros_like(l_ref)
    key_ids = lax.broadcasted_iota(jnp.int32, (BLK, 128), 0).astype(F32)

    def masked(width):
        part = bias[0:width, :]
        return jnp.concatenate([part, part], 1)

    def mark(c, w):
        if w == 1:
            bias[0:ROWS, :] = jnp.zeros((ROWS, 128), F32)
            return
        for k in range(w):
            tile = xs[c + k, ROWS:, 0:128].astype(F32)
            for r in range(CAP):
                at = k * ROWS + r * BLK
                bias[at : at + BLK, :] = jnp.where(key_ids < tile[r : r + 1, :], 0.0, -1e30)

    def project(c, w, g):
        width = w * ROWS
        rows = pl.ds(pl.multiple_of(c * ROWS, ROWS), width)
        tokens = xs[pl.ds(c, w), 0:ROWS, :].reshape(width, D)
        for j in range(4):
            cols = slice(j * 256, (j + 1) * 256)
            part = dot(tokens, wkv[:, cols]).astype(BF)
            kv[rows, cols] = part
            if j < 2:
                kt[g, cols, :width] = part.T
            else:
                vt[j * 256 - D : (j + 1) * 256 - D, :width] = part.T

    def attend(c, w):
        width = w * ROWS
        mark(c, w)
        rows = pl.ds(pl.multiple_of(c * ROWS, ROWS), width)

        def four(q, carry):
            for e in range(4):
                h = 4 * q + e
                mine = pl.ds(pl.multiple_of(h * HD, HD), HD)
                here = pl.ds(pl.multiple_of((2 * q + e // 2) * 128, 128), 128)
                scores = dot(kv[rows, here], qzt[h]) + masked(width)
                old = m_ref[h]
                new = jnp.maximum(old, jnp.max(scores, 0, keepdims=True))
                raised = jnp.exp(scores - new)
                shrink = jnp.exp(old - new)
                l_ref[h] = l_ref[h] * shrink + jnp.sum(raised, 0, keepdims=True)
                m_ref[h] = new
                acc_o[mine, :] = acc_o[mine, :] * shrink + dot(vt[mine, :width], raised.astype(BF))
            return carry

        lax.fori_loop(0, HEADS // 4, four, 0)

    project(0, 1, 0)
    attend(0, 1)

    for i in range(NEAR, n):
        x_copy(i).wait_recv()
        x_onward(i).start()

    for i in range(NEXT, NEAR):
        pack(i)

    def forward(step, carry):
        second, third = (step + 6) // 8, (step + 3) // 8
        g = step + 1 + 3 * second + third * (6 - 2 * step)
        c = CAP * g - 1

        @pl.when(step == 2)
        def _():
            for i in range(NEAR, n):
                x_onward(i).wait_send()
            for i in range(NEXT, NEAR):
                x_copy(i).start()

        @pl.when(step >= 1)
        def _():
            x_arrived(c - 1)

        x_arrived(c)
        project(c, 2, g)
        attend(c, 2)
        return carry

    lax.fori_loop(0, groups, forward, 0)

    def up_of():
        return cot_ref[...].astype(F32)

    def finish(h, carry):
        rows = pl.ds(pl.multiple_of(h * HD, HD), HD)
        total = l_ref[h]
        mixed = acc_o[rows, :] / total
        acc_o[rows, :] = mixed
        m_ref[h] = m_ref[h] + jnp.log(total)
        d_ref[h] = jnp.sum(mixed * dot_t[rows, :].astype(F32), 0, keepdims=True)
        return carry

    lax.fori_loop(0, HEADS, finish, 0)
    def middle():
        mid_ref[...] = (
            grid_ref[...].astype(F32) + dot(acc_o[...].T.astype(BF), wo_ref[...])
        ).astype(BF)
        edges(mid_ref[...], edge.at[1])
        for copy in h_copies(1):
            copy.start()
        centre = mid_ref[...].astype(F32)
        terms = tap_sum.bufs[0]
        terms[core] = jnp.zeros((8, D), F32)
        for row, side in enumerate((up_of(), *(sides[k].astype(F32) for k in (1, 0, 3, 2)))):
            terms[core, row : row + 1, :] = jnp.sum(centre * side, 0, keepdims=True)
        tap_sum.begin()
        attended = acc_o[...].astype(BF)
        early.load(lambda rows, cols: dot(attended[rows, :], gm_ref[:, cols]))
        early.begin()

    for i in range(1, n):
        x_copy(i).wait_send()

    def differentiate(c, w, g):
        width = w * ROWS
        mark(c, w)
        rows = pl.ds(pl.multiple_of(c * ROWS, ROWS), width)

        def four(q, carry):
            for e in range(4):
                h = 4 * q + e
                pair = (2 * q + e // 2) * 128
                mine = pl.ds(pl.multiple_of(h * HD, HD), HD)
                also = pl.ds(pl.multiple_of(D + h * HD, HD), HD)
                keys = kv[rows, pl.ds(pl.multiple_of(pair, 128), 128)]
                values = kv[rows, pl.ds(pl.multiple_of(D + pair, 128), 128)]
                weights = jnp.exp(dot(keys, qzt[h]) + masked(width) - m_ref[h])
                grads = (weights * (dot(values, dozt[h]) - d_ref[h])).astype(BF)
                dkvt[mine, :width] = dot_nt(qt[mine, :], grads).astype(BF)
                dkvt[also, :width] = dot_nt(dot_t[mine, :], weights.astype(BF)).astype(BF)
                acc_q[mine, :] += dot(kt[g, mine, :width], grads)
            return carry

        lax.fori_loop(0, HEADS // 4, four, 0)

        def weigh(j, carry):
            part = pl.ds(pl.multiple_of(j * 256, 256), 256)
            tokens = xs[pl.ds(c, w), 0:ROWS, :].reshape(width, D)
            dwt[part, :] += dot(dkvt[part, :width], tokens)
            return carry

        lax.fori_loop(0, 4, weigh, 0)

    def backward(step, carry):
        g = groups - step
        differentiate(CAP * g - 1, 2, g)

        def turn(j, inner):
            cols = pl.ds(pl.multiple_of(j * 256, 256), 256)
            part = dot(wkv[cols, :], dkvt[...]).astype(BF).T
            send[pl.ds(CAP * g - 2, 2), 0:ROWS, cols] = part.reshape(2, ROWS, 256)
            return inner

        lax.fori_loop(0, 2, turn, 0)
        for k in range(groups):
            @pl.when(step == k)
            def _(k=k):
                first = CAP * (groups - k) - 2
                if first:
                    g_copy(first).start()
                else:
                    ret[0] = send[0, 0:ROWS, :]
                g_copy(first + 1).start()
                if k >= 2:
                    for i in (first + 4, first + 5):
                        if i >= NEAR:
                            g_copy(i).wait_recv()
                            g_onward(i).start()

        pl.when(step == 0)(middle)

        for stage in range(6):
            pl.when(step == stage + 2)(functools.partial(early.step, stage))
        for stage in range(3):
            pl.when(step == stage + 3)(functools.partial(tap_sum.step, stage))

        return carry

    lax.fori_loop(0, groups, backward, 0)
    differentiate(0, 1, 0)

    grad_q = (acc_q[...].T * SCALING).astype(BF)
    dwq = dot(grid_ref[...].T, grad_q)
    late[0].load(lambda rows, cols: dwq[rows, cols])
    late[1].load(lambda rows, cols: dwt[cols, rows].astype(BF).T)
    late[2].load(lambda rows, cols: dwt[D + cols.start : D + cols.stop, rows].astype(BF).T)
    for part in late:
        part.begin()

    def late_step(stage):
        for part in late:
            part.step(stage)

    ggrid_ref[...] = (
        gm_ref[...].astype(F32) + dot_nt(grad_q, wq_ref[...])
        + dot(wkv[...], dkvt[:, :CELLS]).T
    ).astype(BF)
    late_step(0)
    for copy in h_copies(1):
        copy.wait_recv()
    north, south, west, east = around(mid_ref[...], halo.at[1], lat == 0, lat == nlat - 1)
    enc_ref[...] = (
        (1.0 + sten_ref[0:1, :]) * mid_ref[...].astype(F32) + sten_ref[1:2, :] * north
        + sten_ref[2:3, :] * south + sten_ref[3:4, :] * west + sten_ref[4:5, :] * east
    ).astype(BF)
    late_step(1)
    for i in range(1, n):
        if i < NEAR:
            g_copy(i).wait_recv()
        else:
            g_onward(i).wait_recv()
        g_copy(i).wait_send()
        if i >= NEAR:
            g_onward(i).wait_send()


    def unpack(b, carry):
        tile = dest_ref[0, b]
        rank = jnp.int32(0)
        for other in range(blocks):
            rank = rank + ((dest_ref[0, other] == tile) & (other < b)).astype(jnp.int32)
        dy = lax.rem(tile // SIDE - y + SIDE, SIDE)
        dz = lax.rem(lax.rem(tile, SIDE) - z + SIDE, SIDE)
        at = jnp.int32(0)
        for i, (sy, sz) in enumerate(STEPS):
            at = jnp.where((dy == sy) & (dz == sz), i, at)
        both = ret[at]
        gobs_ref[b] = jnp.where(rank == 0, both[:BLK], both[BLK:])
        return carry

    late_step(2)
    lax.fori_loop(0, blocks, unpack, 0)
    late_step(3)
    tap_sum.step(3, taps_ref)
    early.step(6)
    late_step(4)
    early.step(7)
    for stage in range(5, 8):
        late_step(stage)
    tap_sum.close()
    for part in (early, *late):
        part.close()
    for which in range(2):
        for copy in h_copies(which):
            copy.wait_send()


def write_kernel(
    enc, gobs, ggrid, late, early, taps, enc_o, gobs_o, ggrid_o, wq, wk, wv, wo, taps_o,
    enc_v, gobs_v, ggrid_v, late_v, early_v, sums_v, in_sems, out_sems,
):
    pairs = ((late, late_v, None), (early, early_v, None), (gobs, gobs_v, gobs_o), (enc, enc_v, enc_o),
             (ggrid, ggrid_v, ggrid_o))
    loads = [pltpu.make_async_copy(a, b, in_sems.at[k]) for k, (a, b, _) in enumerate(pairs)]
    stores = []

    def store(source, out):
        stores.append(pltpu.make_async_copy(source, out, out_sems.at[len(stores)]))
        stores[-1].start()

    for load in loads:
        load.start()
    taps_o[...] = taps[0:5, :]
    loads[0].wait()
    for out, source, k in (
            (wq, late_v.at[0], 0), (wk, late_v.at[1], 1), (wv, late_v.at[2], 2), (wo, early_v, 3)):
        if k == 3:
            loads[1].wait()
        for f in range(8):
            rows, cols = slice((f % 2) * 256, (f % 2 + 1) * 256), slice((f // 2) * 128, (f // 2 + 1) * 128)
            sums_v[k, rows, cols] = source[f // 4, f % 4].reshape(256, 128).astype(F32)
        store(sums_v.at[k], out)
        if k < 3:
            loads[2 + k].wait()
            store(pairs[2 + k][1], pairs[2 + k][2])
    for copy in stores:
        copy.wait()


def on_device(
    grid_tokens, obs_tokens, destinations, valid_counts, w_query, w_key, w_value, w_out,
    stencil_taps, cotangent,
):
    tile_shape = grid_tokens.shape
    blocks = obs_tokens.shape[0]
    nlat, n = lax.axis_size("lat"), lax.axis_size("lon")
    vmem = pl.BlockSpec(memory_space=pltpu.VMEM)
    smem = pl.BlockSpec(memory_space=pltpu.SMEM)
    lon_sem = pltpu.SemaphoreType.DMA((n,))
    far_sem = pltpu.SemaphoreType.DMA((n - NEAR,))
    halo_sem = pltpu.SemaphoreType.DMA((2, 4))
    ring_sem, core_sem = pltpu.SemaphoreType.DMA((SIDE,)), pltpu.SemaphoreType.DMA((2,))
    sems = [core_sem] * 2 + [ring_sem] * 6
    sums = []
    for _ in range(4):
        for lead in ((2, SIDE, SIDE, SIDE), (SIDE,) * 3, (SIDE,) * 2, (SIDE,)):
            sums += [pltpu.VMEM((*lead, 16, 128), BF)] * 2
        sums += sems * 2
    sums += [pltpu.VMEM((2, 8, D), F32)] + [pltpu.VMEM((SIDE, 8, D), F32)] * 3 + sems
    tile = jax.ShapeDtypeStruct((CELLS, D), BF)
    results = pl.pallas_call(
        functools.partial(kernel, nlat, n),
        out_shape=(
            tile, jax.ShapeDtypeStruct((blocks, BLK, D), BF), tile,
            jax.ShapeDtypeStruct((3, 2, SIDE, SIDE, SIDE, 16, 128), BF),
            jax.ShapeDtypeStruct((2, SIDE, SIDE, SIDE, 16, 128), BF),
            jax.ShapeDtypeStruct((8, D), F32),
        ),
        in_specs=[smem] * 2 + [vmem] * 8,
        out_specs=(vmem,) * 6,
        scratch_shapes=[
            pltpu.VMEM((n, ROWS + EXTRA, D), BF),
            pltpu.VMEM((n + 1, ROWS + EXTRA, D), BF),
            pltpu.VMEM((n, ROWS, D), BF),
            pltpu.VMEM((n - NEAR, ROWS + EXTRA, D), BF),
            pltpu.VMEM((n - NEAR, ROWS, D), BF),
            pltpu.VMEM(((n + 1) * ROWS, 2 * D), BF),
            pltpu.VMEM((n // 2 + 1, D, 2 * ROWS), BF),
            pltpu.VMEM((D, 2 * ROWS), BF),
            pltpu.VMEM((2 * ROWS, 128), F32),
            pltpu.VMEM((D, 2 * D), BF),
            pltpu.VMEM((D, CELLS), BF),
            pltpu.VMEM((HEADS, 2 * HD, CELLS), BF),
            pltpu.VMEM((HEADS, 2 * HD, CELLS), BF),
            pltpu.VMEM((D, CELLS), BF),
            pltpu.VMEM((D, CELLS), F32),
            pltpu.VMEM((D, CELLS), F32),
            pltpu.VMEM((HEADS, 1, CELLS), F32),
            pltpu.VMEM((HEADS, 1, CELLS), F32),
            pltpu.VMEM((HEADS, 1, CELLS), F32),
            pltpu.VMEM((2 * D, 2 * ROWS), BF),
            pltpu.VMEM((2 * D, D), F32),
            pltpu.VMEM((CELLS, D), BF),
            pltpu.VMEM((CELLS, D), BF),
            pltpu.VMEM((4, CELLS, D), BF),
            pltpu.VMEM((2, 4, TILE, D), BF),
            pltpu.VMEM((2, 4, TILE, D), BF),
            lon_sem, lon_sem, far_sem, far_sem, lon_sem, lon_sem, far_sem, far_sem, halo_sem, halo_sem,
            *sums,
        ],
        compiler_params=pltpu.CompilerParams(
            collective_id=0, has_side_effects=True, vmem_limit_bytes=62 * 2**20
        ),
        name="encoder_step",
    )(
        destinations.reshape(1, blocks), valid_counts, obs_tokens, grid_tokens.reshape(CELLS, D),
        cotangent.reshape(CELLS, D), w_query, w_key, w_value, w_out, stencil_taps,
    )
    anywhere = pl.BlockSpec(memory_space=pl.ANY)
    matrix = jax.ShapeDtypeStruct((D, D), F32)
    encoded, grad_obs, grad_grid, *sums = pl.pallas_call(
        write_kernel,
        out_shape=(
            tile, jax.ShapeDtypeStruct((blocks, BLK, D), BF), tile, matrix, matrix, matrix, matrix,
            jax.ShapeDtypeStruct((5, D), F32),
        ),
        in_specs=[anywhere] * 5 + [vmem],
        out_specs=(anywhere,) * 7 + (vmem,),
        scratch_shapes=[
            pltpu.VMEM((CELLS, D), BF), pltpu.VMEM((blocks, BLK, D), BF), pltpu.VMEM((CELLS, D), BF),
            pltpu.VMEM((3, 2, SIDE, SIDE, SIDE, 16, 128), BF), pltpu.VMEM((2, SIDE, SIDE, SIDE, 16, 128), BF),
            pltpu.VMEM((4, D, D), F32), pltpu.SemaphoreType.DMA((5,)), pltpu.SemaphoreType.DMA((7,)),
        ],
        compiler_params=pltpu.CompilerParams(vmem_limit_bytes=62 * 2**20),
        name="write_results",
    )(*results)
    return (encoded.reshape(tile_shape), grad_grid.reshape(tile_shape), grad_obs, *sums)


def solution(mesh):
    in_specs = (
        P("lat", "lon", None),
        P(("lat", "lon"), None, None),
        P(("lat", "lon"), None),
        P(("lat", "lon"), None),
        P(),
        P(),
        P(),
        P(),
        P(),
        P("lat", "lon", None),
    )
    out_specs = (
        P("lat", "lon", None),
        P("lat", "lon", None),
        P(("lat", "lon"), None, None),
        P(),
        P(),
        P(),
        P(),
        P(),
    )
    return jax.shard_map(
        on_device, mesh=mesh, in_specs=in_specs, out_specs=out_specs, check_vma=False
    )
```

```python
import functools

import jax
import jax.numpy as jnp
from jax import lax
from jax.experimental import pallas as pl
from jax.experimental.pallas import tpu as pltpu
from jax.sharding import PartitionSpec as P

D = 512
HEADS = 8
HD = D // HEADS
BLK = 128
CAP = 2
ROWS = CAP * BLK
CELLS = 256
TILE = 16
SCALING = HD ** (-0.5)
MESH = pl.DeviceIdType.MESH
SIDE = 4
STEPS = (
    (0, 0), (0, 1), (0, 3), (1, 0), (3, 0), (1, 1), (1, 3), (3, 1), (3, 3),
    (0, 2), (2, 0), (1, 2), (3, 2), (2, 1), (2, 3), (2, 2),
)
NEXT, NEAR = 5, 9
EXTRA = 16
BF = jnp.bfloat16
F32 = jnp.float32


def dot(a, b):
    return jnp.dot(a, b, preferred_element_type=F32)


def dot_nt(a, b):
    return lax.dot_general(a, b, (((1,), (1,)), ((), ())), preferred_element_type=F32)


def onehot(rows, cols, hit):
    at = [lax.broadcasted_iota(jnp.int32, (rows, cols), k) for k in range(2)]
    return jnp.where(hit(*at), 1.0, 0.0).astype(BF)


def around(cells, halo, first, last):
    top = jnp.where(first, 0.0, halo[0].astype(F32)).astype(BF)
    bottom = jnp.where(last, 0.0, halo[1].astype(F32)).astype(BF)
    side = TILE
    west = dot(onehot(CELLS, CELLS, lambda q, k: (k == q - 1) & (lax.rem(q, side) != 0)), cells)
    west = west + dot(onehot(CELLS, side, lambda q, k: q == k * side), halo[2])
    east = dot(onehot(CELLS, CELLS, lambda q, k: (k == q + 1) & (lax.rem(q, side) != side - 1)), cells)
    east = east + dot(onehot(CELLS, side, lambda q, k: q == k * side + side - 1), halo[3])
    return (
        jnp.concatenate([top, cells[:-side]], 0).astype(F32),
        jnp.concatenate([cells[side:], bottom], 0).astype(F32),
        west,
        east,
    )


def edges(cells, out):
    out[0] = cells[CELLS - TILE :]
    out[1] = cells[:TILE]
    out[2] = dot(onehot(TILE, CELLS, lambda k, q: q == k * TILE + TILE - 1), cells).astype(BF)
    out[3] = dot(onehot(TILE, CELLS, lambda k, q: q == k * TILE), cells).astype(BF)


class Exchange:
    def __init__(self, count, me, whom, copy):
        self.count, self.me, self.whom, self.copy = count, me, whom, copy

    def each(self, body):
        def step(o, carry):
            body(lax.rem(self.me + o, self.count))
            return carry

        if self.count == 2:
            body(1 - self.me)
        else:
            lax.fori_loop(1, self.count, step, 0)

    def start(self):
        self.each(lambda at: self.copy(at, self.me).start())

    def wait(self):
        self.each(lambda at: self.copy(at, at).wait_recv())

    def sent(self):
        self.each(lambda at: self.copy(at, self.me).wait_send())


def scatter(group, src, dst, ssem, rsem):
    count, me, whom = group
    return Exchange(count, me, whom, lambda to, frm: pltpu.make_async_remote_copy(
        src_ref=src.at[to], dst_ref=dst.at[frm], send_sem=ssem.at[to], recv_sem=rsem.at[frm],
        device_id=whom(to), device_id_type=MESH))


def gather(group, buf, ssem, rsem):
    count, me, whom = group
    return Exchange(count, me, whom, lambda to, frm: pltpu.make_async_remote_copy(
        src_ref=buf.at[me], dst_ref=buf.at[frm], send_sem=ssem.at[to], recv_sem=rsem.at[frm],
        device_id=whom(to), device_id_type=MESH))


class MatrixSum:
    def __init__(self, groups, buffers, sems, out):
        self.me = [group[1] for group in groups]
        self.bufs = buffers
        self.out = out
        at, self.stages = out, []
        for k, group in enumerate(groups):
            self.stages.append(scatter(group, buffers[2 * k], buffers[2 * k + 1], *sems[2 * k : 2 * k + 2]))
        for k, group in enumerate(groups):
            self.stages.insert(4, gather(group, at, *sems[8 + 2 * k : 10 + 2 * k]))
            at = at.at[group[1]]
        self.place = at

    def load(self, source):
        per = D // 256
        for c in range(2):
            for x in range(4):
                f = 4 * c + x
                rows = slice((f % per) * 256, (f % per + 1) * 256)
                cols = slice((f // per) * 128, (f // per + 1) * 128)
                self.bufs[0][c, x] = source(rows, cols).astype(BF).reshape(4, 4, 16, 128)

    def begin(self):
        self.stages[0].start()

    def step(self, stage):
        self.stages[stage].wait()
        if stage < 4:
            me, count = self.me[stage], self.stages[stage].count
            own, got = self.bufs[2 * stage], self.bufs[2 * stage + 1]
            held = own[me].astype(F32)
            for o in range(1, count):
                held = held + got[lax.rem(me + o, count)].astype(F32)
            target = self.place if stage == 3 else self.bufs[2 * stage + 2]
            target[...] = held.astype(BF)
        if stage < 7:
            self.stages[stage + 1].start()
        self.stages[stage].sent()


class TapSum:
    def __init__(self, groups, buffers, sems):
        self.bufs = buffers
        self.stages = [
            gather(group, buffers[k], *sems[2 * k : 2 * k + 2]) for k, group in enumerate(groups)
        ]

    def begin(self):
        self.stages[0].start()

    def step(self, stage, out=None):
        self.stages[stage].wait()
        total = self.bufs[stage][0]
        for k in range(1, self.stages[stage].count):
            total = total + self.bufs[stage][k]
        if stage == 3:
            out[...] = total
        else:
            self.bufs[stage + 1][self.stages[stage + 1].me] = total
            self.stages[stage + 1].start()
        self.stages[stage].sent()


def kernel(
    nlat, n, dest_ref, count_ref, obs_ref, grid_ref, cot_ref, wq_ref, wk_ref, wv_ref, wo_ref, sten_ref,
    enc_ref, gobs_ref, ggrid_ref, late_ref, early_ref, taps_ref,
    send, xs, ret, relay, relay_back, kv, kt, vt, bias, wkv, qt, qzt, dozt, dot_t,
    acc_o, acc_q, m_ref, l_ref, d_ref, dkvt, dwt, gm_ref, mid_ref, sides, edge, halo,
    x_ssem, x_rsem, r_ssem, r_rsem, g_ssem, g_rsem, b_ssem, b_rsem, h_ssem, h_rsem,
    *sum_scratch,
):
    lat, me = lax.axis_index("lat"), lax.axis_index("lon")
    groups = n // 2
    blocks = obs_ref.shape[0]
    x_at, core = lat // 2, lax.rem(lat, 2)
    y, z = me // SIDE, lax.rem(me, SIDE)
    on_core = (2, core, lambda at: {"lat": 2 * x_at + at})
    on_x = (SIDE, x_at, lambda at: {"lat": 2 * at + core})
    on_y = (SIDE, y, lambda at: {"lon": at * SIDE + z})
    on_z = (SIDE, z, lambda at: {"lon": y * SIDE + at})
    orders = ((on_x, on_y, on_z), (on_y, on_z, on_x), (on_z, on_x, on_y), (on_x, on_y, on_z))
    *late, early = (
        MatrixSum(
            (on_core, *order), sum_scratch[24 * k : 24 * k + 8], sum_scratch[24 * k + 8 : 24 * k + 24],
            late_ref.at[k] if k < 3 else early_ref)
        for k, order in enumerate(orders)
    )
    tap_sum = TapSum((on_core, on_x, on_y, on_z), sum_scratch[96:100], sum_scratch[100:108])

    way_y, way_z = 1 - 2 * lax.rem(y, 2), 1 - 2 * lax.rem(z, 2)

    def place(dy, dz):
        return lax.rem(y + dy + 2 * SIDE, SIDE) * SIDE + lax.rem(z + dz + 2 * SIDE, SIDE)

    def turned(i):
        return 1 if STEPS[i] in ((0, 2), (2, 0), (2, 2)) else -1

    def leg(i, sign):
        dy, dz = STEPS[i]
        return {"lon": place(
            turned(i) * way_y if dy == 2 else sign * dy, turned(i) * way_z if dz == 2 else sign * dz)}

    def onward(i):
        dy, dz = STEPS[i]
        return {"lon": place(
            -turned(i) * way_y if dy == 2 else 0, -turned(i) * way_z if dz == 2 else 0)}

    barrier = pltpu.get_barrier_semaphore()
    def greet(o, carry, axis, count, at):
        pl.semaphore_signal(
            barrier, inc=1, device_id={axis: lax.rem(at + o, count)}, device_id_type=MESH)
        return carry

    lax.fori_loop(1, nlat, functools.partial(greet, axis="lat", count=nlat, at=lat), 0)
    lax.fori_loop(1, n, functools.partial(greet, axis="lon", count=n, at=me), 0)

    row_ids = lax.broadcasted_iota(jnp.int32, (EXTRA, D), 0)

    def pack(i):
        tile = place(*STEPS[i])
        number = b0 = b1 = c0 = c1 = jnp.int32(0)
        for b in range(blocks):
            hit = dest_ref[0, b] == tile
            one, two = hit & (number == 0), hit & (number == 1)
            number = number + hit.astype(jnp.int32)
            b0, b1 = jnp.where(one, b, b0), jnp.where(two, b, b1)
            c0, c1 = jnp.where(one, count_ref[0, b], c0), jnp.where(two, count_ref[0, b], c1)
        send[i, 0:BLK, :] = obs_ref[b0]
        send[i, BLK:ROWS, :] = obs_ref[b1]
        send[i, ROWS:, :] = jnp.where(row_ids == 0, c0, c1).astype(F32).astype(BF)

    edges(cot_ref[...], edge.at[0])
    pl.semaphore_wait(barrier, nlat + n - 2)

    def remote(src, dst, ssem, rsem, whom):
        return pltpu.make_async_remote_copy(
            src_ref=src, dst_ref=dst, send_sem=ssem, recv_sem=rsem, device_id=whom, device_id_type=MESH)

    def x_copy(i):
        if i < NEAR:
            return remote(send.at[i], xs.at[i + 1], x_ssem.at[i], x_rsem.at[i], leg(i, 1))
        j = i - NEAR
        return remote(send.at[i], relay.at[j], x_ssem.at[i], r_rsem.at[j], leg(i, 1))

    def x_onward(i):
        j = i - NEAR
        return remote(relay.at[j], xs.at[i + 1], r_ssem.at[j], x_rsem.at[i], onward(i))

    def g_copy(i):
        tokens = send.at[i, pl.ds(0, ROWS)]
        if i < NEAR:
            return remote(tokens, ret.at[i], g_ssem.at[i], g_rsem.at[i], leg(i, -1))
        j = i - NEAR
        return remote(tokens, relay_back.at[j], g_ssem.at[i], b_rsem.at[j], leg(i, -1))

    def g_onward(i):
        j = i - NEAR
        return remote(relay_back.at[j], ret.at[i], b_ssem.at[j], g_rsem.at[i], onward(i))

    def x_arrived(i):
        remote(send.at[0], xs.at[i + 1], x_ssem.at[0], x_rsem.at[i], {"lon": me}).wait_recv()

    def h_copies(which):
        whom = (
            {"lat": lax.rem(lat + 1, nlat)}, {"lat": lax.rem(lat + nlat - 1, nlat)},
            {"lon": lax.rem(me + 1, n)}, {"lon": lax.rem(me + n - 1, n)},
        )
        return [
            remote(edge.at[which, k], halo.at[which, k], h_ssem.at[which, k], h_rsem.at[which, k], whom[k])
            for k in range(4)
        ]

    for copy in h_copies(0):
        copy.start()

    for i in (*range(NEAR, n), *range(1, NEXT)):
        pack(i)
        x_copy(i).start()
    pack(0)

    xs[0, 0:ROWS, :] = grid_ref[...]
    xs[1] = send[0]
    wkv[:, :D] = wk_ref[...]
    wkv[:, D:] = wv_ref[...]
    lanes = lax.broadcasted_iota(jnp.int32, (CELLS, 2 * HD), 1)
    queries = dot(grid_ref[...], wq_ref[...]).astype(BF).astype(F32) * SCALING
    for copy in h_copies(0):
        copy.wait_recv()
    up = cot_ref[...].astype(F32)
    around_up = around(cot_ref[...], halo.at[0], lat == 0, lat == nlat - 1)
    for k in range(4):
        sides[k] = around_up[k].astype(BF)
    up_north, up_south, up_west, up_east = around_up
    gm_ref[...] = (
        (1.0 + sten_ref[0:1, :]) * up + sten_ref[1:2, :] * up_south + sten_ref[2:3, :] * up_north
        + sten_ref[3:4, :] * up_east + sten_ref[4:5, :] * up_west
    ).astype(BF)
    ups = dot_nt(gm_ref[...], wo_ref[...]).astype(BF).astype(F32)
    dot_t[...] = ups.T.astype(BF)
    qt[...] = queries.T.astype(BF)
    for h in range(HEADS):
        p, e = h // 2, h % 2
        mine = (lanes >= HD) if e else (lanes < HD)
        picked = jnp.where(mine, queries[:, p * 2 * HD : (p + 1) * 2 * HD], 0.0)
        qzt[h] = picked.T.astype(BF)
        picked = jnp.where(mine, ups[:, p * 2 * HD : (p + 1) * 2 * HD], 0.0)
        dozt[h] = picked.T.astype(BF)
    acc_o[...] = jnp.zeros_like(acc_o)
    acc_q[...] = jnp.zeros_like(acc_q)
    dwt[...] = jnp.zeros_like(dwt)
    m_ref[...] = jnp.full(m_ref.shape, -1e30, F32)
    l_ref[...] = jnp.zeros_like(l_ref)
    key_ids = lax.broadcasted_iota(jnp.int32, (BLK, 128), 0).astype(F32)

    def masked(width):
        part = bias[0:width, :]
        return jnp.concatenate([part, part], 1)

    def mark(c, w):
        if w == 1:
            bias[0:ROWS, :] = jnp.zeros((ROWS, 128), F32)
            return
        for k in range(w):
            tile = xs[c + k, ROWS:, 0:128].astype(F32)
            for r in range(CAP):
                at = k * ROWS + r * BLK
                bias[at : at + BLK, :] = jnp.where(key_ids < tile[r : r + 1, :], 0.0, -1e30)

    def project(c, w, g):
        width = w * ROWS
        rows = pl.ds(pl.multiple_of(c * ROWS, ROWS), width)
        tokens = xs[pl.ds(c, w), 0:ROWS, :].reshape(width, D)
        for j in range(4):
            cols = slice(j * 256, (j + 1) * 256)
            part = dot(tokens, wkv[:, cols]).astype(BF)
            kv[rows, cols] = part
            if j < 2:
                kt[g, cols, :width] = part.T
            else:
                vt[j * 256 - D : (j + 1) * 256 - D, :width] = part.T

    def attend(c, w):
        width = w * ROWS
        mark(c, w)
        rows = pl.ds(pl.multiple_of(c * ROWS, ROWS), width)

        def four(q, carry):
            for e in range(4):
                h = 4 * q + e
                mine = pl.ds(pl.multiple_of(h * HD, HD), HD)
                here = pl.ds(pl.multiple_of((2 * q + e // 2) * 128, 128), 128)
                scores = dot(kv[rows, here], qzt[h]) + masked(width)
                old = m_ref[h]
                new = jnp.maximum(old, jnp.max(scores, 0, keepdims=True))
                raised = jnp.exp(scores - new)
                shrink = jnp.exp(old - new)
                l_ref[h] = l_ref[h] * shrink + jnp.sum(raised, 0, keepdims=True)
                m_ref[h] = new
                acc_o[mine, :] = acc_o[mine, :] * shrink + dot(vt[mine, :width], raised.astype(BF))
            return carry

        lax.fori_loop(0, HEADS // 4, four, 0)

    project(0, 1, 0)
    attend(0, 1)

    for i in range(NEAR, n):
        x_copy(i).wait_recv()
        x_onward(i).start()

    for i in range(NEXT, NEAR):
        pack(i)

    def forward(step, carry):
        second, third = (step + 6) // 8, (step + 3) // 8
        g = step + 1 + 3 * second + third * (6 - 2 * step)
        c = CAP * g - 1

        @pl.when(step == 2)
        def _():
            for i in range(NEAR, n):
                x_onward(i).wait_send()
            for i in range(NEXT, NEAR):
                x_copy(i).start()

        @pl.when(step >= 1)
        def _():
            x_arrived(c - 1)

        x_arrived(c)
        project(c, 2, g)
        attend(c, 2)
        return carry

    lax.fori_loop(0, groups, forward, 0)

    def up_of():
        return cot_ref[...].astype(F32)

    def finish(h, carry):
        rows = pl.ds(pl.multiple_of(h * HD, HD), HD)
        total = l_ref[h]
        mixed = acc_o[rows, :] / total
        acc_o[rows, :] = mixed
        m_ref[h] = m_ref[h] + jnp.log(total)
        d_ref[h] = jnp.sum(mixed * dot_t[rows, :].astype(F32), 0, keepdims=True)
        return carry

    lax.fori_loop(0, HEADS, finish, 0)
    def middle():
        mid_ref[...] = (
            grid_ref[...].astype(F32) + dot(acc_o[...].T.astype(BF), wo_ref[...])
        ).astype(BF)
        edges(mid_ref[...], edge.at[1])
        for copy in h_copies(1):
            copy.start()
        centre = mid_ref[...].astype(F32)
        terms = tap_sum.bufs[0]
        terms[core] = jnp.zeros((8, D), F32)
        for row, side in enumerate((up_of(), *(sides[k].astype(F32) for k in (1, 0, 3, 2)))):
            terms[core, row : row + 1, :] = jnp.sum(centre * side, 0, keepdims=True)
        tap_sum.begin()
        attended = acc_o[...].astype(BF)
        early.load(lambda rows, cols: dot(attended[rows, :], gm_ref[:, cols]))
        early.begin()

    for i in range(1, n):
        x_copy(i).wait_send()

    def differentiate(c, w, g):
        width = w * ROWS
        mark(c, w)
        rows = pl.ds(pl.multiple_of(c * ROWS, ROWS), width)

        def four(q, carry):
            for e in range(4):
                h = 4 * q + e
                pair = (2 * q + e // 2) * 128
                mine = pl.ds(pl.multiple_of(h * HD, HD), HD)
                also = pl.ds(pl.multiple_of(D + h * HD, HD), HD)
                keys = kv[rows, pl.ds(pl.multiple_of(pair, 128), 128)]
                values = kv[rows, pl.ds(pl.multiple_of(D + pair, 128), 128)]
                weights = jnp.exp(dot(keys, qzt[h]) + masked(width) - m_ref[h])
                grads = (weights * (dot(values, dozt[h]) - d_ref[h])).astype(BF)
                dkvt[mine, :width] = dot_nt(qt[mine, :], grads).astype(BF)
                dkvt[also, :width] = dot_nt(dot_t[mine, :], weights.astype(BF)).astype(BF)
                acc_q[mine, :] += dot(kt[g, mine, :width], grads)
            return carry

        lax.fori_loop(0, HEADS // 4, four, 0)

        def weigh(j, carry):
            part = pl.ds(pl.multiple_of(j * 256, 256), 256)
            tokens = xs[pl.ds(c, w), 0:ROWS, :].reshape(width, D)
            dwt[part, :] += dot(dkvt[part, :width], tokens)
            return carry

        lax.fori_loop(0, 4, weigh, 0)

    def backward(step, carry):
        g = groups - step
        differentiate(CAP * g - 1, 2, g)

        def turn(j, inner):
            cols = pl.ds(pl.multiple_of(j * 256, 256), 256)
            part = dot(wkv[cols, :], dkvt[...]).astype(BF).T
            send[pl.ds(CAP * g - 2, 2), 0:ROWS, cols] = part.reshape(2, ROWS, 256)
            return inner

        lax.fori_loop(0, 2, turn, 0)
        for k in range(groups):
            @pl.when(step == k)
            def _(k=k):
                first = CAP * (groups - k) - 2
                if first:
                    g_copy(first).start()
                else:
                    ret[0] = send[0, 0:ROWS, :]
                g_copy(first + 1).start()
                if k >= 4:
                    for i in (first + 8, first + 9):
                        if i >= NEAR:
                            g_copy(i).wait_recv()
                            g_onward(i).start()

        pl.when(step == 0)(middle)

        for stage in range(3):
            pl.when(step == 2 * stage + 2)(functools.partial(early.step, stage))
            pl.when(step == 2 * stage + 3)(functools.partial(tap_sum.step, stage))

        return carry

    lax.fori_loop(0, groups, backward, 0)
    differentiate(0, 1, 0)

    grad_q = (acc_q[...].T * SCALING).astype(BF)
    dwq = dot(grid_ref[...].T, grad_q)
    late[0].load(lambda rows, cols: dwq[rows, cols])
    late[1].load(lambda rows, cols: dwt[cols, rows].astype(BF).T)
    late[2].load(lambda rows, cols: dwt[D + cols.start : D + cols.stop, rows].astype(BF).T)
    for part in late:
        part.begin()
    early.step(3)

    def late_step(stage):
        if stage < 4:
            early.step(stage + 4)
        for part in late:
            part.step(stage)

    ggrid_ref[...] = (
        gm_ref[...].astype(F32) + dot_nt(grad_q, wq_ref[...])
        + dot(wkv[...], dkvt[:, :CELLS]).T
    ).astype(BF)
    late_step(0)
    for copy in h_copies(1):
        copy.wait_recv()
    north, south, west, east = around(mid_ref[...], halo.at[1], lat == 0, lat == nlat - 1)
    enc_ref[...] = (
        (1.0 + sten_ref[0:1, :]) * mid_ref[...].astype(F32) + sten_ref[1:2, :] * north
        + sten_ref[2:3, :] * south + sten_ref[3:4, :] * west + sten_ref[4:5, :] * east
    ).astype(BF)
    late_step(1)
    for i in range(1, n):
        if i < NEAR:
            g_copy(i).wait_recv()
        else:
            g_onward(i).wait_recv()
        g_copy(i).wait_send()
        if i >= NEAR:
            g_onward(i).wait_send()


    def unpack(b, carry):
        tile = dest_ref[0, b]
        rank = jnp.int32(0)
        for other in range(blocks):
            rank = rank + ((dest_ref[0, other] == tile) & (other < b)).astype(jnp.int32)
        dy = lax.rem(tile // SIDE - y + SIDE, SIDE)
        dz = lax.rem(lax.rem(tile, SIDE) - z + SIDE, SIDE)
        at = jnp.int32(0)
        for i, (sy, sz) in enumerate(STEPS):
            at = jnp.where((dy == sy) & (dz == sz), i, at)
        both = ret[at]
        gobs_ref[b] = jnp.where(rank == 0, both[:BLK], both[BLK:])
        return carry

    late_step(2)
    lax.fori_loop(0, blocks, unpack, 0)
    late_step(3)
    tap_sum.step(3, taps_ref)
    for stage in range(4, 8):
        late_step(stage)
    for which in range(2):
        for copy in h_copies(which):
            copy.wait_send()


def write_kernel(
    enc, gobs, ggrid, late, early, taps, enc_o, gobs_o, ggrid_o, wq, wk, wv, wo, taps_o,
    enc_v, gobs_v, ggrid_v, late_v, early_v, sums_v, in_sems, out_sems,
):
    pairs = ((late, late_v, None), (early, early_v, None), (gobs, gobs_v, gobs_o), (enc, enc_v, enc_o),
             (ggrid, ggrid_v, ggrid_o))
    loads = [pltpu.make_async_copy(a, b, in_sems.at[k]) for k, (a, b, _) in enumerate(pairs)]
    stores = []

    def store(source, out):
        stores.append(pltpu.make_async_copy(source, out, out_sems.at[len(stores)]))
        stores[-1].start()

    for load in loads:
        load.start()
    taps_o[...] = taps[0:5, :]
    loads[0].wait()
    for out, source, k in (
            (wq, late_v.at[0], 0), (wk, late_v.at[1], 1), (wv, late_v.at[2], 2), (wo, early_v, 3)):
        if k == 3:
            loads[1].wait()
        for f in range(8):
            rows, cols = slice((f % 2) * 256, (f % 2 + 1) * 256), slice((f // 2) * 128, (f // 2 + 1) * 128)
            sums_v[k, rows, cols] = source[f // 4, f % 4].reshape(256, 128).astype(F32)
        store(sums_v.at[k], out)
        if k < 3:
            loads[2 + k].wait()
            store(pairs[2 + k][1], pairs[2 + k][2])
    for copy in stores:
        copy.wait()


def on_device(
    grid_tokens, obs_tokens, destinations, valid_counts, w_query, w_key, w_value, w_out,
    stencil_taps, cotangent,
):
    tile_shape = grid_tokens.shape
    blocks = obs_tokens.shape[0]
    nlat, n = lax.axis_size("lat"), lax.axis_size("lon")
    vmem = pl.BlockSpec(memory_space=pltpu.VMEM)
    smem = pl.BlockSpec(memory_space=pltpu.SMEM)
    lon_sem = pltpu.SemaphoreType.DMA((n,))
    far_sem = pltpu.SemaphoreType.DMA((n - NEAR,))
    halo_sem = pltpu.SemaphoreType.DMA((2, 4))
    ring_sem, core_sem = pltpu.SemaphoreType.DMA((SIDE,)), pltpu.SemaphoreType.DMA((2,))
    sems = [core_sem] * 2 + [ring_sem] * 6
    sums = []
    for _ in range(4):
        for lead in ((2, SIDE, SIDE, SIDE), (SIDE,) * 3, (SIDE,) * 2, (SIDE,)):
            sums += [pltpu.VMEM((*lead, 16, 128), BF)] * 2
        sums += sems * 2
    sums += [pltpu.VMEM((2, 8, D), F32)] + [pltpu.VMEM((SIDE, 8, D), F32)] * 3 + sems
    tile = jax.ShapeDtypeStruct((CELLS, D), BF)
    results = pl.pallas_call(
        functools.partial(kernel, nlat, n),
        out_shape=(
            tile, jax.ShapeDtypeStruct((blocks, BLK, D), BF), tile,
            jax.ShapeDtypeStruct((3, 2, SIDE, SIDE, SIDE, 16, 128), BF),
            jax.ShapeDtypeStruct((2, SIDE, SIDE, SIDE, 16, 128), BF),
            jax.ShapeDtypeStruct((8, D), F32),
        ),
        in_specs=[smem] * 2 + [vmem] * 8,
        out_specs=(vmem,) * 6,
        scratch_shapes=[
            pltpu.VMEM((n, ROWS + EXTRA, D), BF),
            pltpu.VMEM((n + 1, ROWS + EXTRA, D), BF),
            pltpu.VMEM((n, ROWS, D), BF),
            pltpu.VMEM((n - NEAR, ROWS + EXTRA, D), BF),
            pltpu.VMEM((n - NEAR, ROWS, D), BF),
            pltpu.VMEM(((n + 1) * ROWS, 2 * D), BF),
            pltpu.VMEM((n // 2 + 1, D, 2 * ROWS), BF),
            pltpu.VMEM((D, 2 * ROWS), BF),
            pltpu.VMEM((2 * ROWS, 128), F32),
            pltpu.VMEM((D, 2 * D), BF),
            pltpu.VMEM((D, CELLS), BF),
            pltpu.VMEM((HEADS, 2 * HD, CELLS), BF),
            pltpu.VMEM((HEADS, 2 * HD, CELLS), BF),
            pltpu.VMEM((D, CELLS), BF),
            pltpu.VMEM((D, CELLS), F32),
            pltpu.VMEM((D, CELLS), F32),
            pltpu.VMEM((HEADS, 1, CELLS), F32),
            pltpu.VMEM((HEADS, 1, CELLS), F32),
            pltpu.VMEM((HEADS, 1, CELLS), F32),
            pltpu.VMEM((2 * D, 2 * ROWS), BF),
            pltpu.VMEM((2 * D, D), F32),
            pltpu.VMEM((CELLS, D), BF),
            pltpu.VMEM((CELLS, D), BF),
            pltpu.VMEM((4, CELLS, D), BF),
            pltpu.VMEM((2, 4, TILE, D), BF),
            pltpu.VMEM((2, 4, TILE, D), BF),
            lon_sem, lon_sem, far_sem, far_sem, lon_sem, lon_sem, far_sem, far_sem, halo_sem, halo_sem,
            *sums,
        ],
        compiler_params=pltpu.CompilerParams(
            collective_id=0, has_side_effects=True, vmem_limit_bytes=62 * 2**20
        ),
        name="encoder_step",
    )(
        destinations.reshape(1, blocks), valid_counts, obs_tokens, grid_tokens.reshape(CELLS, D),
        cotangent.reshape(CELLS, D), w_query, w_key, w_value, w_out, stencil_taps,
    )
    anywhere = pl.BlockSpec(memory_space=pl.ANY)
    matrix = jax.ShapeDtypeStruct((D, D), F32)
    encoded, grad_obs, grad_grid, *sums = pl.pallas_call(
        write_kernel,
        out_shape=(
            tile, jax.ShapeDtypeStruct((blocks, BLK, D), BF), tile, matrix, matrix, matrix, matrix,
            jax.ShapeDtypeStruct((5, D), F32),
        ),
        in_specs=[anywhere] * 5 + [vmem],
        out_specs=(anywhere,) * 7 + (vmem,),
        scratch_shapes=[
            pltpu.VMEM((CELLS, D), BF), pltpu.VMEM((blocks, BLK, D), BF), pltpu.VMEM((CELLS, D), BF),
            pltpu.VMEM((3, 2, SIDE, SIDE, SIDE, 16, 128), BF), pltpu.VMEM((2, SIDE, SIDE, SIDE, 16, 128), BF),
            pltpu.VMEM((4, D, D), F32), pltpu.SemaphoreType.DMA((5,)), pltpu.SemaphoreType.DMA((7,)),
        ],
        compiler_params=pltpu.CompilerParams(vmem_limit_bytes=62 * 2**20),
        name="write_results",
    )(*results)
    return (encoded.reshape(tile_shape), grad_grid.reshape(tile_shape), grad_obs, *sums)


def solution(mesh):
    in_specs = (
        P("lat", "lon", None),
        P(("lat", "lon"), None, None),
        P(("lat", "lon"), None),
        P(("lat", "lon"), None),
        P(),
        P(),
        P(),
        P(),
        P(),
        P("lat", "lon", None),
    )
    out_specs = (
        P("lat", "lon", None),
        P("lat", "lon", None),
        P(("lat", "lon"), None, None),
        P(),
        P(),
        P(),
        P(),
        P(),
    )
    return jax.shard_map(
        on_device, mesh=mesh, in_specs=in_specs, out_specs=out_specs, check_vma=False
    )
```

```python
import functools

import jax
import jax.numpy as jnp
from jax import lax
from jax.experimental import pallas as pl
from jax.experimental.pallas import tpu as pltpu
from jax.sharding import PartitionSpec as P

D = 512
HEADS = 8
HD = D // HEADS
BLK = 128
CAP = 2
ROWS = CAP * BLK
CELLS = 256
TILE = 16
SCALING = HD ** (-0.5)
MESH = pl.DeviceIdType.MESH
SIDE = 4
STEPS = (
    (0, 0), (0, 1), (0, 3), (1, 0), (3, 0),
    (0, 2), (2, 0), (1, 2), (3, 2), (2, 1), (2, 3), (2, 2),
    (1, 1), (1, 3), (3, 1), (3, 3),
)
FAR = range(5, 12)
DIAGONAL = range(12, 16)
BACK = (6, 5, 4, 3, 8, 7, 2, 1)
EXTRA = 16
BF = jnp.bfloat16
F32 = jnp.float32


def dot(a, b):
    return jnp.dot(a, b, preferred_element_type=F32)


def dot_nt(a, b):
    return lax.dot_general(a, b, (((1,), (1,)), ((), ())), preferred_element_type=F32)


def onehot(rows, cols, hit):
    at = [lax.broadcasted_iota(jnp.int32, (rows, cols), k) for k in range(2)]
    return jnp.where(hit(*at), 1.0, 0.0).astype(BF)


def around(cells, halo, first, last):
    top = jnp.where(first, 0.0, halo[0].astype(F32)).astype(BF)
    bottom = jnp.where(last, 0.0, halo[1].astype(F32)).astype(BF)
    side = TILE
    west = dot(onehot(CELLS, CELLS, lambda q, k: (k == q - 1) & (lax.rem(q, side) != 0)), cells)
    west = west + dot(onehot(CELLS, side, lambda q, k: q == k * side), halo[2])
    east = dot(onehot(CELLS, CELLS, lambda q, k: (k == q + 1) & (lax.rem(q, side) != side - 1)), cells)
    east = east + dot(onehot(CELLS, side, lambda q, k: q == k * side + side - 1), halo[3])
    return (
        jnp.concatenate([top, cells[:-side]], 0).astype(F32),
        jnp.concatenate([cells[side:], bottom], 0).astype(F32),
        west,
        east,
    )


def edges(cells, out):
    out[0] = cells[CELLS - TILE :]
    out[1] = cells[:TILE]
    out[2] = dot(onehot(TILE, CELLS, lambda k, q: q == k * TILE + TILE - 1), cells).astype(BF)
    out[3] = dot(onehot(TILE, CELLS, lambda k, q: q == k * TILE), cells).astype(BF)


class Exchange:
    def __init__(self, count, me, whom, copy):
        self.count, self.me, self.whom, self.copy = count, me, whom, copy

    def each(self, body):
        def step(o, carry):
            body(lax.rem(self.me + o, self.count))
            return carry

        if self.count == 2:
            body(1 - self.me)
        else:
            lax.fori_loop(1, self.count, step, 0)

    def start(self):
        self.each(lambda at: self.copy(at, self.me).start())

    def wait(self):
        self.each(lambda at: self.copy(at, at).wait_recv())

    def sent(self):
        self.each(lambda at: self.copy(at, self.me).wait_send())


def scatter(group, src, dst, ssem, rsem):
    count, me, whom = group
    return Exchange(count, me, whom, lambda to, frm: pltpu.make_async_remote_copy(
        src_ref=src.at[to], dst_ref=dst.at[frm], send_sem=ssem.at[to], recv_sem=rsem.at[frm],
        device_id=whom(to), device_id_type=MESH))


def gather(group, buf, ssem, rsem):
    count, me, whom = group
    return Exchange(count, me, whom, lambda to, frm: pltpu.make_async_remote_copy(
        src_ref=buf.at[me], dst_ref=buf.at[frm], send_sem=ssem.at[to], recv_sem=rsem.at[frm],
        device_id=whom(to), device_id_type=MESH))


class MatrixSum:
    def __init__(self, groups, buffers, sems, out):
        self.me = [group[1] for group in groups]
        self.bufs = buffers
        self.out = out
        at, self.stages = out, []
        for k, group in enumerate(groups):
            self.stages.append(scatter(group, buffers[2 * k], buffers[2 * k + 1], *sems[2 * k : 2 * k + 2]))
        for k, group in enumerate(groups):
            self.stages.insert(4, gather(group, at, *sems[8 + 2 * k : 10 + 2 * k]))
            at = at.at[group[1]]
        self.place = at

    def load(self, source):
        per = D // 256
        for c in range(2):
            for x in range(4):
                f = 4 * c + x
                rows = slice((f % per) * 256, (f % per + 1) * 256)
                cols = slice((f // per) * 128, (f // per + 1) * 128)
                self.bufs[0][c, x] = source(rows, cols).astype(BF).reshape(4, 4, 16, 128)

    def begin(self):
        self.stages[0].start()

    def step(self, stage):
        self.stages[stage].wait()
        if stage < 4:
            me, count = self.me[stage], self.stages[stage].count
            own, got = self.bufs[2 * stage], self.bufs[2 * stage + 1]
            held = own[me].astype(F32)
            for o in range(1, count):
                held = held + got[lax.rem(me + o, count)].astype(F32)
            target = self.place if stage == 3 else self.bufs[2 * stage + 2]
            target[...] = held.astype(BF)
        if stage < 7:
            self.stages[stage + 1].start()
        self.stages[stage].sent()


class TapSum:
    def __init__(self, groups, buffers, sems):
        self.bufs = buffers
        self.stages = [
            gather(group, buffers[k], *sems[2 * k : 2 * k + 2]) for k, group in enumerate(groups)
        ]

    def begin(self):
        self.stages[0].start()

    def step(self, stage, out=None):
        self.stages[stage].wait()
        total = self.bufs[stage][0]
        for k in range(1, self.stages[stage].count):
            total = total + self.bufs[stage][k]
        if stage == 3:
            out[...] = total
        else:
            self.bufs[stage + 1][self.stages[stage + 1].me] = total
            self.stages[stage + 1].start()
        self.stages[stage].sent()


def kernel(
    nlat, n, dest_ref, count_ref, grid_ref, cot_ref, sten_ref, obs_in, wq_in, wk_in, wv_in, wo_in,
    enc_out, gobs_out, ggrid_out, late_ref, early_ref, taps_ref,
    send, xs, ret, relay, relay_back, kv, kt, vt, bias, wkv, qt, qzt, dozt, dot_t,
    acc_o, acc_q, m_ref, l_ref, d_ref, dkvt, dwt, gm_ref, mid_ref, sides, edge, halo,
    obs_ref, wq_ref, wo_ref, enc_ref, gobs_ref, ggrid_ref, in_sem, out_sem,
    x_ssem, x_rsem, r_ssem, r_rsem, g_ssem, g_rsem, b_ssem, b_rsem, h_ssem, h_rsem,
    *sum_scratch,
):
    lat, me = lax.axis_index("lat"), lax.axis_index("lon")
    groups = n // 2
    blocks = obs_ref.shape[0]
    loads = [
        pltpu.make_async_copy(source, target, in_sem.at[k])
        for k, (source, target) in enumerate((
            (obs_in, obs_ref), (wq_in, wq_ref), (wk_in, wkv.at[:, pl.ds(0, D)]),
            (wv_in, wkv.at[:, pl.ds(D, D)]), (wo_in, wo_ref)))
    ]
    stores = [
        pltpu.make_async_copy(source, target, out_sem.at[k])
        for k, (source, target) in enumerate((
            (ggrid_ref, ggrid_out), (enc_ref, enc_out), (gobs_ref, gobs_out)))
    ]
    x_at, core = lat // 2, lax.rem(lat, 2)
    y, z = me // SIDE, lax.rem(me, SIDE)
    on_core = (2, core, lambda at: {"lat": 2 * x_at + at})
    on_x = (SIDE, x_at, lambda at: {"lat": 2 * at + core})
    on_y = (SIDE, y, lambda at: {"lon": at * SIDE + z})
    on_z = (SIDE, z, lambda at: {"lon": y * SIDE + at})
    orders = ((on_x, on_y, on_z), (on_y, on_z, on_x), (on_z, on_x, on_y), (on_x, on_y, on_z))
    *late, early = (
        MatrixSum(
            (on_core, *order), sum_scratch[24 * k : 24 * k + 8], sum_scratch[24 * k + 8 : 24 * k + 24],
            late_ref.at[k] if k < 3 else early_ref)
        for k, order in enumerate(orders)
    )
    tap_sum = TapSum((on_core, on_x, on_y, on_z), sum_scratch[96:100], sum_scratch[100:108])

    way_y, way_z = 1 - 2 * lax.rem(y, 2), 1 - 2 * lax.rem(z, 2)

    def place(dy, dz):
        return lax.rem(y + dy + 2 * SIDE, SIDE) * SIDE + lax.rem(z + dz + 2 * SIDE, SIDE)

    def turned(i):
        return 1 if STEPS[i] in ((0, 2), (2, 0), (2, 2)) else -1

    def leg(i, sign):
        dy, dz = STEPS[i]
        return {"lon": place(
            turned(i) * way_y if dy == 2 else sign * dy, turned(i) * way_z if dz == 2 else sign * dz)}

    def onward(i):
        dy, dz = STEPS[i]
        return {"lon": place(
            -turned(i) * way_y if dy == 2 else 0, -turned(i) * way_z if dz == 2 else 0)}

    for load in loads:
        load.start()
    barrier = pltpu.get_barrier_semaphore()
    def greet(o, carry, axis, count, at):
        pl.semaphore_signal(
            barrier, inc=1, device_id={axis: lax.rem(at + o, count)}, device_id_type=MESH)
        return carry

    lax.fori_loop(1, nlat, functools.partial(greet, axis="lat", count=nlat, at=lat), 0)
    lax.fori_loop(1, n, functools.partial(greet, axis="lon", count=n, at=me), 0)

    row_ids = lax.broadcasted_iota(jnp.int32, (EXTRA, D), 0)

    def pack(i):
        tile = place(*STEPS[i])
        number = b0 = b1 = c0 = c1 = jnp.int32(0)
        for b in range(blocks):
            hit = dest_ref[0, b] == tile
            one, two = hit & (number == 0), hit & (number == 1)
            number = number + hit.astype(jnp.int32)
            b0, b1 = jnp.where(one, b, b0), jnp.where(two, b, b1)
            c0, c1 = jnp.where(one, count_ref[0, b], c0), jnp.where(two, count_ref[0, b], c1)
        send[i, 0:BLK, :] = obs_ref[b0]
        send[i, BLK:ROWS, :] = obs_ref[b1]
        send[i, ROWS:, :] = jnp.where(row_ids == 0, c0, c1).astype(F32).astype(BF)

    edges(cot_ref[...], edge.at[0])
    loads[0].wait()
    pl.semaphore_wait(barrier, nlat + n - 2)

    def remote(src, dst, ssem, rsem, whom):
        return pltpu.make_async_remote_copy(
            src_ref=src, dst_ref=dst, send_sem=ssem, recv_sem=rsem, device_id=whom, device_id_type=MESH)

    def x_copy(i):
        if i not in FAR:
            return remote(send.at[i], xs.at[i + 1], x_ssem.at[i], x_rsem.at[i], leg(i, 1))
        j = i - FAR.start
        return remote(send.at[i], relay.at[j], x_ssem.at[i], r_rsem.at[j], leg(i, 1))

    def x_onward(i):
        j = i - FAR.start
        return remote(relay.at[j], xs.at[i + 1], r_ssem.at[j], x_rsem.at[i], onward(i))

    def g_copy(i):
        tokens = send.at[i, pl.ds(0, ROWS)]
        if i not in FAR:
            return remote(tokens, ret.at[i], g_ssem.at[i], g_rsem.at[i], leg(i, -1))
        j = i - FAR.start
        return remote(tokens, relay_back.at[j], g_ssem.at[i], b_rsem.at[j], leg(i, -1))

    def g_onward(i):
        j = i - FAR.start
        return remote(relay_back.at[j], ret.at[i], b_ssem.at[j], g_rsem.at[i], onward(i))

    def x_arrived(i):
        remote(send.at[0], xs.at[i + 1], x_ssem.at[0], x_rsem.at[i], {"lon": me}).wait_recv()

    def h_copies(which):
        whom = (
            {"lat": lax.rem(lat + 1, nlat)}, {"lat": lax.rem(lat + nlat - 1, nlat)},
            {"lon": lax.rem(me + 1, n)}, {"lon": lax.rem(me + n - 1, n)},
        )
        return [
            remote(edge.at[which, k], halo.at[which, k], h_ssem.at[which, k], h_rsem.at[which, k], whom[k])
            for k in range(4)
        ]

    for copy in h_copies(0):
        copy.start()

    for i in (*FAR, *range(1, FAR.start)):
        pack(i)
        x_copy(i).start()
    pack(0)

    xs[0, 0:ROWS, :] = grid_ref[...]
    xs[1] = send[0]
    for load in loads[1:]:
        load.wait()
    lanes = lax.broadcasted_iota(jnp.int32, (CELLS, 2 * HD), 1)
    queries = dot(grid_ref[...], wq_ref[...]).astype(BF).astype(F32) * SCALING
    for copy in h_copies(0):
        copy.wait_recv()
    up = cot_ref[...].astype(F32)
    around_up = around(cot_ref[...], halo.at[0], lat == 0, lat == nlat - 1)
    for k in range(4):
        sides[k] = around_up[k].astype(BF)
    up_north, up_south, up_west, up_east = around_up
    gm_ref[...] = (
        (1.0 + sten_ref[0:1, :]) * up + sten_ref[1:2, :] * up_south + sten_ref[2:3, :] * up_north
        + sten_ref[3:4, :] * up_east + sten_ref[4:5, :] * up_west
    ).astype(BF)
    ups = dot_nt(gm_ref[...], wo_ref[...]).astype(BF).astype(F32)
    dot_t[...] = ups.T.astype(BF)
    qt[...] = queries.T.astype(BF)
    for h in range(HEADS):
        p, e = h // 2, h % 2
        mine = (lanes >= HD) if e else (lanes < HD)
        picked = jnp.where(mine, queries[:, p * 2 * HD : (p + 1) * 2 * HD], 0.0)
        qzt[h] = picked.T.astype(BF)
        picked = jnp.where(mine, ups[:, p * 2 * HD : (p + 1) * 2 * HD], 0.0)
        dozt[h] = picked.T.astype(BF)
    acc_o[...] = jnp.zeros_like(acc_o)
    acc_q[...] = jnp.zeros_like(acc_q)
    dwt[...] = jnp.zeros_like(dwt)
    m_ref[...] = jnp.full(m_ref.shape, -1e30, F32)
    l_ref[...] = jnp.zeros_like(l_ref)
    key_ids = lax.broadcasted_iota(jnp.int32, (BLK, 128), 0).astype(F32)

    def masked(width):
        part = bias[0:width, :]
        return jnp.concatenate([part, part], 1)

    def mark(c, w):
        if w == 1:
            bias[0:ROWS, :] = jnp.zeros((ROWS, 128), F32)
            return
        for k in range(w):
            tile = xs[c + k, ROWS:, 0:128].astype(F32)
            for r in range(CAP):
                at = k * ROWS + r * BLK
                bias[at : at + BLK, :] = jnp.where(key_ids < tile[r : r + 1, :], 0.0, -1e30)

    def project(c, w, g):
        width = w * ROWS
        rows = pl.ds(pl.multiple_of(c * ROWS, ROWS), width)
        tokens = xs[pl.ds(c, w), 0:ROWS, :].reshape(width, D)
        for j in range(4):
            cols = slice(j * 256, (j + 1) * 256)
            part = dot(tokens, wkv[:, cols]).astype(BF)
            kv[rows, cols] = part
            if j < 2:
                kt[g, cols, :width] = part.T
            else:
                vt[j * 256 - D : (j + 1) * 256 - D, :width] = part.T

    def attend(c, w):
        width = w * ROWS
        mark(c, w)
        rows = pl.ds(pl.multiple_of(c * ROWS, ROWS), width)

        def four(q, carry):
            for e in range(4):
                h = 4 * q + e
                mine = pl.ds(pl.multiple_of(h * HD, HD), HD)
                here = pl.ds(pl.multiple_of((2 * q + e // 2) * 128, 128), 128)
                scores = dot(kv[rows, here], qzt[h]) + masked(width)
                old = m_ref[h]
                new = jnp.maximum(old, jnp.max(scores, 0, keepdims=True))
                raised = jnp.exp(scores - new)
                shrink = jnp.exp(old - new)
                l_ref[h] = l_ref[h] * shrink + jnp.sum(raised, 0, keepdims=True)
                m_ref[h] = new
                acc_o[mine, :] = acc_o[mine, :] * shrink + dot(vt[mine, :width], raised.astype(BF))
            return carry

        lax.fori_loop(0, HEADS // 4, four, 0)

    project(0, 1, 0)
    attend(0, 1)

    for i in FAR:
        x_copy(i).wait_recv()
        x_onward(i).start()

    for i in DIAGONAL:
        pack(i)

    def forward(step, carry):
        g = step + 1
        c = CAP * g - 1

        @pl.when(step == 2)
        def _():
            for i in FAR:
                x_onward(i).wait_send()
            for i in DIAGONAL:
                x_copy(i).start()

        @pl.when(step >= 1)
        def _():
            x_arrived(c - 1)

        x_arrived(c)
        project(c, 2, g)
        attend(c, 2)
        return carry

    lax.fori_loop(0, groups, forward, 0)

    def up_of():
        return cot_ref[...].astype(F32)

    def finish(h, carry):
        rows = pl.ds(pl.multiple_of(h * HD, HD), HD)
        total = l_ref[h]
        mixed = acc_o[rows, :] / total
        acc_o[rows, :] = mixed
        m_ref[h] = m_ref[h] + jnp.log(total)
        d_ref[h] = jnp.sum(mixed * dot_t[rows, :].astype(F32), 0, keepdims=True)
        return carry

    lax.fori_loop(0, HEADS, finish, 0)
    def middle():
        mid_ref[...] = (
            grid_ref[...].astype(F32) + dot(acc_o[...].T.astype(BF), wo_ref[...])
        ).astype(BF)
        edges(mid_ref[...], edge.at[1])
        for copy in h_copies(1):
            copy.start()
        centre = mid_ref[...].astype(F32)
        terms = tap_sum.bufs[0]
        terms[core] = jnp.zeros((8, D), F32)
        for row, side in enumerate((up_of(), *(sides[k].astype(F32) for k in (1, 0, 3, 2)))):
            terms[core, row : row + 1, :] = jnp.sum(centre * side, 0, keepdims=True)
        tap_sum.begin()
        attended = acc_o[...].astype(BF)
        early.load(lambda rows, cols: dot(attended[rows, :], gm_ref[:, cols]))
        early.begin()

    for i in range(1, n):
        x_copy(i).wait_send()

    def differentiate(c, w, g):
        width = w * ROWS
        mark(c, w)
        rows = pl.ds(pl.multiple_of(c * ROWS, ROWS), width)

        def four(q, carry):
            for e in range(4):
                h = 4 * q + e
                pair = (2 * q + e // 2) * 128
                mine = pl.ds(pl.multiple_of(h * HD, HD), HD)
                also = pl.ds(pl.multiple_of(D + h * HD, HD), HD)
                keys = kv[rows, pl.ds(pl.multiple_of(pair, 128), 128)]
                values = kv[rows, pl.ds(pl.multiple_of(D + pair, 128), 128)]
                weights = jnp.exp(dot(keys, qzt[h]) + masked(width) - m_ref[h])
                grads = (weights * (dot(values, dozt[h]) - d_ref[h])).astype(BF)
                dkvt[mine, :width] = dot_nt(qt[mine, :], grads).astype(BF)
                dkvt[also, :width] = dot_nt(dot_t[mine, :], weights.astype(BF)).astype(BF)
                acc_q[mine, :] += dot(kt[g, mine, :width], grads)
            return carry

        lax.fori_loop(0, HEADS // 4, four, 0)

        def weigh(j, carry):
            part = pl.ds(pl.multiple_of(j * 256, 256), 256)
            tokens = xs[pl.ds(c, w), 0:ROWS, :].reshape(width, D)
            dwt[part, :] += dot(dkvt[part, :width], tokens)
            return carry

        lax.fori_loop(0, 4, weigh, 0)

    def backward(step, carry):
        g = 6 - step + 6 * ((step + 4) // 8) - 4 * ((step + 2) // 8)
        differentiate(CAP * g - 1, 2, g)

        def turn(j, inner):
            cols = pl.ds(pl.multiple_of(j * 256, 256), 256)
            part = dot(wkv[cols, :], dkvt[...]).astype(BF).T
            send[pl.ds(CAP * g - 2, 2), 0:ROWS, cols] = part.reshape(2, ROWS, 256)
            return inner

        lax.fori_loop(0, 2, turn, 0)
        for k in range(groups):
            @pl.when(step == k)
            def _(k=k):
                first = CAP * BACK[k] - 2
                if first:
                    g_copy(first).start()
                else:
                    ret[0] = send[0, 0:ROWS, :]
                g_copy(first + 1).start()
                if k >= 4:
                    for i in (CAP * BACK[k - 4] - 2, CAP * BACK[k - 4] - 1):
                        if i in FAR:
                            g_copy(i).wait_recv()
                            g_onward(i).start()

        pl.when(step == 0)(middle)

        for stage in range(2):
            pl.when(step == 2 * stage + 2)(functools.partial(early.step, stage))
            pl.when(step == 2 * stage + 3)(functools.partial(tap_sum.step, stage))

        return carry

    lax.fori_loop(0, groups, backward, 0)
    differentiate(0, 1, 0)

    grad_q = (acc_q[...].T * SCALING).astype(BF)
    dwq = dot(grid_ref[...].T, grad_q)
    late[0].load(lambda rows, cols: dwq[rows, cols])
    late[1].load(lambda rows, cols: dwt[cols, rows].astype(BF).T)
    late[2].load(lambda rows, cols: dwt[D + cols.start : D + cols.stop, rows].astype(BF).T)
    for part in late:
        part.begin()
    tap_sum.step(2)

    def late_step(stage):
        if stage < 6:
            early.step(stage + 2)
        for part in late:
            part.step(stage)

    ggrid_ref[...] = (
        gm_ref[...].astype(F32) + dot_nt(grad_q, wq_ref[...])
        + dot(wkv[...], dkvt[:, :CELLS]).T
    ).astype(BF)
    stores[0].start()
    late_step(0)
    for copy in h_copies(1):
        copy.wait_recv()
    north, south, west, east = around(mid_ref[...], halo.at[1], lat == 0, lat == nlat - 1)
    enc_ref[...] = (
        (1.0 + sten_ref[0:1, :]) * mid_ref[...].astype(F32) + sten_ref[1:2, :] * north
        + sten_ref[2:3, :] * south + sten_ref[3:4, :] * west + sten_ref[4:5, :] * east
    ).astype(BF)
    stores[1].start()
    late_step(1)
    for i in range(1, n):
        if i not in FAR:
            g_copy(i).wait_recv()
        else:
            g_onward(i).wait_recv()
        g_copy(i).wait_send()
        if i in FAR:
            g_onward(i).wait_send()


    def unpack(b, carry):
        tile = dest_ref[0, b]
        rank = jnp.int32(0)
        for other in range(blocks):
            rank = rank + ((dest_ref[0, other] == tile) & (other < b)).astype(jnp.int32)
        dy = lax.rem(tile // SIDE - y + SIDE, SIDE)
        dz = lax.rem(lax.rem(tile, SIDE) - z + SIDE, SIDE)
        at = jnp.int32(0)
        for i, (sy, sz) in enumerate(STEPS):
            at = jnp.where((dy == sy) & (dz == sz), i, at)
        both = ret[at]
        gobs_ref[b] = jnp.where(rank == 0, both[:BLK], both[BLK:])
        return carry

    late_step(2)
    lax.fori_loop(0, blocks, unpack, 0)
    stores[2].start()
    late_step(3)
    tap_sum.step(3, taps_ref)
    for stage in range(4, 8):
        late_step(stage)
    for which in range(2):
        for copy in h_copies(which):
            copy.wait_send()
    for copy in stores:
        copy.wait()


def write_kernel(
    enc, gobs, ggrid, late, early, taps, enc_o, gobs_o, ggrid_o, wq, wk, wv, wo, taps_o,
    enc_v, gobs_v, ggrid_v, late_v, early_v, sums_v, in_sems, out_sems,
):
    part = gobs.shape[0] // 4
    loads, stores = [], []

    def load(source, target):
        loads.append(pltpu.make_async_copy(source, target, in_sems.at[len(loads)]))
        loads[-1].start()

    def store(source, out):
        stores.append(pltpu.make_async_copy(source, out, out_sems.at[len(stores)]))
        stores[-1].start()

    load(early, early_v)
    for k in range(3):
        load(late.at[k], late_v.at[k])
    for k in range(4):
        load(gobs.at[pl.ds(k * part, part)], gobs_v.at[pl.ds(k * part, part)])
    load(enc, enc_v)
    load(ggrid, ggrid_v)
    taps_o[...] = taps[0:5, :]
    for k, (out, source) in enumerate(
            ((wo, early_v), (wq, late_v.at[0]), (wk, late_v.at[1]), (wv, late_v.at[2]))):
        loads[k].wait()
        for f in range(8):
            rows, cols = slice((f % 2) * 256, (f % 2 + 1) * 256), slice((f // 2) * 128, (f // 2 + 1) * 128)
            sums_v[k, rows, cols] = source[f // 4, f % 4].reshape(256, 128).astype(F32)
        store(sums_v.at[k], out)
    for k in range(4):
        loads[4 + k].wait()
        store(gobs_v.at[pl.ds(k * part, part)], gobs_o.at[pl.ds(k * part, part)])
    loads[8].wait()
    store(enc_v, enc_o)
    loads[9].wait()
    store(ggrid_v, ggrid_o)
    for copy in stores:
        copy.wait()


def on_device(
    grid_tokens, obs_tokens, destinations, valid_counts, w_query, w_key, w_value, w_out,
    stencil_taps, cotangent,
):
    tile_shape = grid_tokens.shape
    blocks = obs_tokens.shape[0]
    nlat, n = lax.axis_size("lat"), lax.axis_size("lon")
    vmem = pl.BlockSpec(memory_space=pltpu.VMEM)
    smem = pl.BlockSpec(memory_space=pltpu.SMEM)
    anywhere = pl.BlockSpec(memory_space=pl.ANY)
    lon_sem = pltpu.SemaphoreType.DMA((n,))
    far_sem = pltpu.SemaphoreType.DMA((len(FAR),))
    halo_sem = pltpu.SemaphoreType.DMA((2, 4))
    ring_sem, core_sem = pltpu.SemaphoreType.DMA((SIDE,)), pltpu.SemaphoreType.DMA((2,))
    sems = [core_sem] * 2 + [ring_sem] * 6
    sums = []
    for _ in range(4):
        for lead in ((2, SIDE, SIDE, SIDE), (SIDE,) * 3, (SIDE,) * 2, (SIDE,)):
            sums += [pltpu.VMEM((*lead, 16, 128), BF)] * 2
        sums += sems * 2
    sums += [pltpu.VMEM((2, 8, D), F32)] + [pltpu.VMEM((SIDE, 8, D), F32)] * 3 + sems
    tile = jax.ShapeDtypeStruct((CELLS, D), BF)
    results = pl.pallas_call(
        functools.partial(kernel, nlat, n),
        out_shape=(
            tile, jax.ShapeDtypeStruct((blocks, BLK, D), BF), tile,
            jax.ShapeDtypeStruct((3, 2, SIDE, SIDE, SIDE, 16, 128), BF),
            jax.ShapeDtypeStruct((2, SIDE, SIDE, SIDE, 16, 128), BF),
            jax.ShapeDtypeStruct((8, D), F32),
        ),
        in_specs=[smem] * 2 + [vmem] * 3 + [anywhere] * 5,
        out_specs=(anywhere,) * 3 + (vmem,) * 3,
        scratch_shapes=[
            pltpu.VMEM((n, ROWS + EXTRA, D), BF),
            pltpu.VMEM((n + 1, ROWS + EXTRA, D), BF),
            pltpu.VMEM((n, ROWS, D), BF),
            pltpu.VMEM((len(FAR), ROWS + EXTRA, D), BF),
            pltpu.VMEM((len(FAR), ROWS, D), BF),
            pltpu.VMEM(((n + 1) * ROWS, 2 * D), BF),
            pltpu.VMEM((n // 2 + 1, D, 2 * ROWS), BF),
            pltpu.VMEM((D, 2 * ROWS), BF),
            pltpu.VMEM((2 * ROWS, 128), F32),
            pltpu.VMEM((D, 2 * D), BF),
            pltpu.VMEM((D, CELLS), BF),
            pltpu.VMEM((HEADS, 2 * HD, CELLS), BF),
            pltpu.VMEM((HEADS, 2 * HD, CELLS), BF),
            pltpu.VMEM((D, CELLS), BF),
            pltpu.VMEM((D, CELLS), F32),
            pltpu.VMEM((D, CELLS), F32),
            pltpu.VMEM((HEADS, 1, CELLS), F32),
            pltpu.VMEM((HEADS, 1, CELLS), F32),
            pltpu.VMEM((HEADS, 1, CELLS), F32),
            pltpu.VMEM((2 * D, 2 * ROWS), BF),
            pltpu.VMEM((2 * D, D), F32),
            pltpu.VMEM((CELLS, D), BF),
            pltpu.VMEM((CELLS, D), BF),
            pltpu.VMEM((4, CELLS, D), BF),
            pltpu.VMEM((2, 4, TILE, D), BF),
            pltpu.VMEM((2, 4, TILE, D), BF),
            pltpu.VMEM((blocks, BLK, D), BF),
            pltpu.VMEM((D, D), BF),
            pltpu.VMEM((D, D), BF),
            pltpu.VMEM((CELLS, D), BF),
            pltpu.VMEM((blocks, BLK, D), BF),
            pltpu.VMEM((CELLS, D), BF),
            pltpu.SemaphoreType.DMA((5,)),
            pltpu.SemaphoreType.DMA((3,)),
            lon_sem, lon_sem, far_sem, far_sem, lon_sem, lon_sem, far_sem, far_sem, halo_sem, halo_sem,
            *sums,
        ],
        compiler_params=pltpu.CompilerParams(
            collective_id=0, has_side_effects=True, vmem_limit_bytes=62 * 2**20
        ),
        name="encoder_step",
    )(
        destinations.reshape(1, blocks), valid_counts, grid_tokens.reshape(CELLS, D),
        cotangent.reshape(CELLS, D), stencil_taps, obs_tokens, w_query, w_key, w_value, w_out,
    )
    matrix = jax.ShapeDtypeStruct((D, D), F32)
    encoded, grad_obs, grad_grid, *sums = pl.pallas_call(
        write_kernel,
        out_shape=(
            tile, jax.ShapeDtypeStruct((blocks, BLK, D), BF), tile, matrix, matrix, matrix, matrix,
            jax.ShapeDtypeStruct((5, D), F32),
        ),
        in_specs=[anywhere] * 5 + [vmem],
        out_specs=(anywhere,) * 7 + (vmem,),
        scratch_shapes=[
            pltpu.VMEM((CELLS, D), BF), pltpu.VMEM((blocks, BLK, D), BF), pltpu.VMEM((CELLS, D), BF),
            pltpu.VMEM((3, 2, SIDE, SIDE, SIDE, 16, 128), BF), pltpu.VMEM((2, SIDE, SIDE, SIDE, 16, 128), BF),
            pltpu.VMEM((4, D, D), F32), pltpu.SemaphoreType.DMA((10,)), pltpu.SemaphoreType.DMA((10,)),
        ],
        compiler_params=pltpu.CompilerParams(vmem_limit_bytes=62 * 2**20),
        name="write_results",
    )(*results)
    return (encoded.reshape(tile_shape), grad_grid.reshape(tile_shape), grad_obs, *sums)


def solution(mesh):
    in_specs = (
        P("lat", "lon", None),
        P(("lat", "lon"), None, None),
        P(("lat", "lon"), None),
        P(("lat", "lon"), None),
        P(),
        P(),
        P(),
        P(),
        P(),
        P("lat", "lon", None),
    )
    out_specs = (
        P("lat", "lon", None),
        P("lat", "lon", None),
        P(("lat", "lon"), None, None),
        P(),
        P(),
        P(),
        P(),
        P(),
    )
    return jax.shard_map(
        on_device, mesh=mesh, in_specs=in_specs, out_specs=out_specs, check_vma=False
    )
```

```python
import functools

import jax
import jax.numpy as jnp
from jax import lax
from jax.experimental import pallas as pl
from jax.experimental.pallas import tpu as pltpu
from jax.sharding import PartitionSpec as P

D = 512
HEADS = 8
HD = D // HEADS
BLK = 128
CAP = 2
ROWS = CAP * BLK
CELLS = 256
TILE = 16
SCALING = HD ** (-0.5)
MESH = pl.DeviceIdType.MESH
SIDE = 4
STEPS = (
    (0, 0), (0, 1), (0, 3), (1, 0), (3, 0),
    (0, 2), (2, 0), (1, 2), (3, 2), (2, 1), (2, 3), (2, 2),
    (1, 1), (1, 3), (3, 1), (3, 3),
)
FAR = range(5, 12)
DIAGONAL = range(12, 16)
BACK = (6, 5, 4, 3, 8, 7, 2, 1)
EXTRA = 16
BF = jnp.bfloat16
F32 = jnp.float32


def dot(a, b):
    return jnp.dot(a, b, preferred_element_type=F32)


def dot_nt(a, b):
    return lax.dot_general(a, b, (((1,), (1,)), ((), ())), preferred_element_type=F32)


def onehot(rows, cols, hit):
    at = [lax.broadcasted_iota(jnp.int32, (rows, cols), k) for k in range(2)]
    return jnp.where(hit(*at), 1.0, 0.0).astype(BF)


def around(cells, halo, first, last):
    top = jnp.where(first, 0.0, halo[0].astype(F32)).astype(BF)
    bottom = jnp.where(last, 0.0, halo[1].astype(F32)).astype(BF)
    side = TILE
    west = dot(onehot(CELLS, CELLS, lambda q, k: (k == q - 1) & (lax.rem(q, side) != 0)), cells)
    west = west + dot(onehot(CELLS, side, lambda q, k: q == k * side), halo[2])
    east = dot(onehot(CELLS, CELLS, lambda q, k: (k == q + 1) & (lax.rem(q, side) != side - 1)), cells)
    east = east + dot(onehot(CELLS, side, lambda q, k: q == k * side + side - 1), halo[3])
    return (
        jnp.concatenate([top, cells[:-side]], 0).astype(F32),
        jnp.concatenate([cells[side:], bottom], 0).astype(F32),
        west,
        east,
    )


def edges(cells, out):
    out[0] = cells[CELLS - TILE :]
    out[1] = cells[:TILE]
    out[2] = dot(onehot(TILE, CELLS, lambda k, q: q == k * TILE + TILE - 1), cells).astype(BF)
    out[3] = dot(onehot(TILE, CELLS, lambda k, q: q == k * TILE), cells).astype(BF)


class Exchange:
    def __init__(self, count, me, whom, copy):
        self.count, self.me, self.whom, self.copy = count, me, whom, copy

    def each(self, body):
        def step(o, carry):
            body(lax.rem(self.me + o, self.count))
            return carry

        if self.count == 2:
            body(1 - self.me)
        else:
            lax.fori_loop(1, self.count, step, 0)

    def start(self):
        self.each(lambda at: self.copy(at, self.me).start())

    def wait(self):
        self.each(lambda at: self.copy(at, at).wait_recv())

    def sent(self):
        self.each(lambda at: self.copy(at, self.me).wait_send())


def scatter(group, src, dst, ssem, rsem):
    count, me, whom = group
    return Exchange(count, me, whom, lambda to, frm: pltpu.make_async_remote_copy(
        src_ref=src.at[to], dst_ref=dst.at[frm], send_sem=ssem.at[to], recv_sem=rsem.at[frm],
        device_id=whom(to), device_id_type=MESH))


def gather(group, buf, ssem, rsem):
    count, me, whom = group
    return Exchange(count, me, whom, lambda to, frm: pltpu.make_async_remote_copy(
        src_ref=buf.at[me], dst_ref=buf.at[frm], send_sem=ssem.at[to], recv_sem=rsem.at[frm],
        device_id=whom(to), device_id_type=MESH))


class MatrixSum:
    def __init__(self, groups, buffers, sems, out):
        self.me = [group[1] for group in groups]
        self.bufs = buffers
        self.out = out
        at, self.stages = out, []
        for k, group in enumerate(groups):
            self.stages.append(scatter(group, buffers[2 * k], buffers[2 * k + 1], *sems[2 * k : 2 * k + 2]))
        for k, group in enumerate(groups):
            self.stages.insert(4, gather(group, at, *sems[8 + 2 * k : 10 + 2 * k]))
            at = at.at[group[1]]
        self.place = at

    def load(self, source):
        per = D // 256
        for c in range(2):
            for x in range(4):
                f = 4 * c + x
                rows = slice((f % per) * 256, (f % per + 1) * 256)
                cols = slice((f // per) * 128, (f // per + 1) * 128)
                self.bufs[0][c, x] = source(rows, cols).astype(BF).reshape(4, 4, 16, 128)

    def begin(self):
        self.stages[0].start()

    def step(self, stage):
        self.stages[stage].wait()
        if stage < 4:
            me, count = self.me[stage], self.stages[stage].count
            own, got = self.bufs[2 * stage], self.bufs[2 * stage + 1]
            held = own[me].astype(F32)
            for o in range(1, count):
                held = held + got[lax.rem(me + o, count)].astype(F32)
            target = self.place if stage == 3 else self.bufs[2 * stage + 2]
            target[...] = held.astype(BF)
        if stage < 7:
            self.stages[stage + 1].start()
        self.stages[stage].sent()


class TapSum:
    def __init__(self, groups, buffers, sems):
        self.bufs = buffers
        self.stages = [
            gather(group, buffers[k], *sems[2 * k : 2 * k + 2]) for k, group in enumerate(groups)
        ]

    def begin(self):
        self.stages[0].start()

    def step(self, stage, out=None):
        self.stages[stage].wait()
        total = self.bufs[stage][0]
        for k in range(1, self.stages[stage].count):
            total = total + self.bufs[stage][k]
        if stage == 3:
            out[...] = total
        else:
            self.bufs[stage + 1][self.stages[stage + 1].me] = total
            self.stages[stage + 1].start()
        self.stages[stage].sent()


def kernel(
    nlat, n, dest_ref, count_ref, grid_ref, cot_ref, sten_ref, obs_in, wq_in, wk_in, wv_in, wo_in,
    enc_out, gobs_out, ggrid_out, late_ref, early_ref, taps_ref,
    send, xs, ret, relay, relay_back, kv, kt, vt, bias, wkv, qt, qzt, dozt, dot_t,
    acc_o, acc_q, m_ref, l_ref, d_ref, dkvt, dwt, gm_ref, mid_ref, sides, edge, halo,
    obs_ref, wq_ref, wo_ref, enc_ref, gobs_ref, ggrid_ref, in_sem, out_sem,
    x_ssem, x_rsem, r_ssem, r_rsem, g_ssem, g_rsem, b_ssem, b_rsem, h_ssem, h_rsem,
    *sum_scratch,
):
    lat, me = lax.axis_index("lat"), lax.axis_index("lon")
    groups = n // 2
    blocks = obs_ref.shape[0]
    loads = [
        pltpu.make_async_copy(source, target, in_sem.at[k])
        for k, (source, target) in enumerate((
            (obs_in, obs_ref), (wq_in, wq_ref), (wk_in, wkv.at[:, pl.ds(0, D)]),
            (wv_in, wkv.at[:, pl.ds(D, D)]), (wo_in, wo_ref)))
    ]
    stores = [
        pltpu.make_async_copy(source, target, out_sem.at[k])
        for k, (source, target) in enumerate((
            (ggrid_ref, ggrid_out), (enc_ref, enc_out), (gobs_ref, gobs_out)))
    ]
    x_at, core = lat // 2, lax.rem(lat, 2)
    y, z = me // SIDE, lax.rem(me, SIDE)
    on_core = (2, core, lambda at: {"lat": 2 * x_at + at})
    on_x = (SIDE, x_at, lambda at: {"lat": 2 * at + core})
    on_y = (SIDE, y, lambda at: {"lon": at * SIDE + z})
    on_z = (SIDE, z, lambda at: {"lon": y * SIDE + at})
    orders = ((on_x, on_y, on_z), (on_y, on_z, on_x), (on_z, on_x, on_y), (on_x, on_y, on_z))
    *late, early = (
        MatrixSum(
            (on_core, *order), sum_scratch[24 * k : 24 * k + 8], sum_scratch[24 * k + 8 : 24 * k + 24],
            late_ref.at[k] if k < 3 else early_ref)
        for k, order in enumerate(orders)
    )
    tap_sum = TapSum((on_core, on_x, on_y, on_z), sum_scratch[96:100], sum_scratch[100:108])

    way_y, way_z = 1 - 2 * lax.rem(y, 2), 1 - 2 * lax.rem(z, 2)

    def place(dy, dz):
        return lax.rem(y + dy + 2 * SIDE, SIDE) * SIDE + lax.rem(z + dz + 2 * SIDE, SIDE)

    def turned(i):
        return 1 if STEPS[i] in ((0, 2), (2, 0), (2, 2)) else -1

    def leg(i, sign):
        dy, dz = STEPS[i]
        return {"lon": place(
            turned(i) * way_y if dy == 2 else sign * dy, turned(i) * way_z if dz == 2 else sign * dz)}

    def onward(i):
        dy, dz = STEPS[i]
        return {"lon": place(
            -turned(i) * way_y if dy == 2 else 0, -turned(i) * way_z if dz == 2 else 0)}

    for load in loads:
        load.start()
    barrier = pltpu.get_barrier_semaphore()
    def greet(o, carry, axis, count, at):
        pl.semaphore_signal(
            barrier, inc=1, device_id={axis: lax.rem(at + o, count)}, device_id_type=MESH)
        return carry

    lax.fori_loop(1, nlat, functools.partial(greet, axis="lat", count=nlat, at=lat), 0)
    lax.fori_loop(1, n, functools.partial(greet, axis="lon", count=n, at=me), 0)

    row_ids = lax.broadcasted_iota(jnp.int32, (EXTRA, D), 0)

    def pack(i):
        tile = place(*STEPS[i])
        number = b0 = b1 = c0 = c1 = jnp.int32(0)
        for b in range(blocks):
            hit = dest_ref[0, b] == tile
            one, two = hit & (number == 0), hit & (number == 1)
            number = number + hit.astype(jnp.int32)
            b0, b1 = jnp.where(one, b, b0), jnp.where(two, b, b1)
            c0, c1 = jnp.where(one, count_ref[0, b], c0), jnp.where(two, count_ref[0, b], c1)
        send[i, 0:BLK, :] = obs_ref[b0]
        send[i, BLK:ROWS, :] = obs_ref[b1]
        send[i, ROWS:, :] = jnp.where(row_ids == 0, c0, c1).astype(F32).astype(BF)

    edges(cot_ref[...], edge.at[0])
    loads[0].wait()
    pl.semaphore_wait(barrier, nlat + n - 2)

    def remote(src, dst, ssem, rsem, whom):
        return pltpu.make_async_remote_copy(
            src_ref=src, dst_ref=dst, send_sem=ssem, recv_sem=rsem, device_id=whom, device_id_type=MESH)

    def x_copy(i):
        if i not in FAR:
            return remote(send.at[i], xs.at[i + 1], x_ssem.at[i], x_rsem.at[i], leg(i, 1))
        j = i - FAR.start
        return remote(send.at[i], relay.at[j], x_ssem.at[i], r_rsem.at[j], leg(i, 1))

    def x_onward(i):
        j = i - FAR.start
        return remote(relay.at[j], xs.at[i + 1], r_ssem.at[j], x_rsem.at[i], onward(i))

    def g_copy(i):
        tokens = send.at[i, pl.ds(0, ROWS)]
        if i not in FAR:
            return remote(tokens, ret.at[i], g_ssem.at[i], g_rsem.at[i], leg(i, -1))
        j = i - FAR.start
        return remote(tokens, relay_back.at[j], g_ssem.at[i], b_rsem.at[j], leg(i, -1))

    def g_onward(i):
        j = i - FAR.start
        return remote(relay_back.at[j], ret.at[i], b_ssem.at[j], g_rsem.at[i], onward(i))

    def x_arrived(i):
        remote(send.at[0], xs.at[i + 1], x_ssem.at[0], x_rsem.at[i], {"lon": me}).wait_recv()

    def h_copies(which):
        whom = (
            {"lat": lax.rem(lat + 1, nlat)}, {"lat": lax.rem(lat + nlat - 1, nlat)},
            {"lon": lax.rem(me + 1, n)}, {"lon": lax.rem(me + n - 1, n)},
        )
        return [
            remote(edge.at[which, k], halo.at[which, k], h_ssem.at[which, k], h_rsem.at[which, k], whom[k])
            for k in range(4)
        ]

    for copy in h_copies(0):
        copy.start()

    for i in (*FAR, *range(1, FAR.start)):
        pack(i)
        x_copy(i).start()
    pack(0)

    xs[0, 0:ROWS, :] = grid_ref[...]
    xs[1] = send[0]
    for load in loads[1:]:
        load.wait()
    lanes = lax.broadcasted_iota(jnp.int32, (CELLS, 2 * HD), 1)
    queries = dot(grid_ref[...], wq_ref[...]).astype(BF).astype(F32) * SCALING
    for copy in h_copies(0):
        copy.wait_recv()
    up = cot_ref[...].astype(F32)
    around_up = around(cot_ref[...], halo.at[0], lat == 0, lat == nlat - 1)
    for k in range(4):
        sides[k] = around_up[k].astype(BF)
    up_north, up_south, up_west, up_east = around_up
    gm_ref[...] = (
        (1.0 + sten_ref[0:1, :]) * up + sten_ref[1:2, :] * up_south + sten_ref[2:3, :] * up_north
        + sten_ref[3:4, :] * up_east + sten_ref[4:5, :] * up_west
    ).astype(BF)
    ups = dot_nt(gm_ref[...], wo_ref[...]).astype(BF).astype(F32)
    dot_t[...] = ups.T.astype(BF)
    qt[...] = queries.T.astype(BF)
    for h in range(HEADS):
        p, e = h // 2, h % 2
        mine = (lanes >= HD) if e else (lanes < HD)
        picked = jnp.where(mine, queries[:, p * 2 * HD : (p + 1) * 2 * HD], 0.0)
        qzt[h] = picked.T.astype(BF)
        picked = jnp.where(mine, ups[:, p * 2 * HD : (p + 1) * 2 * HD], 0.0)
        dozt[h] = picked.T.astype(BF)
    acc_o[...] = jnp.zeros_like(acc_o)
    acc_q[...] = jnp.zeros_like(acc_q)
    dwt[...] = jnp.zeros_like(dwt)
    m_ref[...] = jnp.full(m_ref.shape, -1e30, F32)
    l_ref[...] = jnp.zeros_like(l_ref)
    key_ids = lax.broadcasted_iota(jnp.int32, (BLK, 128), 0).astype(F32)

    def masked(width):
        part = bias[0:width, :]
        return jnp.concatenate([part, part], 1)

    def mark(c, w):
        if w == 1:
            bias[0:ROWS, :] = jnp.zeros((ROWS, 128), F32)
            return
        for k in range(w):
            tile = xs[c + k, ROWS:, 0:128].astype(F32)
            for r in range(CAP):
                at = k * ROWS + r * BLK
                bias[at : at + BLK, :] = jnp.where(key_ids < tile[r : r + 1, :], 0.0, -1e30)

    def project(c, w, g):
        width = w * ROWS
        rows = pl.ds(pl.multiple_of(c * ROWS, ROWS), width)
        tokens = xs[pl.ds(c, w), 0:ROWS, :].reshape(width, D)
        for j in range(4):
            cols = slice(j * 256, (j + 1) * 256)
            part = dot(tokens, wkv[:, cols]).astype(BF)
            kv[rows, cols] = part
            if j < 2:
                kt[g, cols, :width] = part.T
            else:
                vt[j * 256 - D : (j + 1) * 256 - D, :width] = part.T

    def attend(c, w):
        width = w * ROWS
        mark(c, w)
        rows = pl.ds(pl.multiple_of(c * ROWS, ROWS), width)

        def four(q, carry):
            for e in range(4):
                h = 4 * q + e
                mine = pl.ds(pl.multiple_of(h * HD, HD), HD)
                here = pl.ds(pl.multiple_of((2 * q + e // 2) * 128, 128), 128)
                scores = dot(kv[rows, here], qzt[h]) + masked(width)
                old = m_ref[h]
                new = jnp.maximum(old, jnp.max(scores, 0, keepdims=True))
                raised = jnp.exp(scores - new)
                shrink = jnp.exp(old - new)
                l_ref[h] = l_ref[h] * shrink + jnp.sum(raised, 0, keepdims=True)
                m_ref[h] = new
                acc_o[mine, :] = acc_o[mine, :] * shrink + dot(vt[mine, :width], raised.astype(BF))
            return carry

        lax.fori_loop(0, HEADS // 4, four, 0)

    project(0, 1, 0)
    attend(0, 1)

    for i in FAR:
        x_copy(i).wait_recv()
        x_onward(i).start()

    for i in DIAGONAL:
        pack(i)

    def forward(step, carry):
        g = step + 1
        c = CAP * g - 1

        @pl.when(step == 2)
        def _():
            for i in FAR:
                x_onward(i).wait_send()
            for i in DIAGONAL:
                x_copy(i).start()

        @pl.when(step >= 1)
        def _():
            x_arrived(c - 1)

        x_arrived(c)
        project(c, 2, g)
        attend(c, 2)
        return carry

    lax.fori_loop(0, groups, forward, 0)

    def up_of():
        return cot_ref[...].astype(F32)

    def finish(h, carry):
        rows = pl.ds(pl.multiple_of(h * HD, HD), HD)
        total = l_ref[h]
        mixed = acc_o[rows, :] / total
        acc_o[rows, :] = mixed
        m_ref[h] = m_ref[h] + jnp.log(total)
        d_ref[h] = jnp.sum(mixed * dot_t[rows, :].astype(F32), 0, keepdims=True)
        return carry

    lax.fori_loop(0, HEADS, finish, 0)
    def middle():
        mid_ref[...] = (
            grid_ref[...].astype(F32) + dot(acc_o[...].T.astype(BF), wo_ref[...])
        ).astype(BF)
        edges(mid_ref[...], edge.at[1])
        for copy in h_copies(1):
            copy.start()
        centre = mid_ref[...].astype(F32)
        terms = tap_sum.bufs[0]
        terms[core] = jnp.zeros((8, D), F32)
        for row, side in enumerate((up_of(), *(sides[k].astype(F32) for k in (1, 0, 3, 2)))):
            terms[core, row : row + 1, :] = jnp.sum(centre * side, 0, keepdims=True)
        tap_sum.begin()
        attended = acc_o[...].astype(BF)
        early.load(lambda rows, cols: dot(attended[rows, :], gm_ref[:, cols]))
        early.begin()

    for i in range(1, n):
        x_copy(i).wait_send()

    def differentiate(c, w, g):
        width = w * ROWS
        mark(c, w)
        rows = pl.ds(pl.multiple_of(c * ROWS, ROWS), width)

        def four(q, carry):
            for e in range(4):
                h = 4 * q + e
                pair = (2 * q + e // 2) * 128
                mine = pl.ds(pl.multiple_of(h * HD, HD), HD)
                also = pl.ds(pl.multiple_of(D + h * HD, HD), HD)
                keys = kv[rows, pl.ds(pl.multiple_of(pair, 128), 128)]
                values = kv[rows, pl.ds(pl.multiple_of(D + pair, 128), 128)]
                weights = jnp.exp(dot(keys, qzt[h]) + masked(width) - m_ref[h])
                grads = (weights * (dot(values, dozt[h]) - d_ref[h])).astype(BF)
                dkvt[mine, :width] = dot_nt(qt[mine, :], grads).astype(BF)
                dkvt[also, :width] = dot_nt(dot_t[mine, :], weights.astype(BF)).astype(BF)
                acc_q[mine, :] += dot(kt[g, mine, :width], grads)
            return carry

        lax.fori_loop(0, HEADS // 4, four, 0)

    def accumulate(c, w):
        width = w * ROWS

        def weigh(j, carry):
            part = pl.ds(pl.multiple_of(j * 256, 256), 256)
            tokens = xs[pl.ds(c, w), 0:ROWS, :].reshape(width, D)
            dwt[part, :] += dot(dkvt[part, :width], tokens)
            return carry

        lax.fori_loop(0, 4, weigh, 0)

    def backward(step, carry):
        g = 6 - step + 6 * ((step + 4) // 8) - 4 * ((step + 2) // 8)
        differentiate(CAP * g - 1, 2, g)

        def turn(j, inner):
            cols = pl.ds(pl.multiple_of(j * 256, 256), 256)
            part = dot(wkv[cols, :], dkvt[...]).astype(BF).T
            send[pl.ds(CAP * g - 2, 2), 0:ROWS, cols] = part.reshape(2, ROWS, 256)
            return inner

        lax.fori_loop(0, 2, turn, 0)
        for k in range(groups):
            @pl.when(step == k)
            def _(k=k):
                first = CAP * BACK[k] - 2
                if first:
                    g_copy(first).start()
                else:
                    ret[0] = send[0, 0:ROWS, :]
                g_copy(first + 1).start()
                if k >= 4:
                    for i in (CAP * BACK[k - 4] - 2, CAP * BACK[k - 4] - 1):
                        if i in FAR:
                            g_copy(i).wait_recv()
                            g_onward(i).start()

        accumulate(CAP * g - 1, 2)
        pl.when(step == 0)(middle)

        for stage in range(2):
            pl.when(step == 2 * stage + 2)(functools.partial(early.step, stage))
            pl.when(step == 2 * stage + 3)(functools.partial(tap_sum.step, stage))

        return carry

    lax.fori_loop(0, groups, backward, 0)
    differentiate(0, 1, 0)
    accumulate(0, 1)

    late[1].load(lambda rows, cols: dwt[cols, rows].astype(BF).T)
    late[1].begin()
    late[2].load(lambda rows, cols: dwt[D + cols.start : D + cols.stop, rows].astype(BF).T)
    late[2].begin()
    grad_q = (acc_q[...].T * SCALING).astype(BF)
    dwq = dot(grid_ref[...].T, grad_q)
    late[0].load(lambda rows, cols: dwq[rows, cols])
    late[0].begin()
    tap_sum.step(2)

    def late_step(stage):
        if stage < 6:
            early.step(stage + 2)
        for part in (late[1], late[2], late[0]):
            part.step(stage)

    ggrid_ref[...] = (
        gm_ref[...].astype(F32) + dot_nt(grad_q, wq_ref[...])
        + dot(wkv[...], dkvt[:, :CELLS]).T
    ).astype(BF)
    stores[0].start()
    late_step(0)
    for copy in h_copies(1):
        copy.wait_recv()
    north, south, west, east = around(mid_ref[...], halo.at[1], lat == 0, lat == nlat - 1)
    enc_ref[...] = (
        (1.0 + sten_ref[0:1, :]) * mid_ref[...].astype(F32) + sten_ref[1:2, :] * north
        + sten_ref[2:3, :] * south + sten_ref[3:4, :] * west + sten_ref[4:5, :] * east
    ).astype(BF)
    stores[1].start()
    late_step(1)
    late_step(2)
    late_step(3)
    tap_sum.step(3, taps_ref)
    late_step(4)
    late_step(5)
    for i in range(1, n):
        if i not in FAR:
            g_copy(i).wait_recv()
        else:
            g_onward(i).wait_recv()
        g_copy(i).wait_send()
        if i in FAR:
            g_onward(i).wait_send()


    def unpack(b, carry):
        tile = dest_ref[0, b]
        rank = jnp.int32(0)
        for other in range(blocks):
            rank = rank + ((dest_ref[0, other] == tile) & (other < b)).astype(jnp.int32)
        dy = lax.rem(tile // SIDE - y + SIDE, SIDE)
        dz = lax.rem(lax.rem(tile, SIDE) - z + SIDE, SIDE)
        at = jnp.int32(0)
        for i, (sy, sz) in enumerate(STEPS):
            at = jnp.where((dy == sy) & (dz == sz), i, at)
        both = ret[at]
        gobs_ref[b] = jnp.where(rank == 0, both[:BLK], both[BLK:])
        return carry

    lax.fori_loop(0, blocks, unpack, 0)
    stores[2].start()
    late_step(6)
    late_step(7)
    for which in range(2):
        for copy in h_copies(which):
            copy.wait_send()
    for copy in stores:
        copy.wait()


def write_kernel(
    enc, gobs, ggrid, late, early, taps, enc_o, gobs_o, ggrid_o, wq, wk, wv, wo, taps_o,
    enc_v, gobs_v, ggrid_v, late_v, early_v, sums_v, in_sems, out_sems,
):
    part = gobs.shape[0] // 4
    loads, stores = [], []

    def load(source, target):
        loads.append(pltpu.make_async_copy(source, target, in_sems.at[len(loads)]))
        loads[-1].start()

    def store(source, out):
        stores.append(pltpu.make_async_copy(source, out, out_sems.at[len(stores)]))
        stores[-1].start()

    load(early, early_v)
    for k in range(3):
        load(late.at[k], late_v.at[k])
    for k in range(4):
        load(gobs.at[pl.ds(k * part, part)], gobs_v.at[pl.ds(k * part, part)])
    load(enc, enc_v)
    load(ggrid, ggrid_v)
    taps_o[...] = taps[0:5, :]
    for k, (out, source) in enumerate(
            ((wo, early_v), (wq, late_v.at[0]), (wk, late_v.at[1]), (wv, late_v.at[2]))):
        loads[k].wait()
        for f in range(8):
            rows, cols = slice((f % 2) * 256, (f % 2 + 1) * 256), slice((f // 2) * 128, (f // 2 + 1) * 128)
            sums_v[k, rows, cols] = source[f // 4, f % 4].reshape(256, 128).astype(F32)
        store(sums_v.at[k], out)
    for k in range(4):
        loads[4 + k].wait()
        store(gobs_v.at[pl.ds(k * part, part)], gobs_o.at[pl.ds(k * part, part)])
    loads[8].wait()
    store(enc_v, enc_o)
    loads[9].wait()
    store(ggrid_v, ggrid_o)
    for copy in stores:
        copy.wait()


def on_device(
    grid_tokens, obs_tokens, destinations, valid_counts, w_query, w_key, w_value, w_out,
    stencil_taps, cotangent,
):
    tile_shape = grid_tokens.shape
    blocks = obs_tokens.shape[0]
    nlat, n = lax.axis_size("lat"), lax.axis_size("lon")
    vmem = pl.BlockSpec(memory_space=pltpu.VMEM)
    smem = pl.BlockSpec(memory_space=pltpu.SMEM)
    anywhere = pl.BlockSpec(memory_space=pl.ANY)
    lon_sem = pltpu.SemaphoreType.DMA((n,))
    far_sem = pltpu.SemaphoreType.DMA((len(FAR),))
    halo_sem = pltpu.SemaphoreType.DMA((2, 4))
    ring_sem, core_sem = pltpu.SemaphoreType.DMA((SIDE,)), pltpu.SemaphoreType.DMA((2,))
    sems = [core_sem] * 2 + [ring_sem] * 6
    sums = []
    for _ in range(4):
        for lead in ((2, SIDE, SIDE, SIDE), (SIDE,) * 3, (SIDE,) * 2, (SIDE,)):
            sums += [pltpu.VMEM((*lead, 16, 128), BF)] * 2
        sums += sems * 2
    sums += [pltpu.VMEM((2, 8, D), F32)] + [pltpu.VMEM((SIDE, 8, D), F32)] * 3 + sems
    tile = jax.ShapeDtypeStruct((CELLS, D), BF)
    results = pl.pallas_call(
        functools.partial(kernel, nlat, n),
        out_shape=(
            tile, jax.ShapeDtypeStruct((blocks, BLK, D), BF), tile,
            jax.ShapeDtypeStruct((3, 2, SIDE, SIDE, SIDE, 16, 128), BF),
            jax.ShapeDtypeStruct((2, SIDE, SIDE, SIDE, 16, 128), BF),
            jax.ShapeDtypeStruct((8, D), F32),
        ),
        in_specs=[smem] * 2 + [vmem] * 3 + [anywhere] * 5,
        out_specs=(anywhere,) * 3 + (vmem,) * 3,
        scratch_shapes=[
            pltpu.VMEM((n, ROWS + EXTRA, D), BF),
            pltpu.VMEM((n + 1, ROWS + EXTRA, D), BF),
            pltpu.VMEM((n, ROWS, D), BF),
            pltpu.VMEM((len(FAR), ROWS + EXTRA, D), BF),
            pltpu.VMEM((len(FAR), ROWS, D), BF),
            pltpu.VMEM(((n + 1) * ROWS, 2 * D), BF),
            pltpu.VMEM((n // 2 + 1, D, 2 * ROWS), BF),
            pltpu.VMEM((D, 2 * ROWS), BF),
            pltpu.VMEM((2 * ROWS, 128), F32),
            pltpu.VMEM((D, 2 * D), BF),
            pltpu.VMEM((D, CELLS), BF),
            pltpu.VMEM((HEADS, 2 * HD, CELLS), BF),
            pltpu.VMEM((HEADS, 2 * HD, CELLS), BF),
            pltpu.VMEM((D, CELLS), BF),
            pltpu.VMEM((D, CELLS), F32),
            pltpu.VMEM((D, CELLS), F32),
            pltpu.VMEM((HEADS, 1, CELLS), F32),
            pltpu.VMEM((HEADS, 1, CELLS), F32),
            pltpu.VMEM((HEADS, 1, CELLS), F32),
            pltpu.VMEM((2 * D, 2 * ROWS), BF),
            pltpu.VMEM((2 * D, D), F32),
            pltpu.VMEM((CELLS, D), BF),
            pltpu.VMEM((CELLS, D), BF),
            pltpu.VMEM((4, CELLS, D), BF),
            pltpu.VMEM((2, 4, TILE, D), BF),
            pltpu.VMEM((2, 4, TILE, D), BF),
            pltpu.VMEM((blocks, BLK, D), BF),
            pltpu.VMEM((D, D), BF),
            pltpu.VMEM((D, D), BF),
            pltpu.VMEM((CELLS, D), BF),
            pltpu.VMEM((blocks, BLK, D), BF),
            pltpu.VMEM((CELLS, D), BF),
            pltpu.SemaphoreType.DMA((5,)),
            pltpu.SemaphoreType.DMA((3,)),
            lon_sem, lon_sem, far_sem, far_sem, lon_sem, lon_sem, far_sem, far_sem, halo_sem, halo_sem,
            *sums,
        ],
        compiler_params=pltpu.CompilerParams(
            collective_id=0, has_side_effects=True, vmem_limit_bytes=62 * 2**20
        ),
        name="encoder_step",
    )(
        destinations.reshape(1, blocks), valid_counts, grid_tokens.reshape(CELLS, D),
        cotangent.reshape(CELLS, D), stencil_taps, obs_tokens, w_query, w_key, w_value, w_out,
    )
    matrix = jax.ShapeDtypeStruct((D, D), F32)
    encoded, grad_obs, grad_grid, *sums = pl.pallas_call(
        write_kernel,
        out_shape=(
            tile, jax.ShapeDtypeStruct((blocks, BLK, D), BF), tile, matrix, matrix, matrix, matrix,
            jax.ShapeDtypeStruct((5, D), F32),
        ),
        in_specs=[anywhere] * 5 + [vmem],
        out_specs=(anywhere,) * 7 + (vmem,),
        scratch_shapes=[
            pltpu.VMEM((CELLS, D), BF), pltpu.VMEM((blocks, BLK, D), BF), pltpu.VMEM((CELLS, D), BF),
            pltpu.VMEM((3, 2, SIDE, SIDE, SIDE, 16, 128), BF), pltpu.VMEM((2, SIDE, SIDE, SIDE, 16, 128), BF),
            pltpu.VMEM((4, D, D), F32), pltpu.SemaphoreType.DMA((10,)), pltpu.SemaphoreType.DMA((10,)),
        ],
        compiler_params=pltpu.CompilerParams(vmem_limit_bytes=62 * 2**20),
        name="write_results",
    )(*results)
    return (encoded.reshape(tile_shape), grad_grid.reshape(tile_shape), grad_obs, *sums)


def solution(mesh):
    in_specs = (
        P("lat", "lon", None),
        P(("lat", "lon"), None, None),
        P(("lat", "lon"), None),
        P(("lat", "lon"), None),
        P(),
        P(),
        P(),
        P(),
        P(),
        P("lat", "lon", None),
    )
    out_specs = (
        P("lat", "lon", None),
        P("lat", "lon", None),
        P(("lat", "lon"), None, None),
        P(),
        P(),
        P(),
        P(),
        P(),
    )
    return jax.shard_map(
        on_device, mesh=mesh, in_specs=in_specs, out_specs=out_specs, check_vma=False
    )
```

```python
import functools

import jax
import jax.numpy as jnp
from jax import lax
from jax.experimental import pallas as pl
from jax.experimental.pallas import tpu as pltpu
from jax.sharding import PartitionSpec as P

D = 512
HEADS = 8
HD = D // HEADS
BLK = 128
CAP = 2
ROWS = CAP * BLK
CELLS = 256
TILE = 16
SCALING = HD ** (-0.5)
MESH = pl.DeviceIdType.MESH
SIDE = 4
STEPS = (
    (0, 0), (0, 1), (0, 3), (1, 0), (3, 0),
    (0, 2), (2, 0), (1, 2), (3, 2), (2, 1), (2, 3), (2, 2),
    (1, 1), (1, 3), (3, 1), (3, 3),
)
FAR = range(5, 12)
DIAGONAL = range(12, 16)
BACK = (6, 5, 4, 3, 8, 7, 2, 1)
EXTRA = 16
BF = jnp.bfloat16
F32 = jnp.float32


def dot(a, b):
    return jnp.dot(a, b, preferred_element_type=F32)


def dot_nt(a, b):
    return lax.dot_general(a, b, (((1,), (1,)), ((), ())), preferred_element_type=F32)


def onehot(rows, cols, hit):
    at = [lax.broadcasted_iota(jnp.int32, (rows, cols), k) for k in range(2)]
    return jnp.where(hit(*at), 1.0, 0.0).astype(BF)


def around(cells, halo, first, last):
    top = jnp.where(first, 0.0, halo[0].astype(F32)).astype(BF)
    bottom = jnp.where(last, 0.0, halo[1].astype(F32)).astype(BF)
    side = TILE
    west = dot(onehot(CELLS, CELLS, lambda q, k: (k == q - 1) & (lax.rem(q, side) != 0)), cells)
    west = west + dot(onehot(CELLS, side, lambda q, k: q == k * side), halo[2])
    east = dot(onehot(CELLS, CELLS, lambda q, k: (k == q + 1) & (lax.rem(q, side) != side - 1)), cells)
    east = east + dot(onehot(CELLS, side, lambda q, k: q == k * side + side - 1), halo[3])
    return (
        jnp.concatenate([top, cells[:-side]], 0).astype(F32),
        jnp.concatenate([cells[side:], bottom], 0).astype(F32),
        west,
        east,
    )


def edges(cells, out):
    out[0] = cells[CELLS - TILE :]
    out[1] = cells[:TILE]
    out[2] = dot(onehot(TILE, CELLS, lambda k, q: q == k * TILE + TILE - 1), cells).astype(BF)
    out[3] = dot(onehot(TILE, CELLS, lambda k, q: q == k * TILE), cells).astype(BF)


class Exchange:
    def __init__(self, group, copy):
        self.count, self.me, self.peers, _ = group
        self.copy = copy

    def each(self, body):
        for at in self.peers:
            body(at)

    def start(self):
        self.each(lambda at: self.copy(at, self.me).start())

    def wait(self):
        self.each(lambda at: self.copy(at, at).wait_recv())

    def sent(self):
        self.each(lambda at: self.copy(at, self.me).wait_send())


def scatter(group, src, dst, ssem, rsem):
    whom = group[3]
    return Exchange(group, lambda to, frm: pltpu.make_async_remote_copy(
        src_ref=src.at[to], dst_ref=dst.at[frm], send_sem=ssem.at[to], recv_sem=rsem.at[frm],
        device_id=whom(to), device_id_type=MESH))


def gather(group, buf, ssem, rsem):
    _, me, _, whom = group
    return Exchange(group, lambda to, frm: pltpu.make_async_remote_copy(
        src_ref=buf.at[me], dst_ref=buf.at[frm], send_sem=ssem.at[to], recv_sem=rsem.at[frm],
        device_id=whom(to), device_id_type=MESH))


class MatrixSum:
    def __init__(self, groups, buffers, sems, out):
        self.me = [group[1] for group in groups]
        self.bufs = buffers
        self.out = out
        at, self.stages = out, []
        for k, group in enumerate(groups):
            self.stages.append(scatter(group, buffers[2 * k], buffers[2 * k + 1], *sems[2 * k : 2 * k + 2]))
        for k, group in enumerate(groups):
            self.stages.insert(4, gather(group, at, *sems[8 + 2 * k : 10 + 2 * k]))
            at = at.at[group[1]]
        self.place = at

    def load(self, source):
        per = D // 256
        for c in range(2):
            for x in range(4):
                f = 4 * c + x
                rows = slice((f % per) * 256, (f % per + 1) * 256)
                cols = slice((f // per) * 128, (f // per + 1) * 128)
                self.bufs[0][c, x] = source(rows, cols).astype(BF).reshape(4, 4, 16, 128)

    def begin(self):
        self.stages[0].start()

    def step(self, stage):
        self.stages[stage].wait()
        if stage < 4:
            me = self.me[stage]
            own, got = self.bufs[2 * stage], self.bufs[2 * stage + 1]
            held = own[me].astype(F32)
            for at in self.stages[stage].peers:
                held = held + got[at].astype(F32)
            target = self.place if stage == 3 else self.bufs[2 * stage + 2]
            target[...] = held.astype(BF)
        if stage < 7:
            self.stages[stage + 1].start()
        self.stages[stage].sent()


class TapSum:
    def __init__(self, groups, buffers, sems):
        self.bufs = buffers
        self.stages = [
            gather(group, buffers[k], *sems[2 * k : 2 * k + 2]) for k, group in enumerate(groups)
        ]

    def begin(self):
        self.stages[0].start()

    def step(self, stage, out=None):
        self.stages[stage].wait()
        total = self.bufs[stage][0]
        for k in range(1, self.stages[stage].count):
            total = total + self.bufs[stage][k]
        if stage == 3:
            out[...] = total
        else:
            self.bufs[stage + 1][self.stages[stage + 1].me] = total
            self.stages[stage + 1].start()
        self.stages[stage].sent()


def kernel(
    nlat, n, dest_ref, count_ref, grid_ref, cot_ref, sten_ref, obs_in, wq_in, wk_in, wv_in, wo_in,
    enc_out, gobs_out, ggrid_out, late_ref, early_ref, taps_ref,
    send, xs, ret, relay, relay_back, kv, kt, vt, bias, wkv, qt, qzt, dozt, dot_t,
    acc_o, acc_q, m_ref, l_ref, d_ref, dkvt, dwt, gm_ref, mid_ref, sides, edge, halo,
    obs_ref, wq_ref, wo_ref, enc_ref, gobs_ref, ggrid_ref, in_sem, out_sem,
    x_ssem, x_rsem, r_ssem, r_rsem, g_ssem, g_rsem, b_ssem, b_rsem, h_ssem, h_rsem,
    *sum_scratch,
):
    lat, me = lax.axis_index("lat"), lax.axis_index("lon")
    groups = n // 2
    blocks = obs_ref.shape[0]
    loads = [
        pltpu.make_async_copy(source, target, in_sem.at[k])
        for k, (source, target) in enumerate((
            (obs_in, obs_ref), (wq_in, wq_ref), (wk_in, wkv.at[:, pl.ds(0, D)]),
            (wv_in, wkv.at[:, pl.ds(D, D)]), (wo_in, wo_ref)))
    ]
    stores = [
        pltpu.make_async_copy(source, target, out_sem.at[k])
        for k, (source, target) in enumerate((
            (ggrid_ref, ggrid_out), (enc_ref, enc_out), (gobs_ref, gobs_out)))
    ]
    x_at, core = lat // 2, lax.rem(lat, 2)
    y, z = me // SIDE, lax.rem(me, SIDE)

    def ring(me, whom):
        return SIDE, me, [lax.rem(me + o, SIDE) for o in range(1, SIDE)], whom

    on_core = (2, core, [1 - core], lambda at: {"lat": 2 * x_at + at})
    on_x = ring(x_at, lambda at: {"lat": 2 * at + core})
    on_y = ring(y, lambda at: {"lon": at * SIDE + z})
    on_z = ring(z, lambda at: {"lon": y * SIDE + at})
    orders = ((on_x, on_y, on_z), (on_y, on_z, on_x), (on_z, on_x, on_y), (on_x, on_y, on_z))
    *late, early = (
        MatrixSum(
            (on_core, *order), sum_scratch[24 * k : 24 * k + 8], sum_scratch[24 * k + 8 : 24 * k + 24],
            late_ref.at[k] if k < 3 else early_ref)
        for k, order in enumerate(orders)
    )
    tap_sum = TapSum((on_core, on_x, on_y, on_z), sum_scratch[96:100], sum_scratch[100:108])

    way_y, way_z = 1 - 2 * lax.rem(y, 2), 1 - 2 * lax.rem(z, 2)

    def place(dy, dz):
        return lax.rem(y + dy + 2 * SIDE, SIDE) * SIDE + lax.rem(z + dz + 2 * SIDE, SIDE)

    def turned(i):
        return 1 if STEPS[i] in ((0, 2), (2, 0), (2, 2)) else -1

    def leg(i, sign):
        dy, dz = STEPS[i]
        return {"lon": place(
            turned(i) * way_y if dy == 2 else sign * dy, turned(i) * way_z if dz == 2 else sign * dz)}

    def onward(i):
        dy, dz = STEPS[i]
        return {"lon": place(
            -turned(i) * way_y if dy == 2 else 0, -turned(i) * way_z if dz == 2 else 0)}

    for load in loads:
        load.start()
    barrier = pltpu.get_barrier_semaphore()
    def greet(o, carry, axis, count, at):
        pl.semaphore_signal(
            barrier, inc=1, device_id={axis: lax.rem(at + o, count)}, device_id_type=MESH)
        return carry

    lax.fori_loop(1, nlat, functools.partial(greet, axis="lat", count=nlat, at=lat), 0)
    lax.fori_loop(1, n, functools.partial(greet, axis="lon", count=n, at=me), 0)

    row_ids = lax.broadcasted_iota(jnp.int32, (EXTRA, D), 0)

    def pack(i):
        tile = place(*STEPS[i])
        number = b0 = b1 = c0 = c1 = jnp.int32(0)
        for b in range(blocks):
            hit = dest_ref[0, b] == tile
            one, two = hit & (number == 0), hit & (number == 1)
            number = number + hit.astype(jnp.int32)
            b0, b1 = jnp.where(one, b, b0), jnp.where(two, b, b1)
            c0, c1 = jnp.where(one, count_ref[0, b], c0), jnp.where(two, count_ref[0, b], c1)
        send[i, 0:BLK, :] = obs_ref[b0]
        send[i, BLK:ROWS, :] = obs_ref[b1]
        send[i, ROWS:, :] = jnp.where(row_ids == 0, c0, c1).astype(F32).astype(BF)

    edges(cot_ref[...], edge.at[0])
    loads[0].wait()
    pl.semaphore_wait(barrier, nlat + n - 2)

    def remote(src, dst, ssem, rsem, whom):
        return pltpu.make_async_remote_copy(
            src_ref=src, dst_ref=dst, send_sem=ssem, recv_sem=rsem, device_id=whom, device_id_type=MESH)

    def x_copy(i):
        if i not in FAR:
            return remote(send.at[i], xs.at[i + 1], x_ssem.at[i], x_rsem.at[i], leg(i, 1))
        j = i - FAR.start
        return remote(send.at[i], relay.at[j], x_ssem.at[i], r_rsem.at[j], leg(i, 1))

    def x_onward(i):
        j = i - FAR.start
        return remote(relay.at[j], xs.at[i + 1], r_ssem.at[j], x_rsem.at[i], onward(i))

    def g_copy(i):
        tokens = send.at[i, pl.ds(0, ROWS)]
        if i not in FAR:
            return remote(tokens, ret.at[i], g_ssem.at[i], g_rsem.at[i], leg(i, -1))
        j = i - FAR.start
        return remote(tokens, relay_back.at[j], g_ssem.at[i], b_rsem.at[j], leg(i, -1))

    def g_onward(i):
        j = i - FAR.start
        return remote(relay_back.at[j], ret.at[i], b_ssem.at[j], g_rsem.at[i], onward(i))

    def x_arrived(i):
        remote(send.at[0], xs.at[i + 1], x_ssem.at[0], x_rsem.at[i], {"lon": me}).wait_recv()

    def h_copies(which):
        whom = (
            {"lat": lax.rem(lat + 1, nlat)}, {"lat": lax.rem(lat + nlat - 1, nlat)},
            {"lon": lax.rem(me + 1, n)}, {"lon": lax.rem(me + n - 1, n)},
        )
        return [
            remote(edge.at[which, k], halo.at[which, k], h_ssem.at[which, k], h_rsem.at[which, k], whom[k])
            for k in range(4)
        ]

    for copy in h_copies(0):
        copy.start()

    for i in (*FAR, *range(1, FAR.start)):
        pack(i)
        x_copy(i).start()
    pack(0)

    xs[0, 0:ROWS, :] = grid_ref[...]
    xs[1] = send[0]
    for load in loads[1:]:
        load.wait()
    lanes = lax.broadcasted_iota(jnp.int32, (CELLS, 2 * HD), 1)
    queries = dot(grid_ref[...], wq_ref[...]).astype(BF).astype(F32) * SCALING
    for copy in h_copies(0):
        copy.wait_recv()
    up = cot_ref[...].astype(F32)
    around_up = around(cot_ref[...], halo.at[0], lat == 0, lat == nlat - 1)
    for k in range(4):
        sides[k] = around_up[k].astype(BF)
    up_north, up_south, up_west, up_east = around_up
    gm_ref[...] = (
        (1.0 + sten_ref[0:1, :]) * up + sten_ref[1:2, :] * up_south + sten_ref[2:3, :] * up_north
        + sten_ref[3:4, :] * up_east + sten_ref[4:5, :] * up_west
    ).astype(BF)
    ups = dot_nt(gm_ref[...], wo_ref[...]).astype(BF).astype(F32)
    dot_t[...] = ups.T.astype(BF)
    qt[...] = queries.T.astype(BF)
    for h in range(HEADS):
        p, e = h // 2, h % 2
        mine = (lanes >= HD) if e else (lanes < HD)
        picked = jnp.where(mine, queries[:, p * 2 * HD : (p + 1) * 2 * HD], 0.0)
        qzt[h] = picked.T.astype(BF)
        picked = jnp.where(mine, ups[:, p * 2 * HD : (p + 1) * 2 * HD], 0.0)
        dozt[h] = picked.T.astype(BF)
    acc_o[...] = jnp.zeros_like(acc_o)
    acc_q[...] = jnp.zeros_like(acc_q)
    dwt[...] = jnp.zeros_like(dwt)
    m_ref[...] = jnp.full(m_ref.shape, -1e30, F32)
    l_ref[...] = jnp.zeros_like(l_ref)
    key_ids = lax.broadcasted_iota(jnp.int32, (BLK, 128), 0).astype(F32)

    def masked(width):
        part = bias[0:width, :]
        return jnp.concatenate([part, part], 1)

    def mark(c, w):
        if w == 1:
            bias[0:ROWS, :] = jnp.zeros((ROWS, 128), F32)
            return
        for k in range(w):
            tile = xs[c + k, ROWS:, 0:128].astype(F32)
            for r in range(CAP):
                at = k * ROWS + r * BLK
                bias[at : at + BLK, :] = jnp.where(key_ids < tile[r : r + 1, :], 0.0, -1e30)

    def project(c, w, g):
        width = w * ROWS
        rows = pl.ds(pl.multiple_of(c * ROWS, ROWS), width)
        tokens = xs[pl.ds(c, w), 0:ROWS, :].reshape(width, D)
        for j in range(4):
            cols = slice(j * 256, (j + 1) * 256)
            part = dot(tokens, wkv[:, cols]).astype(BF)
            kv[rows, cols] = part
            if j < 2:
                kt[g, cols, :width] = part.T
            else:
                vt[j * 256 - D : (j + 1) * 256 - D, :width] = part.T

    def attend(c, w):
        width = w * ROWS
        mark(c, w)
        rows = pl.ds(pl.multiple_of(c * ROWS, ROWS), width)

        def four(q, carry):
            for e in range(4):
                h = 4 * q + e
                mine = pl.ds(pl.multiple_of(h * HD, HD), HD)
                here = pl.ds(pl.multiple_of((2 * q + e // 2) * 128, 128), 128)
                scores = dot(kv[rows, here], qzt[h]) + masked(width)
                old = m_ref[h]
                new = jnp.maximum(old, jnp.max(scores, 0, keepdims=True))
                raised = jnp.exp(scores - new)
                shrink = jnp.exp(old - new)
                l_ref[h] = l_ref[h] * shrink + jnp.sum(raised, 0, keepdims=True)
                m_ref[h] = new
                acc_o[mine, :] = acc_o[mine, :] * shrink + dot(vt[mine, :width], raised.astype(BF))
            return carry

        lax.fori_loop(0, HEADS // 4, four, 0)

    project(0, 1, 0)
    attend(0, 1)

    for i in FAR:
        x_copy(i).wait_recv()
        x_onward(i).start()

    for i in DIAGONAL:
        pack(i)

    def forward(step, carry):
        g = step + 1
        c = CAP * g - 1

        @pl.when(step == 2)
        def _():
            for i in FAR:
                x_onward(i).wait_send()
            for i in DIAGONAL:
                x_copy(i).start()

        @pl.when(step >= 1)
        def _():
            x_arrived(c - 1)

        x_arrived(c)
        project(c, 2, g)
        attend(c, 2)
        return carry

    lax.fori_loop(0, groups, forward, 0)

    def up_of():
        return cot_ref[...].astype(F32)

    def finish(h, carry):
        rows = pl.ds(pl.multiple_of(h * HD, HD), HD)
        total = l_ref[h]
        mixed = acc_o[rows, :] / total
        acc_o[rows, :] = mixed
        m_ref[h] = m_ref[h] + jnp.log(total)
        d_ref[h] = jnp.sum(mixed * dot_t[rows, :].astype(F32), 0, keepdims=True)
        return carry

    lax.fori_loop(0, HEADS, finish, 0)
    def middle():
        mid_ref[...] = (
            grid_ref[...].astype(F32) + dot(acc_o[...].T.astype(BF), wo_ref[...])
        ).astype(BF)
        edges(mid_ref[...], edge.at[1])
        for copy in h_copies(1):
            copy.start()
        centre = mid_ref[...].astype(F32)
        terms = tap_sum.bufs[0]
        terms[core] = jnp.zeros((8, D), F32)
        for row, side in enumerate((up_of(), *(sides[k].astype(F32) for k in (1, 0, 3, 2)))):
            terms[core, row : row + 1, :] = jnp.sum(centre * side, 0, keepdims=True)
        tap_sum.begin()
        attended = acc_o[...].astype(BF)
        early.load(lambda rows, cols: dot(attended[rows, :], gm_ref[:, cols]))
        early.begin()

    for i in range(1, n):
        x_copy(i).wait_send()

    def differentiate(c, w, g):
        width = w * ROWS
        mark(c, w)
        rows = pl.ds(pl.multiple_of(c * ROWS, ROWS), width)

        def four(q, carry):
            for e in range(4):
                h = 4 * q + e
                pair = (2 * q + e // 2) * 128
                mine = pl.ds(pl.multiple_of(h * HD, HD), HD)
                also = pl.ds(pl.multiple_of(D + h * HD, HD), HD)
                keys = kv[rows, pl.ds(pl.multiple_of(pair, 128), 128)]
                values = kv[rows, pl.ds(pl.multiple_of(D + pair, 128), 128)]
                weights = jnp.exp(dot(keys, qzt[h]) + masked(width) - m_ref[h])
                grads = (weights * (dot(values, dozt[h]) - d_ref[h])).astype(BF)
                dkvt[mine, :width] = dot_nt(qt[mine, :], grads).astype(BF)
                dkvt[also, :width] = dot_nt(dot_t[mine, :], weights.astype(BF)).astype(BF)
                acc_q[mine, :] += dot(kt[g, mine, :width], grads)
            return carry

        lax.fori_loop(0, HEADS // 4, four, 0)

    def accumulate(c, w):
        width = w * ROWS

        def weigh(j, carry):
            part = pl.ds(pl.multiple_of(j * 256, 256), 256)
            tokens = xs[pl.ds(c, w), 0:ROWS, :].reshape(width, D)
            dwt[part, :] += dot(dkvt[part, :width], tokens)
            return carry

        lax.fori_loop(0, 4, weigh, 0)

    def forward_back(k):
        for i in (CAP * BACK[k] - 2, CAP * BACK[k] - 1):
            if i in FAR:
                g_copy(i).wait_recv()
                g_onward(i).start()

    def backward(step, carry):
        g = 6 - step + 6 * ((step + 4) // 8) - 4 * ((step + 2) // 8)
        differentiate(CAP * g - 1, 2, g)

        def turn(j, inner):
            cols = pl.ds(pl.multiple_of(j * 256, 256), 256)
            part = dot(wkv[cols, :], dkvt[...]).astype(BF).T
            send[pl.ds(CAP * g - 2, 2), 0:ROWS, cols] = part.reshape(2, ROWS, 256)
            return inner

        lax.fori_loop(0, 2, turn, 0)
        for k in range(groups):
            @pl.when(step == k)
            def _(k=k):
                first = CAP * BACK[k] - 2
                if first:
                    g_copy(first).start()
                else:
                    ret[0] = send[0, 0:ROWS, :]
                g_copy(first + 1).start()
                if k >= 6:
                    forward_back(k - 6)

        accumulate(CAP * g - 1, 2)
        pl.when(step == 0)(middle)

        for stage in range(2):
            pl.when(step == 2 * stage + 2)(functools.partial(early.step, stage))
            pl.when(step == 2 * stage + 3)(functools.partial(tap_sum.step, stage))

        return carry

    lax.fori_loop(0, groups, backward, 0)
    forward_back(2)
    forward_back(3)
    differentiate(0, 1, 0)
    accumulate(0, 1)

    late[1].load(lambda rows, cols: dwt[cols, rows].astype(BF).T)
    late[1].begin()
    late[2].load(lambda rows, cols: dwt[D + cols.start : D + cols.stop, rows].astype(BF).T)
    late[2].begin()
    grad_q = (acc_q[...].T * SCALING).astype(BF)
    dwq = dot(grid_ref[...].T, grad_q)
    late[0].load(lambda rows, cols: dwq[rows, cols])
    late[0].begin()
    tap_sum.step(2)

    def late_step(stage):
        if stage < 6:
            early.step(stage + 2)
        for part in (late[1], late[2], late[0]):
            part.step(stage)

    ggrid_ref[...] = (
        gm_ref[...].astype(F32) + dot_nt(grad_q, wq_ref[...])
        + dot(wkv[...], dkvt[:, :CELLS]).T
    ).astype(BF)
    stores[0].start()
    late_step(0)
    for copy in h_copies(1):
        copy.wait_recv()
    north, south, west, east = around(mid_ref[...], halo.at[1], lat == 0, lat == nlat - 1)
    enc_ref[...] = (
        (1.0 + sten_ref[0:1, :]) * mid_ref[...].astype(F32) + sten_ref[1:2, :] * north
        + sten_ref[2:3, :] * south + sten_ref[3:4, :] * west + sten_ref[4:5, :] * east
    ).astype(BF)
    stores[1].start()
    late_step(1)
    late_step(2)
    late_step(3)
    tap_sum.step(3, taps_ref)
    late_step(4)
    late_step(5)
    for i in range(1, n):
        if i not in FAR:
            g_copy(i).wait_recv()
        else:
            g_onward(i).wait_recv()
        g_copy(i).wait_send()
        if i in FAR:
            g_onward(i).wait_send()


    def unpack(b, carry):
        tile = dest_ref[0, b]
        rank = jnp.int32(0)
        for other in range(blocks):
            rank = rank + ((dest_ref[0, other] == tile) & (other < b)).astype(jnp.int32)
        dy = lax.rem(tile // SIDE - y + SIDE, SIDE)
        dz = lax.rem(lax.rem(tile, SIDE) - z + SIDE, SIDE)
        at = jnp.int32(0)
        for i, (sy, sz) in enumerate(STEPS):
            at = jnp.where((dy == sy) & (dz == sz), i, at)
        both = ret[at]
        gobs_ref[b] = jnp.where(rank == 0, both[:BLK], both[BLK:])
        return carry

    lax.fori_loop(0, blocks, unpack, 0)
    stores[2].start()
    late_step(6)
    late_step(7)
    for which in range(2):
        for copy in h_copies(which):
            copy.wait_send()
    for copy in stores:
        copy.wait()


def write_kernel(
    enc, gobs, ggrid, late, early, taps, enc_o, gobs_o, ggrid_o, wq, wk, wv, wo, taps_o,
    enc_v, gobs_v, ggrid_v, late_v, early_v, sums_v, in_sems, out_sems,
):
    part = gobs.shape[0] // 4
    loads, stores = [], []

    def load(source, target):
        loads.append(pltpu.make_async_copy(source, target, in_sems.at[len(loads)]))
        loads[-1].start()

    def store(source, out):
        stores.append(pltpu.make_async_copy(source, out, out_sems.at[len(stores)]))
        stores[-1].start()

    load(early, early_v)
    for k in range(3):
        load(late.at[k], late_v.at[k])
    for k in range(4):
        load(gobs.at[pl.ds(k * part, part)], gobs_v.at[pl.ds(k * part, part)])
    load(enc, enc_v)
    load(ggrid, ggrid_v)
    taps_o[...] = taps[0:5, :]
    for k, (out, source) in enumerate(
            ((wo, early_v), (wq, late_v.at[0]), (wk, late_v.at[1]), (wv, late_v.at[2]))):
        loads[k].wait()
        for f in range(8):
            rows, cols = slice((f % 2) * 256, (f % 2 + 1) * 256), slice((f // 2) * 128, (f // 2 + 1) * 128)
            sums_v[k, rows, cols] = source[f // 4, f % 4].reshape(256, 128).astype(F32)
        store(sums_v.at[k], out)
    for k in range(4):
        loads[4 + k].wait()
        store(gobs_v.at[pl.ds(k * part, part)], gobs_o.at[pl.ds(k * part, part)])
    loads[8].wait()
    store(enc_v, enc_o)
    loads[9].wait()
    store(ggrid_v, ggrid_o)
    for copy in stores:
        copy.wait()


def on_device(
    grid_tokens, obs_tokens, destinations, valid_counts, w_query, w_key, w_value, w_out,
    stencil_taps, cotangent,
):
    tile_shape = grid_tokens.shape
    blocks = obs_tokens.shape[0]
    nlat, n = lax.axis_size("lat"), lax.axis_size("lon")
    vmem = pl.BlockSpec(memory_space=pltpu.VMEM)
    smem = pl.BlockSpec(memory_space=pltpu.SMEM)
    anywhere = pl.BlockSpec(memory_space=pl.ANY)
    lon_sem = pltpu.SemaphoreType.DMA((n,))
    far_sem = pltpu.SemaphoreType.DMA((len(FAR),))
    halo_sem = pltpu.SemaphoreType.DMA((2, 4))
    ring_sem, core_sem = pltpu.SemaphoreType.DMA((SIDE,)), pltpu.SemaphoreType.DMA((2,))
    sems = [core_sem] * 2 + [ring_sem] * 6
    sums = []
    for _ in range(4):
        for lead in ((2, SIDE, SIDE, SIDE), (SIDE,) * 3, (SIDE,) * 2, (SIDE,)):
            sums += [pltpu.VMEM((*lead, 16, 128), BF)] * 2
        sums += sems * 2
    sums += [pltpu.VMEM((2, 8, D), F32)] + [pltpu.VMEM((SIDE, 8, D), F32)] * 3 + sems
    tile = jax.ShapeDtypeStruct((CELLS, D), BF)
    results = pl.pallas_call(
        functools.partial(kernel, nlat, n),
        out_shape=(
            tile, jax.ShapeDtypeStruct((blocks, BLK, D), BF), tile,
            jax.ShapeDtypeStruct((3, 2, SIDE, SIDE, SIDE, 16, 128), BF),
            jax.ShapeDtypeStruct((2, SIDE, SIDE, SIDE, 16, 128), BF),
            jax.ShapeDtypeStruct((8, D), F32),
        ),
        in_specs=[smem] * 2 + [vmem] * 3 + [anywhere] * 5,
        out_specs=(anywhere,) * 3 + (vmem,) * 3,
        scratch_shapes=[
            pltpu.VMEM((n, ROWS + EXTRA, D), BF),
            pltpu.VMEM((n + 1, ROWS + EXTRA, D), BF),
            pltpu.VMEM((n, ROWS, D), BF),
            pltpu.VMEM((len(FAR), ROWS + EXTRA, D), BF),
            pltpu.VMEM((len(FAR), ROWS, D), BF),
            pltpu.VMEM(((n + 1) * ROWS, 2 * D), BF),
            pltpu.VMEM((n // 2 + 1, D, 2 * ROWS), BF),
            pltpu.VMEM((D, 2 * ROWS), BF),
            pltpu.VMEM((2 * ROWS, 128), F32),
            pltpu.VMEM((D, 2 * D), BF),
            pltpu.VMEM((D, CELLS), BF),
            pltpu.VMEM((HEADS, 2 * HD, CELLS), BF),
            pltpu.VMEM((HEADS, 2 * HD, CELLS), BF),
            pltpu.VMEM((D, CELLS), BF),
            pltpu.VMEM((D, CELLS), F32),
            pltpu.VMEM((D, CELLS), F32),
            pltpu.VMEM((HEADS, 1, CELLS), F32),
            pltpu.VMEM((HEADS, 1, CELLS), F32),
            pltpu.VMEM((HEADS, 1, CELLS), F32),
            pltpu.VMEM((2 * D, 2 * ROWS), BF),
            pltpu.VMEM((2 * D, D), F32),
            pltpu.VMEM((CELLS, D), BF),
            pltpu.VMEM((CELLS, D), BF),
            pltpu.VMEM((4, CELLS, D), BF),
            pltpu.VMEM((2, 4, TILE, D), BF),
            pltpu.VMEM((2, 4, TILE, D), BF),
            pltpu.VMEM((blocks, BLK, D), BF),
            pltpu.VMEM((D, D), BF),
            pltpu.VMEM((D, D), BF),
            pltpu.VMEM((CELLS, D), BF),
            pltpu.VMEM((blocks, BLK, D), BF),
            pltpu.VMEM((CELLS, D), BF),
            pltpu.SemaphoreType.DMA((5,)),
            pltpu.SemaphoreType.DMA((3,)),
            lon_sem, lon_sem, far_sem, far_sem, lon_sem, lon_sem, far_sem, far_sem, halo_sem, halo_sem,
            *sums,
        ],
        compiler_params=pltpu.CompilerParams(
            collective_id=0, has_side_effects=True, vmem_limit_bytes=62 * 2**20
        ),
        name="encoder_step",
    )(
        destinations.reshape(1, blocks), valid_counts, grid_tokens.reshape(CELLS, D),
        cotangent.reshape(CELLS, D), stencil_taps, obs_tokens, w_query, w_key, w_value, w_out,
    )
    matrix = jax.ShapeDtypeStruct((D, D), F32)
    encoded, grad_obs, grad_grid, *sums = pl.pallas_call(
        write_kernel,
        out_shape=(
            tile, jax.ShapeDtypeStruct((blocks, BLK, D), BF), tile, matrix, matrix, matrix, matrix,
            jax.ShapeDtypeStruct((5, D), F32),
        ),
        in_specs=[anywhere] * 5 + [vmem],
        out_specs=(anywhere,) * 7 + (vmem,),
        scratch_shapes=[
            pltpu.VMEM((CELLS, D), BF), pltpu.VMEM((blocks, BLK, D), BF), pltpu.VMEM((CELLS, D), BF),
            pltpu.VMEM((3, 2, SIDE, SIDE, SIDE, 16, 128), BF), pltpu.VMEM((2, SIDE, SIDE, SIDE, 16, 128), BF),
            pltpu.VMEM((4, D, D), F32), pltpu.SemaphoreType.DMA((10,)), pltpu.SemaphoreType.DMA((10,)),
        ],
        compiler_params=pltpu.CompilerParams(vmem_limit_bytes=62 * 2**20),
        name="write_results",
    )(*results)
    return (encoded.reshape(tile_shape), grad_grid.reshape(tile_shape), grad_obs, *sums)


def solution(mesh):
    in_specs = (
        P("lat", "lon", None),
        P(("lat", "lon"), None, None),
        P(("lat", "lon"), None),
        P(("lat", "lon"), None),
        P(),
        P(),
        P(),
        P(),
        P(),
        P("lat", "lon", None),
    )
    out_specs = (
        P("lat", "lon", None),
        P("lat", "lon", None),
        P(("lat", "lon"), None, None),
        P(),
        P(),
        P(),
        P(),
        P(),
    )
    return jax.shard_map(
        on_device, mesh=mesh, in_specs=in_specs, out_specs=out_specs, check_vma=False
    )
```

```python
import functools

import jax
import jax.numpy as jnp
from jax import lax
from jax.experimental import pallas as pl
from jax.experimental.pallas import tpu as pltpu
from jax.sharding import PartitionSpec as P

D = 512
HEADS = 8
HD = D // HEADS
BLK = 128
CAP = 2
ROWS = CAP * BLK
CELLS = 256
TILE = 16
SCALING = HD ** (-0.5)
MESH = pl.DeviceIdType.MESH
SIDE = 4
STEPS = (
    (0, 0), (0, 1), (0, 3), (1, 0), (3, 0),
    (0, 2), (2, 0), (1, 2), (3, 2), (2, 1), (2, 3), (2, 2),
    (1, 1), (1, 3), (3, 1), (3, 3),
)
FAR = range(5, 12)
DIAGONAL = range(12, 16)
BACK = (6, 5, 4, 3, 8, 7, 2, 1)
EXTRA = 16
BF = jnp.bfloat16
F32 = jnp.float32


def dot(a, b):
    return jnp.dot(a, b, preferred_element_type=F32)


def dot_nt(a, b):
    return lax.dot_general(a, b, (((1,), (1,)), ((), ())), preferred_element_type=F32)


def onehot(rows, cols, hit):
    at = [lax.broadcasted_iota(jnp.int32, (rows, cols), k) for k in range(2)]
    return jnp.where(hit(*at), 1.0, 0.0).astype(BF)


def around(cells, halo, first, last):
    top = jnp.where(first, 0.0, halo[0].astype(F32)).astype(BF)
    bottom = jnp.where(last, 0.0, halo[1].astype(F32)).astype(BF)
    side = TILE
    west = dot(onehot(CELLS, CELLS, lambda q, k: (k == q - 1) & (lax.rem(q, side) != 0)), cells)
    west = west + dot(onehot(CELLS, side, lambda q, k: q == k * side), halo[2])
    east = dot(onehot(CELLS, CELLS, lambda q, k: (k == q + 1) & (lax.rem(q, side) != side - 1)), cells)
    east = east + dot(onehot(CELLS, side, lambda q, k: q == k * side + side - 1), halo[3])
    return (
        jnp.concatenate([top, cells[:-side]], 0).astype(F32),
        jnp.concatenate([cells[side:], bottom], 0).astype(F32),
        west,
        east,
    )


def edges(cells, out):
    out[0] = cells[CELLS - TILE :]
    out[1] = cells[:TILE]
    out[2] = dot(onehot(TILE, CELLS, lambda k, q: q == k * TILE + TILE - 1), cells).astype(BF)
    out[3] = dot(onehot(TILE, CELLS, lambda k, q: q == k * TILE), cells).astype(BF)


class Exchange:
    def __init__(self, group, copy, every):
        self.count, self.me, self.peers, _ = group
        self.copy, self.every = copy, every

    def start(self):
        for at in self.peers:
            self.copy(at).start()

    def wait(self):
        self.every.wait_recv()

    def sent(self):
        self.every.wait_send()


def exchange(group, pieces, dst, ssem, rsem):
    count, me, peers, whom = group

    def copy(src, into, to):
        return pltpu.make_async_remote_copy(
            src_ref=src, dst_ref=into, send_sem=ssem, recv_sem=rsem, device_id=whom(to),
            device_id_type=MESH)

    whole = dst.at[pl.ds(0, count - 1)]
    return Exchange(group, lambda to: copy(pieces(to), dst.at[me], to), copy(whole, whole, peers[0]))


def scatter(group, src, dst, ssem, rsem):
    return exchange(group, lambda to: src.at[to], dst, ssem, rsem)


def gather(group, buf, ssem, rsem):
    return exchange(group, lambda to: buf.at[group[1]], buf, ssem, rsem)


class MatrixSum:
    def __init__(self, groups, buffers, sems, out):
        self.me = [group[1] for group in groups]
        self.bufs = buffers
        self.out = out
        at, self.stages = out, []
        for k, group in enumerate(groups):
            self.stages.append(scatter(group, buffers[2 * k], buffers[2 * k + 1], *sems[2 * k : 2 * k + 2]))
        for k, group in enumerate(groups):
            self.stages.insert(4, gather(group, at, *sems[8 + 2 * k : 10 + 2 * k]))
            at = at.at[group[1]]
        self.place = at

    def load(self, source):
        per = D // 256
        for c in range(2):
            for x in range(4):
                f = 4 * c + x
                rows = slice((f % per) * 256, (f % per + 1) * 256)
                cols = slice((f // per) * 128, (f // per + 1) * 128)
                self.bufs[0][c, x] = source(rows, cols).astype(BF).reshape(4, 4, 16, 128)

    def begin(self):
        self.stages[0].start()

    def step(self, stage):
        self.stages[stage].wait()
        if stage < 4:
            me = self.me[stage]
            own, got = self.bufs[2 * stage], self.bufs[2 * stage + 1]
            held = own[me].astype(F32)
            for at in self.stages[stage].peers:
                held = held + got[at].astype(F32)
            target = self.place if stage == 3 else self.bufs[2 * stage + 2]
            target[...] = held.astype(BF)
        if stage < 7:
            self.stages[stage + 1].start()
        self.stages[stage].sent()


class TapSum:
    def __init__(self, groups, buffers, sems):
        self.bufs = buffers
        self.stages = [
            gather(group, buffers[k], *sems[2 * k : 2 * k + 2]) for k, group in enumerate(groups)
        ]

    def begin(self):
        self.stages[0].start()

    def step(self, stage, out=None):
        self.stages[stage].wait()
        total = self.bufs[stage][0]
        for k in range(1, self.stages[stage].count):
            total = total + self.bufs[stage][k]
        if stage == 3:
            out[...] = total
        else:
            self.bufs[stage + 1][self.stages[stage + 1].me] = total
            self.stages[stage + 1].start()
        self.stages[stage].sent()


def kernel(
    nlat, n, dest_ref, count_ref, grid_ref, cot_ref, sten_ref, obs_in, wq_in, wk_in, wv_in, wo_in,
    enc_out, gobs_out, ggrid_out, late_ref, early_ref, taps_ref,
    send, xs, ret, relay, relay_back, kv, kt, vt, bias, wkv, qt, qzt, dozt, dot_t,
    acc_o, acc_q, m_ref, l_ref, d_ref, dkvt, dwt, gm_ref, mid_ref, sides, edge, halo,
    obs_ref, wq_ref, wo_ref, enc_ref, gobs_ref, ggrid_ref, in_sem, out_sem,
    x_ssem, x_rsem, r_ssem, r_rsem, g_ssem, g_rsem, b_ssem, b_rsem, h_ssem, h_rsem,
    *sum_scratch,
):
    lat, me = lax.axis_index("lat"), lax.axis_index("lon")
    groups = n // 2
    blocks = obs_ref.shape[0]
    loads = [
        pltpu.make_async_copy(source, target, in_sem.at[k])
        for k, (source, target) in enumerate((
            (obs_in, obs_ref), (wq_in, wq_ref), (wk_in, wkv.at[:, pl.ds(0, D)]),
            (wv_in, wkv.at[:, pl.ds(D, D)]), (wo_in, wo_ref)))
    ]
    stores = [
        pltpu.make_async_copy(source, target, out_sem.at[k])
        for k, (source, target) in enumerate((
            (ggrid_ref, ggrid_out), (enc_ref, enc_out), (gobs_ref, gobs_out)))
    ]
    x_at, core = lat // 2, lax.rem(lat, 2)
    y, z = me // SIDE, lax.rem(me, SIDE)

    def ring(me, whom):
        return SIDE, me, [lax.rem(me + o, SIDE) for o in range(1, SIDE)], whom

    on_core = (2, core, [1 - core], lambda at: {"lat": 2 * x_at + at})
    on_x = ring(x_at, lambda at: {"lat": 2 * at + core})
    on_y = ring(y, lambda at: {"lon": at * SIDE + z})
    on_z = ring(z, lambda at: {"lon": y * SIDE + at})
    orders = ((on_x, on_y, on_z), (on_y, on_z, on_x), (on_z, on_x, on_y), (on_x, on_y, on_z))
    *late, early = (
        MatrixSum(
            (on_core, *order), sum_scratch[24 * k : 24 * k + 8], sum_scratch[24 * k + 8 : 24 * k + 24],
            late_ref.at[k] if k < 3 else early_ref)
        for k, order in enumerate(orders)
    )
    tap_sum = TapSum((on_core, on_x, on_y, on_z), sum_scratch[96:100], sum_scratch[100:108])

    way_y, way_z = 1 - 2 * lax.rem(y, 2), 1 - 2 * lax.rem(z, 2)

    def place(dy, dz):
        return lax.rem(y + dy + 2 * SIDE, SIDE) * SIDE + lax.rem(z + dz + 2 * SIDE, SIDE)

    def turned(i):
        return 1 if STEPS[i] in ((0, 2), (2, 0), (2, 2)) else -1

    def leg(i, sign):
        dy, dz = STEPS[i]
        return {"lon": place(
            turned(i) * way_y if dy == 2 else sign * dy, turned(i) * way_z if dz == 2 else sign * dz)}

    def onward(i):
        dy, dz = STEPS[i]
        return {"lon": place(
            -turned(i) * way_y if dy == 2 else 0, -turned(i) * way_z if dz == 2 else 0)}

    for load in loads:
        load.start()
    barrier = pltpu.get_barrier_semaphore()
    def greet(o, carry, axis, count, at):
        pl.semaphore_signal(
            barrier, inc=1, device_id={axis: lax.rem(at + o, count)}, device_id_type=MESH)
        return carry

    lax.fori_loop(1, nlat, functools.partial(greet, axis="lat", count=nlat, at=lat), 0)
    lax.fori_loop(1, n, functools.partial(greet, axis="lon", count=n, at=me), 0)

    row_ids = lax.broadcasted_iota(jnp.int32, (EXTRA, D), 0)

    def pack(i):
        tile = place(*STEPS[i])
        number = b0 = b1 = c0 = c1 = jnp.int32(0)
        for b in range(blocks):
            hit = dest_ref[0, b] == tile
            one, two = hit & (number == 0), hit & (number == 1)
            number = number + hit.astype(jnp.int32)
            b0, b1 = jnp.where(one, b, b0), jnp.where(two, b, b1)
            c0, c1 = jnp.where(one, count_ref[0, b], c0), jnp.where(two, count_ref[0, b], c1)
        send[i, 0:BLK, :] = obs_ref[b0]
        send[i, BLK:ROWS, :] = obs_ref[b1]
        send[i, ROWS:, :] = jnp.where(row_ids == 0, c0, c1).astype(F32).astype(BF)

    edges(cot_ref[...], edge.at[0])
    loads[0].wait()
    pl.semaphore_wait(barrier, nlat + n - 2)

    def remote(src, dst, ssem, rsem, whom):
        return pltpu.make_async_remote_copy(
            src_ref=src, dst_ref=dst, send_sem=ssem, recv_sem=rsem, device_id=whom, device_id_type=MESH)

    def x_copy(i):
        if i not in FAR:
            return remote(send.at[i], xs.at[i + 1], x_ssem.at[i], x_rsem.at[i], leg(i, 1))
        j = i - FAR.start
        return remote(send.at[i], relay.at[j], x_ssem.at[i], r_rsem.at[j], leg(i, 1))

    def x_onward(i):
        j = i - FAR.start
        return remote(relay.at[j], xs.at[i + 1], r_ssem.at[j], x_rsem.at[i], onward(i))

    def g_copy(i):
        tokens = send.at[i, pl.ds(0, ROWS)]
        if i not in FAR:
            return remote(tokens, ret.at[i], g_ssem.at[i], g_rsem.at[i], leg(i, -1))
        j = i - FAR.start
        return remote(tokens, relay_back.at[j], g_ssem.at[i], b_rsem.at[j], leg(i, -1))

    def g_onward(i):
        j = i - FAR.start
        return remote(relay_back.at[j], ret.at[i], b_ssem.at[j], g_rsem.at[i], onward(i))

    def x_arrived(i):
        remote(send.at[0], xs.at[i + 1], x_ssem.at[0], x_rsem.at[i], {"lon": me}).wait_recv()

    def h_copies(which):
        whom = (
            {"lat": lax.rem(lat + 1, nlat)}, {"lat": lax.rem(lat + nlat - 1, nlat)},
            {"lon": lax.rem(me + 1, n)}, {"lon": lax.rem(me + n - 1, n)},
        )
        return [
            remote(edge.at[which, k], halo.at[which, k], h_ssem.at[which, k], h_rsem.at[which, k], whom[k])
            for k in range(4)
        ]

    for copy in h_copies(0):
        copy.start()

    for i in (*FAR, *range(1, FAR.start)):
        pack(i)
        x_copy(i).start()
    pack(0)

    xs[0, 0:ROWS, :] = grid_ref[...]
    xs[1] = send[0]
    for load in loads[1:]:
        load.wait()
    lanes = lax.broadcasted_iota(jnp.int32, (CELLS, 2 * HD), 1)
    queries = dot(grid_ref[...], wq_ref[...]).astype(BF).astype(F32) * SCALING
    for copy in h_copies(0):
        copy.wait_recv()
    up = cot_ref[...].astype(F32)
    around_up = around(cot_ref[...], halo.at[0], lat == 0, lat == nlat - 1)
    for k in range(4):
        sides[k] = around_up[k].astype(BF)
    up_north, up_south, up_west, up_east = around_up
    gm_ref[...] = (
        (1.0 + sten_ref[0:1, :]) * up + sten_ref[1:2, :] * up_south + sten_ref[2:3, :] * up_north
        + sten_ref[3:4, :] * up_east + sten_ref[4:5, :] * up_west
    ).astype(BF)
    ups = dot_nt(gm_ref[...], wo_ref[...]).astype(BF).astype(F32)
    dot_t[...] = ups.T.astype(BF)
    qt[...] = queries.T.astype(BF)
    for h in range(HEADS):
        p, e = h // 2, h % 2
        mine = (lanes >= HD) if e else (lanes < HD)
        picked = jnp.where(mine, queries[:, p * 2 * HD : (p + 1) * 2 * HD], 0.0)
        qzt[h] = picked.T.astype(BF)
        picked = jnp.where(mine, ups[:, p * 2 * HD : (p + 1) * 2 * HD], 0.0)
        dozt[h] = picked.T.astype(BF)
    acc_o[...] = jnp.zeros_like(acc_o)
    acc_q[...] = jnp.zeros_like(acc_q)
    dwt[...] = jnp.zeros_like(dwt)
    m_ref[...] = jnp.full(m_ref.shape, -1e30, F32)
    l_ref[...] = jnp.zeros_like(l_ref)
    key_ids = lax.broadcasted_iota(jnp.int32, (BLK, 128), 0).astype(F32)

    def masked(width):
        part = bias[0:width, :]
        return jnp.concatenate([part, part], 1)

    def mark(c, w):
        if w == 1:
            bias[0:ROWS, :] = jnp.zeros((ROWS, 128), F32)
            return
        for k in range(w):
            tile = xs[c + k, ROWS:, 0:128].astype(F32)
            for r in range(CAP):
                at = k * ROWS + r * BLK
                bias[at : at + BLK, :] = jnp.where(key_ids < tile[r : r + 1, :], 0.0, -1e30)

    def project(c, w, g):
        width = w * ROWS
        rows = pl.ds(pl.multiple_of(c * ROWS, ROWS), width)
        tokens = xs[pl.ds(c, w), 0:ROWS, :].reshape(width, D)
        for j in range(4):
            cols = slice(j * 256, (j + 1) * 256)
            part = dot(tokens, wkv[:, cols]).astype(BF)
            kv[rows, cols] = part
            if j < 2:
                kt[g, cols, :width] = part.T
            else:
                vt[j * 256 - D : (j + 1) * 256 - D, :width] = part.T

    def attend(c, w):
        width = w * ROWS
        mark(c, w)
        rows = pl.ds(pl.multiple_of(c * ROWS, ROWS), width)

        def four(q, carry):
            for e in range(4):
                h = 4 * q + e
                mine = pl.ds(pl.multiple_of(h * HD, HD), HD)
                here = pl.ds(pl.multiple_of((2 * q + e // 2) * 128, 128), 128)
                scores = dot(kv[rows, here], qzt[h]) + masked(width)
                old = m_ref[h]
                new = jnp.maximum(old, jnp.max(scores, 0, keepdims=True))
                raised = jnp.exp(scores - new)
                shrink = jnp.exp(old - new)
                l_ref[h] = l_ref[h] * shrink + jnp.sum(raised, 0, keepdims=True)
                m_ref[h] = new
                acc_o[mine, :] = acc_o[mine, :] * shrink + dot(vt[mine, :width], raised.astype(BF))
            return carry

        lax.fori_loop(0, HEADS // 4, four, 0)

    project(0, 1, 0)
    attend(0, 1)

    for i in FAR:
        x_copy(i).wait_recv()
        x_onward(i).start()

    for i in DIAGONAL:
        pack(i)

    def forward(step, carry):
        g = step + 1
        c = CAP * g - 1

        @pl.when(step == 2)
        def _():
            for i in FAR:
                x_onward(i).wait_send()
            for i in DIAGONAL:
                x_copy(i).start()

        @pl.when(step >= 1)
        def _():
            x_arrived(c - 1)

        x_arrived(c)
        project(c, 2, g)
        attend(c, 2)
        return carry

    lax.fori_loop(0, groups, forward, 0)

    def up_of():
        return cot_ref[...].astype(F32)

    def finish(h, carry):
        rows = pl.ds(pl.multiple_of(h * HD, HD), HD)
        total = l_ref[h]
        mixed = acc_o[rows, :] / total
        acc_o[rows, :] = mixed
        m_ref[h] = m_ref[h] + jnp.log(total)
        d_ref[h] = jnp.sum(mixed * dot_t[rows, :].astype(F32), 0, keepdims=True)
        return carry

    lax.fori_loop(0, HEADS, finish, 0)
    def middle():
        mid_ref[...] = (
            grid_ref[...].astype(F32) + dot(acc_o[...].T.astype(BF), wo_ref[...])
        ).astype(BF)
        edges(mid_ref[...], edge.at[1])
        for copy in h_copies(1):
            copy.start()
        centre = mid_ref[...].astype(F32)
        terms = tap_sum.bufs[0]
        terms[core] = jnp.zeros((8, D), F32)
        for row, side in enumerate((up_of(), *(sides[k].astype(F32) for k in (1, 0, 3, 2)))):
            terms[core, row : row + 1, :] = jnp.sum(centre * side, 0, keepdims=True)
        tap_sum.begin()
        attended = acc_o[...].astype(BF)
        early.load(lambda rows, cols: dot(attended[rows, :], gm_ref[:, cols]))
        early.begin()

    for i in range(1, n):
        x_copy(i).wait_send()

    def differentiate(c, w, g, half):
        width = w * ROWS
        lanes = pl.ds(pl.multiple_of(half * 2 * ROWS, 2 * ROWS), width)
        mark(c, w)
        rows = pl.ds(pl.multiple_of(c * ROWS, ROWS), width)

        def four(q, carry):
            for e in range(4):
                h = 4 * q + e
                pair = (2 * q + e // 2) * 128
                mine = pl.ds(pl.multiple_of(h * HD, HD), HD)
                also = pl.ds(pl.multiple_of(D + h * HD, HD), HD)
                keys = kv[rows, pl.ds(pl.multiple_of(pair, 128), 128)]
                values = kv[rows, pl.ds(pl.multiple_of(D + pair, 128), 128)]
                weights = jnp.exp(dot(keys, qzt[h]) + masked(width) - m_ref[h])
                grads = (weights * (dot(values, dozt[h]) - d_ref[h])).astype(BF)
                dkvt[mine, lanes] = dot_nt(qt[mine, :], grads).astype(BF)
                dkvt[also, lanes] = dot_nt(dot_t[mine, :], weights.astype(BF)).astype(BF)
                acc_q[mine, :] += dot(kt[g, mine, :width], grads)
            return carry

        lax.fori_loop(0, HEADS // 4, four, 0)

    def accumulate(c, w):
        width = w * ROWS

        def weigh(j, carry):
            part = pl.ds(pl.multiple_of(j * 256, 256), 256)
            tokens = xs[pl.ds(c, w), 0:ROWS, :].reshape(width, D)
            dwt[part, :] += dot(dkvt[part, :width], tokens)
            return carry

        lax.fori_loop(0, 4, weigh, 0)

    def forward_back(k):
        for i in (CAP * BACK[k] - 2, CAP * BACK[k] - 1):
            if i in FAR:
                g_copy(i).wait_recv()
                g_onward(i).start()

    def backward(step, carry):
        g = 6 - step + 6 * ((step + 4) // 8) - 4 * ((step + 2) // 8)
        half = 1 - lax.rem(step, 2)
        differentiate(CAP * g - 1, 2, g, half)
        lanes = pl.ds(pl.multiple_of(half * 2 * ROWS, 2 * ROWS), 2 * ROWS)

        def turn(j, inner):
            cols = pl.ds(pl.multiple_of(j * 256, 256), 256)
            part = dot(wkv[cols, :], dkvt[:, lanes]).astype(BF).T
            send[pl.ds(CAP * g - 2, 2), 0:ROWS, cols] = part.reshape(2, ROWS, 256)
            return inner

        lax.fori_loop(0, 2, turn, 0)
        for k in range(groups):
            @pl.when(step == k)
            def _(k=k):
                first = CAP * BACK[k] - 2
                if first:
                    g_copy(first).start()
                else:
                    ret[0] = send[0, 0:ROWS, :]
                g_copy(first + 1).start()
                if k >= 6:
                    forward_back(k - 6)

        @pl.when(half == 0)
        def _():
            accumulate(CAP * g - 1, 4)

        pl.when(step == 0)(middle)

        for stage in range(2):
            pl.when(step == 2 * stage + 2)(functools.partial(early.step, stage))
            pl.when(step == 2 * stage + 3)(functools.partial(tap_sum.step, stage))

        return carry

    lax.fori_loop(0, groups, backward, 0)
    forward_back(2)
    forward_back(3)
    differentiate(0, 1, 0, 0)
    accumulate(0, 1)

    late[1].load(lambda rows, cols: dwt[cols, rows].astype(BF).T)
    late[1].begin()
    late[2].load(lambda rows, cols: dwt[D + cols.start : D + cols.stop, rows].astype(BF).T)
    late[2].begin()
    grad_q = (acc_q[...].T * SCALING).astype(BF)
    dwq = dot(grid_ref[...].T, grad_q)
    late[0].load(lambda rows, cols: dwq[rows, cols])
    late[0].begin()
    tap_sum.step(2)

    def late_step(stage):
        if stage < 6:
            early.step(stage + 2)
        for part in (late[1], late[2], late[0]):
            part.step(stage)

    ggrid_ref[...] = (
        gm_ref[...].astype(F32) + dot_nt(grad_q, wq_ref[...])
        + dot(wkv[...], dkvt[:, :CELLS]).T
    ).astype(BF)
    stores[0].start()
    late_step(0)
    for copy in h_copies(1):
        copy.wait_recv()
    north, south, west, east = around(mid_ref[...], halo.at[1], lat == 0, lat == nlat - 1)
    enc_ref[...] = (
        (1.0 + sten_ref[0:1, :]) * mid_ref[...].astype(F32) + sten_ref[1:2, :] * north
        + sten_ref[2:3, :] * south + sten_ref[3:4, :] * west + sten_ref[4:5, :] * east
    ).astype(BF)
    stores[1].start()
    late_step(1)
    late_step(2)
    late_step(3)
    tap_sum.step(3, taps_ref)
    late_step(4)
    late_step(5)
    for i in range(1, n):
        if i not in FAR:
            g_copy(i).wait_recv()
        else:
            g_onward(i).wait_recv()
        g_copy(i).wait_send()
        if i in FAR:
            g_onward(i).wait_send()


    def unpack(b, carry):
        tile = dest_ref[0, b]
        rank = jnp.int32(0)
        for other in range(blocks):
            rank = rank + ((dest_ref[0, other] == tile) & (other < b)).astype(jnp.int32)
        dy = lax.rem(tile // SIDE - y + SIDE, SIDE)
        dz = lax.rem(lax.rem(tile, SIDE) - z + SIDE, SIDE)
        at = jnp.int32(0)
        for i, (sy, sz) in enumerate(STEPS):
            at = jnp.where((dy == sy) & (dz == sz), i, at)
        both = ret[at]
        gobs_ref[b] = jnp.where(rank == 0, both[:BLK], both[BLK:])
        return carry

    lax.fori_loop(0, blocks, unpack, 0)
    stores[2].start()
    late_step(6)
    late_step(7)
    for which in range(2):
        for copy in h_copies(which):
            copy.wait_send()
    for copy in stores:
        copy.wait()


def write_kernel(
    enc, gobs, ggrid, late, early, taps, enc_o, gobs_o, ggrid_o, wq, wk, wv, wo, taps_o,
    enc_v, gobs_v, ggrid_v, late_v, early_v, sums_v, in_sems, out_sems,
):
    part = gobs.shape[0] // 4
    loads, stores = [], []

    def load(source, target):
        loads.append(pltpu.make_async_copy(source, target, in_sems.at[len(loads)]))
        loads[-1].start()

    def store(source, out):
        stores.append(pltpu.make_async_copy(source, out, out_sems.at[len(stores)]))
        stores[-1].start()

    load(early, early_v)
    for k in range(3):
        load(late.at[k], late_v.at[k])
    for k in range(4):
        load(gobs.at[pl.ds(k * part, part)], gobs_v.at[pl.ds(k * part, part)])
    load(enc, enc_v)
    load(ggrid, ggrid_v)
    taps_o[...] = taps[0:5, :]
    for k, (out, source) in enumerate(
            ((wo, early_v), (wq, late_v.at[0]), (wk, late_v.at[1]), (wv, late_v.at[2]))):
        loads[k].wait()
        for f in range(8):
            rows, cols = slice((f % 2) * 256, (f % 2 + 1) * 256), slice((f // 2) * 128, (f // 2 + 1) * 128)
            sums_v[k, rows, cols] = source[f // 4, f % 4].reshape(256, 128).astype(F32)
        store(sums_v.at[k], out)
    for k in range(4):
        loads[4 + k].wait()
        store(gobs_v.at[pl.ds(k * part, part)], gobs_o.at[pl.ds(k * part, part)])
    loads[8].wait()
    store(enc_v, enc_o)
    loads[9].wait()
    store(ggrid_v, ggrid_o)
    for copy in stores:
        copy.wait()


def on_device(
    grid_tokens, obs_tokens, destinations, valid_counts, w_query, w_key, w_value, w_out,
    stencil_taps, cotangent,
):
    tile_shape = grid_tokens.shape
    blocks = obs_tokens.shape[0]
    nlat, n = lax.axis_size("lat"), lax.axis_size("lon")
    vmem = pl.BlockSpec(memory_space=pltpu.VMEM)
    smem = pl.BlockSpec(memory_space=pltpu.SMEM)
    anywhere = pl.BlockSpec(memory_space=pl.ANY)
    lon_sem = pltpu.SemaphoreType.DMA((n,))
    far_sem = pltpu.SemaphoreType.DMA((len(FAR),))
    halo_sem = pltpu.SemaphoreType.DMA((2, 4))
    sems = [pltpu.SemaphoreType.DMA] * 8
    sums = []
    for _ in range(4):
        for lead in ((2, SIDE, SIDE, SIDE), (SIDE,) * 3, (SIDE,) * 2, (SIDE,)):
            sums += [pltpu.VMEM((*lead, 16, 128), BF)] * 2
        sums += sems * 2
    sums += [pltpu.VMEM((2, 8, D), F32)] + [pltpu.VMEM((SIDE, 8, D), F32)] * 3 + sems
    tile = jax.ShapeDtypeStruct((CELLS, D), BF)
    results = pl.pallas_call(
        functools.partial(kernel, nlat, n),
        out_shape=(
            tile, jax.ShapeDtypeStruct((blocks, BLK, D), BF), tile,
            jax.ShapeDtypeStruct((3, 2, SIDE, SIDE, SIDE, 16, 128), BF),
            jax.ShapeDtypeStruct((2, SIDE, SIDE, SIDE, 16, 128), BF),
            jax.ShapeDtypeStruct((8, D), F32),
        ),
        in_specs=[smem] * 2 + [vmem] * 3 + [anywhere] * 5,
        out_specs=(anywhere,) * 3 + (vmem,) * 3,
        scratch_shapes=[
            pltpu.VMEM((n, ROWS + EXTRA, D), BF),
            pltpu.VMEM((n + 1, ROWS + EXTRA, D), BF),
            pltpu.VMEM((n, ROWS, D), BF),
            pltpu.VMEM((len(FAR), ROWS + EXTRA, D), BF),
            pltpu.VMEM((len(FAR), ROWS, D), BF),
            pltpu.VMEM(((n + 1) * ROWS, 2 * D), BF),
            pltpu.VMEM((n // 2 + 1, D, 2 * ROWS), BF),
            pltpu.VMEM((D, 2 * ROWS), BF),
            pltpu.VMEM((2 * ROWS, 128), F32),
            pltpu.VMEM((D, 2 * D), BF),
            pltpu.VMEM((D, CELLS), BF),
            pltpu.VMEM((HEADS, 2 * HD, CELLS), BF),
            pltpu.VMEM((HEADS, 2 * HD, CELLS), BF),
            pltpu.VMEM((D, CELLS), BF),
            pltpu.VMEM((D, CELLS), F32),
            pltpu.VMEM((D, CELLS), F32),
            pltpu.VMEM((HEADS, 1, CELLS), F32),
            pltpu.VMEM((HEADS, 1, CELLS), F32),
            pltpu.VMEM((HEADS, 1, CELLS), F32),
            pltpu.VMEM((2 * D, 4 * ROWS), BF),
            pltpu.VMEM((2 * D, D), F32),
            pltpu.VMEM((CELLS, D), BF),
            pltpu.VMEM((CELLS, D), BF),
            pltpu.VMEM((4, CELLS, D), BF),
            pltpu.VMEM((2, 4, TILE, D), BF),
            pltpu.VMEM((2, 4, TILE, D), BF),
            pltpu.VMEM((blocks, BLK, D), BF),
            pltpu.VMEM((D, D), BF),
            pltpu.VMEM((D, D), BF),
            pltpu.VMEM((CELLS, D), BF),
            pltpu.VMEM((blocks, BLK, D), BF),
            pltpu.VMEM((CELLS, D), BF),
            pltpu.SemaphoreType.DMA((5,)),
            pltpu.SemaphoreType.DMA((3,)),
            lon_sem, lon_sem, far_sem, far_sem, lon_sem, lon_sem, far_sem, far_sem, halo_sem, halo_sem,
            *sums,
        ],
        compiler_params=pltpu.CompilerParams(
            collective_id=0, has_side_effects=True, vmem_limit_bytes=62 * 2**20
        ),
        name="encoder_step",
    )(
        destinations.reshape(1, blocks), valid_counts, grid_tokens.reshape(CELLS, D),
        cotangent.reshape(CELLS, D), stencil_taps, obs_tokens, w_query, w_key, w_value, w_out,
    )
    matrix = jax.ShapeDtypeStruct((D, D), F32)
    encoded, grad_obs, grad_grid, *sums = pl.pallas_call(
        write_kernel,
        out_shape=(
            tile, jax.ShapeDtypeStruct((blocks, BLK, D), BF), tile, matrix, matrix, matrix, matrix,
            jax.ShapeDtypeStruct((5, D), F32),
        ),
        in_specs=[anywhere] * 5 + [vmem],
        out_specs=(anywhere,) * 7 + (vmem,),
        scratch_shapes=[
            pltpu.VMEM((CELLS, D), BF), pltpu.VMEM((blocks, BLK, D), BF), pltpu.VMEM((CELLS, D), BF),
            pltpu.VMEM((3, 2, SIDE, SIDE, SIDE, 16, 128), BF), pltpu.VMEM((2, SIDE, SIDE, SIDE, 16, 128), BF),
            pltpu.VMEM((4, D, D), F32), pltpu.SemaphoreType.DMA((10,)), pltpu.SemaphoreType.DMA((10,)),
        ],
        compiler_params=pltpu.CompilerParams(vmem_limit_bytes=62 * 2**20),
        name="write_results",
    )(*results)
    return (encoded.reshape(tile_shape), grad_grid.reshape(tile_shape), grad_obs, *sums)


def solution(mesh):
    in_specs = (
        P("lat", "lon", None),
        P(("lat", "lon"), None, None),
        P(("lat", "lon"), None),
        P(("lat", "lon"), None),
        P(),
        P(),
        P(),
        P(),
        P(),
        P("lat", "lon", None),
    )
    out_specs = (
        P("lat", "lon", None),
        P("lat", "lon", None),
        P(("lat", "lon"), None, None),
        P(),
        P(),
        P(),
        P(),
        P(),
    )
    return jax.shard_map(
        on_device, mesh=mesh, in_specs=in_specs, out_specs=out_specs, check_vma=False
    )
```

```python
import functools

import jax
import jax.numpy as jnp
from jax import lax
from jax.experimental import pallas as pl
from jax.experimental.pallas import tpu as pltpu
from jax.sharding import PartitionSpec as P

D = 512
HEADS = 8
HD = D // HEADS
BLK = 128
CAP = 2
ROWS = CAP * BLK
CELLS = 256
TILE = 16
VROWS = HD + 16
SCALING = HD ** (-0.5)
MESH = pl.DeviceIdType.MESH
SIDE = 4
STEPS = (
    (0, 0), (0, 1), (0, 3), (1, 0), (3, 0),
    (0, 2), (2, 0), (1, 2), (3, 2), (2, 1), (2, 3), (2, 2),
    (1, 1), (1, 3), (3, 1), (3, 3),
)
FAR = range(5, 12)
DIAGONAL = range(12, 16)
BACK = (6, 5, 4, 3, 8, 7, 2, 1)
EXTRA = 16
BF = jnp.bfloat16
F32 = jnp.float32


def dot(a, b):
    return jnp.dot(a, b, preferred_element_type=F32)


def dot_nt(a, b):
    return lax.dot_general(a, b, (((1,), (1,)), ((), ())), preferred_element_type=F32)


def onehot(rows, cols, hit):
    at = [lax.broadcasted_iota(jnp.int32, (rows, cols), k) for k in range(2)]
    return jnp.where(hit(*at), 1.0, 0.0).astype(BF)


def around(cells, halo, first, last):
    top = jnp.where(first, 0.0, halo[0].astype(F32)).astype(BF)
    bottom = jnp.where(last, 0.0, halo[1].astype(F32)).astype(BF)
    side = TILE
    west = dot(onehot(CELLS, CELLS, lambda q, k: (k == q - 1) & (lax.rem(q, side) != 0)), cells)
    west = west + dot(onehot(CELLS, side, lambda q, k: q == k * side), halo[2])
    east = dot(onehot(CELLS, CELLS, lambda q, k: (k == q + 1) & (lax.rem(q, side) != side - 1)), cells)
    east = east + dot(onehot(CELLS, side, lambda q, k: q == k * side + side - 1), halo[3])
    return (
        jnp.concatenate([top, cells[:-side]], 0).astype(F32),
        jnp.concatenate([cells[side:], bottom], 0).astype(F32),
        west,
        east,
    )


def edges(cells, out):
    out[0] = cells[CELLS - TILE :]
    out[1] = cells[:TILE]
    out[2] = dot(onehot(TILE, CELLS, lambda k, q: q == k * TILE + TILE - 1), cells).astype(BF)
    out[3] = dot(onehot(TILE, CELLS, lambda k, q: q == k * TILE), cells).astype(BF)


class Exchange:
    def __init__(self, group, copy, every):
        self.count, self.me, self.peers, _ = group
        self.copy, self.every = copy, every

    def start(self):
        for at in self.peers:
            self.copy(at).start()

    def wait(self):
        self.every.wait_recv()

    def sent(self):
        self.every.wait_send()


def exchange(group, pieces, dst, ssem, rsem):
    count, me, peers, whom = group

    def copy(src, into, to):
        return pltpu.make_async_remote_copy(
            src_ref=src, dst_ref=into, send_sem=ssem, recv_sem=rsem, device_id=whom(to),
            device_id_type=MESH)

    whole = dst.at[pl.ds(0, count - 1)]
    return Exchange(group, lambda to: copy(pieces(to), dst.at[me], to), copy(whole, whole, peers[0]))


def scatter(group, src, dst, ssem, rsem):
    return exchange(group, lambda to: src.at[to], dst, ssem, rsem)


def gather(group, buf, ssem, rsem):
    return exchange(group, lambda to: buf.at[group[1]], buf, ssem, rsem)


class MatrixSum:
    def __init__(self, groups, buffers, sems, out):
        self.me = [group[1] for group in groups]
        self.bufs = buffers
        self.out = out
        at, self.stages = out, []
        for k, group in enumerate(groups):
            self.stages.append(scatter(group, buffers[2 * k], buffers[2 * k + 1], *sems[2 * k : 2 * k + 2]))
        for k, group in enumerate(groups):
            self.stages.insert(4, gather(group, at, *sems[8 + 2 * k : 10 + 2 * k]))
            at = at.at[group[1]]
        self.place = at

    def load(self, source):
        per = D // 256
        for c in range(2):
            for x in range(4):
                f = 4 * c + x
                rows = slice((f % per) * 256, (f % per + 1) * 256)
                cols = slice((f // per) * 128, (f // per + 1) * 128)
                self.bufs[0][c, x] = source(rows, cols).astype(BF).reshape(4, 4, 16, 128)

    def begin(self):
        self.stages[0].start()

    def step(self, stage):
        self.stages[stage].wait()
        if stage < 4:
            me = self.me[stage]
            own, got = self.bufs[2 * stage], self.bufs[2 * stage + 1]
            held = own[me].astype(F32)
            for at in self.stages[stage].peers:
                held = held + got[at].astype(F32)
            target = self.place if stage == 3 else self.bufs[2 * stage + 2]
            target[...] = held.astype(BF)
        if stage < 7:
            self.stages[stage + 1].start()
        self.stages[stage].sent()


class TapSum:
    def __init__(self, groups, buffers, sems):
        self.bufs = buffers
        self.stages = [
            gather(group, buffers[k], *sems[2 * k : 2 * k + 2]) for k, group in enumerate(groups)
        ]

    def begin(self):
        self.stages[0].start()

    def step(self, stage, out=None):
        self.stages[stage].wait()
        total = self.bufs[stage][0]
        for k in range(1, self.stages[stage].count):
            total = total + self.bufs[stage][k]
        if stage == 3:
            out[...] = total
        else:
            self.bufs[stage + 1][self.stages[stage + 1].me] = total
            self.stages[stage + 1].start()
        self.stages[stage].sent()


def kernel(
    nlat, n, dest_ref, count_ref, grid_ref, cot_ref, sten_ref, obs_in, wq_in, wk_in, wv_in, wo_in,
    enc_out, gobs_out, ggrid_out, late_ref, early_ref, taps_ref,
    send, xs, ret, relay, relay_back, kv, kt, vt, bias, wkv, qt, qzt, dozt, dot_t,
    acc_o, acc_q, m_ref, l_ref, d_ref, dkvt, dwt, gm_ref, mid_ref, sides, edge, halo,
    obs_ref, wq_ref, wo_ref, enc_ref, gobs_ref, ggrid_ref, in_sem, out_sem,
    x_ssem, x_rsem, r_ssem, r_rsem, g_ssem, g_rsem, b_ssem, b_rsem, h_ssem, h_rsem,
    *sum_scratch,
):
    lat, me = lax.axis_index("lat"), lax.axis_index("lon")
    groups = n // 2
    blocks = obs_ref.shape[0]
    loads = [
        pltpu.make_async_copy(source, target, in_sem.at[k])
        for k, (source, target) in enumerate((
            (obs_in, obs_ref), (wq_in, wq_ref), (wk_in, wkv.at[:, pl.ds(0, D)]),
            (wv_in, wkv.at[:, pl.ds(D, D)]), (wo_in, wo_ref)))
    ]
    stores = [
        pltpu.make_async_copy(source, target, out_sem.at[k])
        for k, (source, target) in enumerate((
            (ggrid_ref, ggrid_out), (enc_ref, enc_out), (gobs_ref, gobs_out)))
    ]
    x_at, core = lat // 2, lax.rem(lat, 2)
    y, z = me // SIDE, lax.rem(me, SIDE)

    def ring(me, whom):
        return SIDE, me, [lax.rem(me + o, SIDE) for o in range(1, SIDE)], whom

    on_core = (2, core, [1 - core], lambda at: {"lat": 2 * x_at + at})
    on_x = ring(x_at, lambda at: {"lat": 2 * at + core})
    on_y = ring(y, lambda at: {"lon": at * SIDE + z})
    on_z = ring(z, lambda at: {"lon": y * SIDE + at})
    orders = ((on_x, on_y, on_z), (on_y, on_z, on_x), (on_z, on_x, on_y), (on_x, on_y, on_z))
    *late, early = (
        MatrixSum(
            (on_core, *order), sum_scratch[24 * k : 24 * k + 8], sum_scratch[24 * k + 8 : 24 * k + 24],
            late_ref.at[k] if k < 3 else early_ref)
        for k, order in enumerate(orders)
    )
    tap_sum = TapSum((on_core, on_x, on_y, on_z), sum_scratch[96:100], sum_scratch[100:108])

    way_y, way_z = 1 - 2 * lax.rem(y, 2), 1 - 2 * lax.rem(z, 2)

    def place(dy, dz):
        return lax.rem(y + dy + 2 * SIDE, SIDE) * SIDE + lax.rem(z + dz + 2 * SIDE, SIDE)

    def turned(i):
        return 1 if STEPS[i] in ((0, 2), (2, 0), (2, 2)) else -1

    def leg(i, sign):
        dy, dz = STEPS[i]
        return {"lon": place(
            turned(i) * way_y if dy == 2 else sign * dy, turned(i) * way_z if dz == 2 else sign * dz)}

    def onward(i):
        dy, dz = STEPS[i]
        return {"lon": place(
            -turned(i) * way_y if dy == 2 else 0, -turned(i) * way_z if dz == 2 else 0)}

    for load in loads:
        load.start()
    barrier = pltpu.get_barrier_semaphore()
    def greet(o, carry, axis, count, at):
        pl.semaphore_signal(
            barrier, inc=1, device_id={axis: lax.rem(at + o, count)}, device_id_type=MESH)
        return carry

    lax.fori_loop(1, nlat, functools.partial(greet, axis="lat", count=nlat, at=lat), 0)
    lax.fori_loop(1, n, functools.partial(greet, axis="lon", count=n, at=me), 0)

    row_ids = lax.broadcasted_iota(jnp.int32, (EXTRA, D), 0)

    def pack(i):
        tile = place(*STEPS[i])
        number = b0 = b1 = c0 = c1 = jnp.int32(0)
        for b in range(blocks):
            hit = dest_ref[0, b] == tile
            one, two = hit & (number == 0), hit & (number == 1)
            number = number + hit.astype(jnp.int32)
            b0, b1 = jnp.where(one, b, b0), jnp.where(two, b, b1)
            c0, c1 = jnp.where(one, count_ref[0, b], c0), jnp.where(two, count_ref[0, b], c1)
        send[i, 0:BLK, :] = obs_ref[b0]
        send[i, BLK:ROWS, :] = obs_ref[b1]
        send[i, ROWS:, :] = jnp.where(row_ids == 0, c0, c1).astype(F32).astype(BF)

    edges(cot_ref[...], edge.at[0])
    loads[0].wait()
    pl.semaphore_wait(barrier, nlat + n - 2)

    def remote(src, dst, ssem, rsem, whom):
        return pltpu.make_async_remote_copy(
            src_ref=src, dst_ref=dst, send_sem=ssem, recv_sem=rsem, device_id=whom, device_id_type=MESH)

    def x_copy(i):
        if i not in FAR:
            return remote(send.at[i], xs.at[i + 1], x_ssem.at[i], x_rsem.at[i], leg(i, 1))
        j = i - FAR.start
        return remote(send.at[i], relay.at[j], x_ssem.at[i], r_rsem.at[j], leg(i, 1))

    def x_onward(i):
        j = i - FAR.start
        return remote(relay.at[j], xs.at[i + 1], r_ssem.at[j], x_rsem.at[i], onward(i))

    def g_copy(i):
        tokens = send.at[i, pl.ds(0, ROWS)]
        if i not in FAR:
            return remote(tokens, ret.at[i], g_ssem.at[i], g_rsem.at[i], leg(i, -1))
        j = i - FAR.start
        return remote(tokens, relay_back.at[j], g_ssem.at[i], b_rsem.at[j], leg(i, -1))

    def g_onward(i):
        j = i - FAR.start
        return remote(relay_back.at[j], ret.at[i], b_ssem.at[j], g_rsem.at[i], onward(i))

    def x_arrived(i):
        remote(send.at[0], xs.at[i + 1], x_ssem.at[0], x_rsem.at[i], {"lon": me}).wait_recv()

    def h_copies(which):
        whom = (
            {"lat": lax.rem(lat + 1, nlat)}, {"lat": lax.rem(lat + nlat - 1, nlat)},
            {"lon": lax.rem(me + 1, n)}, {"lon": lax.rem(me + n - 1, n)},
        )
        return [
            remote(edge.at[which, k], halo.at[which, k], h_ssem.at[which, k], h_rsem.at[which, k], whom[k])
            for k in range(4)
        ]

    for copy in h_copies(0):
        copy.start()

    for i in (*FAR, *range(1, FAR.start)):
        pack(i)
        x_copy(i).start()
    pack(0)

    xs[0, 0:ROWS, :] = grid_ref[...]
    xs[1] = send[0]
    for load in loads[1:]:
        load.wait()
    lanes = lax.broadcasted_iota(jnp.int32, (CELLS, 2 * HD), 1)
    queries = dot(grid_ref[...], wq_ref[...]).astype(BF).astype(F32) * SCALING
    for copy in h_copies(0):
        copy.wait_recv()
    up = cot_ref[...].astype(F32)
    around_up = around(cot_ref[...], halo.at[0], lat == 0, lat == nlat - 1)
    for k in range(4):
        sides[k] = around_up[k].astype(BF)
    up_north, up_south, up_west, up_east = around_up
    gm_ref[...] = (
        (1.0 + sten_ref[0:1, :]) * up + sten_ref[1:2, :] * up_south + sten_ref[2:3, :] * up_north
        + sten_ref[3:4, :] * up_east + sten_ref[4:5, :] * up_west
    ).astype(BF)
    ups = dot_nt(gm_ref[...], wo_ref[...]).astype(BF).astype(F32)
    dot_t[...] = ups.T.astype(BF)
    qt[...] = queries.T.astype(BF)
    for h in range(HEADS):
        p, e = h // 2, h % 2
        mine = (lanes >= HD) if e else (lanes < HD)
        picked = jnp.where(mine, queries[:, p * 2 * HD : (p + 1) * 2 * HD], 0.0)
        qzt[h] = picked.T.astype(BF)
        picked = jnp.where(mine, ups[:, p * 2 * HD : (p + 1) * 2 * HD], 0.0)
        dozt[h] = picked.T.astype(BF)
    acc_o[...] = jnp.zeros_like(acc_o)
    acc_q[...] = jnp.zeros_like(acc_q)
    dwt[...] = jnp.zeros_like(dwt)
    m_ref[...] = jnp.full(m_ref.shape, -1e30, F32)
    l_ref[...] = jnp.zeros_like(l_ref)
    for h in range(HEADS):
        vt[h * VROWS + HD : (h + 1) * VROWS, :] = jnp.ones((VROWS - HD, 2 * ROWS), BF)
    key_ids = lax.broadcasted_iota(jnp.int32, (BLK, 128), 0).astype(F32)

    def masked(width):
        part = bias[0:width, :]
        return jnp.concatenate([part, part], 1)

    def mark(c, w):
        if w == 1:
            bias[0:ROWS, :] = jnp.zeros((ROWS, 128), F32)
            return
        for k in range(w):
            tile = xs[c + k, ROWS:, 0:128].astype(F32)
            for r in range(CAP):
                at = k * ROWS + r * BLK
                bias[at : at + BLK, :] = jnp.where(key_ids < tile[r : r + 1, :], 0.0, -1e30)

    def project(c, w, g):
        width = w * ROWS
        rows = pl.ds(pl.multiple_of(c * ROWS, ROWS), width)
        tokens = xs[pl.ds(c, w), 0:ROWS, :].reshape(width, D)
        for j in range(4):
            cols = slice(j * 256, (j + 1) * 256)
            part = dot(tokens, wkv[:, cols]).astype(BF)
            kv[rows, cols] = part
            if j < 2:
                kt[g, cols, :width] = part.T
            else:
                turned_part = part.T
                for e in range(4):
                    h = (j - 2) * 4 + e
                    vt[h * VROWS : h * VROWS + HD, :width] = turned_part[e * HD : (e + 1) * HD, :]

    def attend(c, w):
        width = w * ROWS
        mark(c, w)
        rows = pl.ds(pl.multiple_of(c * ROWS, ROWS), width)

        for h in range(HEADS):
            mine = slice(h * HD, (h + 1) * HD)
            here = slice((h // 2) * 128, (h // 2 + 1) * 128)
            scores = dot(kv[rows, here], qzt[h]) + masked(width)
            old = m_ref[h]
            new = jnp.maximum(old, jnp.max(scores, 0, keepdims=True))
            raised = jnp.exp(scores - new).astype(BF)
            shrink = jnp.exp(old - new)
            mixed = dot(vt[h * VROWS : (h + 1) * VROWS, :width], raised)
            l_ref[h] = l_ref[h] * shrink + mixed[HD : HD + 1, :]
            m_ref[h] = new
            acc_o[mine, :] = acc_o[mine, :] * shrink + mixed[:HD, :]

    project(0, 1, 0)
    attend(0, 1)

    for i in FAR:
        x_copy(i).wait_recv()
        x_onward(i).start()

    for i in DIAGONAL:
        pack(i)

    def forward(step, carry):
        g = step + 1
        c = CAP * g - 1

        @pl.when(step == 2)
        def _():
            for i in FAR:
                x_onward(i).wait_send()
            for i in DIAGONAL:
                x_copy(i).start()

        @pl.when(step >= 1)
        def _():
            x_arrived(c - 1)

        x_arrived(c)
        project(c, 2, g)
        attend(c, 2)
        return carry

    lax.fori_loop(0, groups, forward, 0)

    def up_of():
        return cot_ref[...].astype(F32)

    def finish(h, carry):
        rows = pl.ds(pl.multiple_of(h * HD, HD), HD)
        total = l_ref[h]
        mixed = acc_o[rows, :] / total
        acc_o[rows, :] = mixed
        m_ref[h] = m_ref[h] + jnp.log(total)
        d_ref[h] = jnp.sum(mixed * dot_t[rows, :].astype(F32), 0, keepdims=True)
        return carry

    lax.fori_loop(0, HEADS, finish, 0)
    def middle():
        mid_ref[...] = (
            grid_ref[...].astype(F32) + dot(acc_o[...].T.astype(BF), wo_ref[...])
        ).astype(BF)
        edges(mid_ref[...], edge.at[1])
        for copy in h_copies(1):
            copy.start()
        centre = mid_ref[...].astype(F32)
        terms = tap_sum.bufs[0]
        terms[core] = jnp.zeros((8, D), F32)
        for row, side in enumerate((up_of(), *(sides[k].astype(F32) for k in (1, 0, 3, 2)))):
            terms[core, row : row + 1, :] = jnp.sum(centre * side, 0, keepdims=True)
        tap_sum.begin()
        attended = acc_o[...].astype(BF)
        early.load(lambda rows, cols: dot(attended[rows, :], gm_ref[:, cols]))
        early.begin()

    for i in range(1, n):
        x_copy(i).wait_send()

    def differentiate(c, w, g, half):
        width = w * ROWS
        lanes = pl.ds(pl.multiple_of(half * 2 * ROWS, 2 * ROWS), width)
        mark(c, w)
        rows = pl.ds(pl.multiple_of(c * ROWS, ROWS), width)

        def four(q, carry):
            for e in range(4):
                h = 4 * q + e
                pair = (2 * q + e // 2) * 128
                mine = pl.ds(pl.multiple_of(h * HD, HD), HD)
                also = pl.ds(pl.multiple_of(D + h * HD, HD), HD)
                keys = kv[rows, pl.ds(pl.multiple_of(pair, 128), 128)]
                values = kv[rows, pl.ds(pl.multiple_of(D + pair, 128), 128)]
                weights = jnp.exp(dot(keys, qzt[h]) + masked(width) - m_ref[h])
                grads = (weights * (dot(values, dozt[h]) - d_ref[h])).astype(BF)
                dkvt[mine, lanes] = dot_nt(qt[mine, :], grads).astype(BF)
                dkvt[also, lanes] = dot_nt(dot_t[mine, :], weights.astype(BF)).astype(BF)
                acc_q[mine, :] += dot(kt[g, mine, :width], grads)
            return carry

        lax.fori_loop(0, HEADS // 4, four, 0)

    def accumulate(c, w):
        width = w * ROWS

        def weigh(j, carry):
            part = pl.ds(pl.multiple_of(j * 256, 256), 256)
            tokens = xs[pl.ds(c, w), 0:ROWS, :].reshape(width, D)
            dwt[part, :] += dot(dkvt[part, :width], tokens)
            return carry

        lax.fori_loop(0, 4, weigh, 0)

    def forward_back(k):
        for i in (CAP * BACK[k] - 2, CAP * BACK[k] - 1):
            if i in FAR:
                g_copy(i).wait_recv()
                g_onward(i).start()

    def backward(step, carry):
        g = 6 - step + 6 * ((step + 4) // 8) - 4 * ((step + 2) // 8)
        half = 1 - lax.rem(step, 2)
        differentiate(CAP * g - 1, 2, g, half)
        lanes = pl.ds(pl.multiple_of(half * 2 * ROWS, 2 * ROWS), 2 * ROWS)

        def turn(j, inner):
            cols = pl.ds(pl.multiple_of(j * 256, 256), 256)
            part = dot(wkv[cols, :], dkvt[:, lanes]).astype(BF).T
            send[pl.ds(CAP * g - 2, 2), 0:ROWS, cols] = part.reshape(2, ROWS, 256)
            return inner

        lax.fori_loop(0, 2, turn, 0)
        for k in range(groups):
            @pl.when(step == k)
            def _(k=k):
                first = CAP * BACK[k] - 2
                if first:
                    g_copy(first).start()
                else:
                    ret[0] = send[0, 0:ROWS, :]
                g_copy(first + 1).start()
                if k >= 6:
                    forward_back(k - 6)

        @pl.when(half == 0)
        def _():
            accumulate(CAP * g - 1, 4)

        pl.when(step == 0)(middle)

        for stage in range(2):
            pl.when(step == 2 * stage + 2)(functools.partial(early.step, stage))
            pl.when(step == 2 * stage + 3)(functools.partial(tap_sum.step, stage))

        return carry

    lax.fori_loop(0, groups, backward, 0)
    forward_back(2)
    forward_back(3)
    differentiate(0, 1, 0, 0)
    accumulate(0, 1)

    late[1].load(lambda rows, cols: dwt[cols, rows].astype(BF).T)
    late[1].begin()
    late[2].load(lambda rows, cols: dwt[D + cols.start : D + cols.stop, rows].astype(BF).T)
    late[2].begin()
    grad_q = (acc_q[...].T * SCALING).astype(BF)
    dwq = dot(grid_ref[...].T, grad_q)
    late[0].load(lambda rows, cols: dwq[rows, cols])
    late[0].begin()
    tap_sum.step(2)

    def late_step(stage):
        if stage < 6:
            early.step(stage + 2)
        for part in (late[1], late[2], late[0]):
            part.step(stage)

    ggrid_ref[...] = (
        gm_ref[...].astype(F32) + dot_nt(grad_q, wq_ref[...])
        + dot(wkv[...], dkvt[:, :CELLS]).T
    ).astype(BF)
    stores[0].start()
    late_step(0)
    for copy in h_copies(1):
        copy.wait_recv()
    north, south, west, east = around(mid_ref[...], halo.at[1], lat == 0, lat == nlat - 1)
    enc_ref[...] = (
        (1.0 + sten_ref[0:1, :]) * mid_ref[...].astype(F32) + sten_ref[1:2, :] * north
        + sten_ref[2:3, :] * south + sten_ref[3:4, :] * west + sten_ref[4:5, :] * east
    ).astype(BF)
    stores[1].start()
    late_step(1)
    late_step(2)
    late_step(3)
    tap_sum.step(3, taps_ref)
    late_step(4)
    late_step(5)
    for i in range(1, n):
        if i not in FAR:
            g_copy(i).wait_recv()
        else:
            g_onward(i).wait_recv()
        g_copy(i).wait_send()
        if i in FAR:
            g_onward(i).wait_send()


    def unpack(b, carry):
        tile = dest_ref[0, b]
        rank = jnp.int32(0)
        for other in range(blocks):
            rank = rank + ((dest_ref[0, other] == tile) & (other < b)).astype(jnp.int32)
        dy = lax.rem(tile // SIDE - y + SIDE, SIDE)
        dz = lax.rem(lax.rem(tile, SIDE) - z + SIDE, SIDE)
        at = jnp.int32(0)
        for i, (sy, sz) in enumerate(STEPS):
            at = jnp.where((dy == sy) & (dz == sz), i, at)
        both = ret[at]
        gobs_ref[b] = jnp.where(rank == 0, both[:BLK], both[BLK:])
        return carry

    lax.fori_loop(0, blocks, unpack, 0)
    stores[2].start()
    late_step(6)
    late_step(7)
    for which in range(2):
        for copy in h_copies(which):
            copy.wait_send()
    for copy in stores:
        copy.wait()


def write_kernel(
    enc, gobs, ggrid, late, early, taps, enc_o, gobs_o, ggrid_o, wq, wk, wv, wo, taps_o,
    enc_v, gobs_v, ggrid_v, late_v, early_v, sums_v, in_sems, out_sems,
):
    part = gobs.shape[0] // 4
    loads, stores = [], []

    def load(source, target):
        loads.append(pltpu.make_async_copy(source, target, in_sems.at[len(loads)]))
        loads[-1].start()

    def store(source, out):
        stores.append(pltpu.make_async_copy(source, out, out_sems.at[len(stores)]))
        stores[-1].start()

    load(early, early_v)
    for k in range(3):
        load(late.at[k], late_v.at[k])
    for k in range(4):
        load(gobs.at[pl.ds(k * part, part)], gobs_v.at[pl.ds(k * part, part)])
    load(enc, enc_v)
    load(ggrid, ggrid_v)
    taps_o[...] = taps[0:5, :]
    for k, (out, source) in enumerate(
            ((wo, early_v), (wq, late_v.at[0]), (wk, late_v.at[1]), (wv, late_v.at[2]))):
        loads[k].wait()
        for f in range(8):
            rows, cols = slice((f % 2) * 256, (f % 2 + 1) * 256), slice((f // 2) * 128, (f // 2 + 1) * 128)
            sums_v[k, rows, cols] = source[f // 4, f % 4].reshape(256, 128).astype(F32)
        store(sums_v.at[k], out)
    for k in range(4):
        loads[4 + k].wait()
        store(gobs_v.at[pl.ds(k * part, part)], gobs_o.at[pl.ds(k * part, part)])
    loads[8].wait()
    store(enc_v, enc_o)
    loads[9].wait()
    store(ggrid_v, ggrid_o)
    for copy in stores:
        copy.wait()


def on_device(
    grid_tokens, obs_tokens, destinations, valid_counts, w_query, w_key, w_value, w_out,
    stencil_taps, cotangent,
):
    tile_shape = grid_tokens.shape
    blocks = obs_tokens.shape[0]
    nlat, n = lax.axis_size("lat"), lax.axis_size("lon")
    vmem = pl.BlockSpec(memory_space=pltpu.VMEM)
    smem = pl.BlockSpec(memory_space=pltpu.SMEM)
    anywhere = pl.BlockSpec(memory_space=pl.ANY)
    lon_sem = pltpu.SemaphoreType.DMA((n,))
    far_sem = pltpu.SemaphoreType.DMA((len(FAR),))
    halo_sem = pltpu.SemaphoreType.DMA((2, 4))
    sems = [pltpu.SemaphoreType.DMA] * 8
    sums = []
    for _ in range(4):
        for lead in ((2, SIDE, SIDE, SIDE), (SIDE,) * 3, (SIDE,) * 2, (SIDE,)):
            sums += [pltpu.VMEM((*lead, 16, 128), BF)] * 2
        sums += sems * 2
    sums += [pltpu.VMEM((2, 8, D), F32)] + [pltpu.VMEM((SIDE, 8, D), F32)] * 3 + sems
    tile = jax.ShapeDtypeStruct((CELLS, D), BF)
    results = pl.pallas_call(
        functools.partial(kernel, nlat, n),
        out_shape=(
            tile, jax.ShapeDtypeStruct((blocks, BLK, D), BF), tile,
            jax.ShapeDtypeStruct((3, 2, SIDE, SIDE, SIDE, 16, 128), BF),
            jax.ShapeDtypeStruct((2, SIDE, SIDE, SIDE, 16, 128), BF),
            jax.ShapeDtypeStruct((8, D), F32),
        ),
        in_specs=[smem] * 2 + [vmem] * 3 + [anywhere] * 5,
        out_specs=(anywhere,) * 3 + (vmem,) * 3,
        scratch_shapes=[
            pltpu.VMEM((n, ROWS + EXTRA, D), BF),
            pltpu.VMEM((n + 1, ROWS + EXTRA, D), BF),
            pltpu.VMEM((n, ROWS, D), BF),
            pltpu.VMEM((len(FAR), ROWS + EXTRA, D), BF),
            pltpu.VMEM((len(FAR), ROWS, D), BF),
            pltpu.VMEM(((n + 1) * ROWS, 2 * D), BF),
            pltpu.VMEM((n // 2 + 1, D, 2 * ROWS), BF),
            pltpu.VMEM((HEADS * VROWS, 2 * ROWS), BF),
            pltpu.VMEM((2 * ROWS, 128), F32),
            pltpu.VMEM((D, 2 * D), BF),
            pltpu.VMEM((D, CELLS), BF),
            pltpu.VMEM((HEADS, 2 * HD, CELLS), BF),
            pltpu.VMEM((HEADS, 2 * HD, CELLS), BF),
            pltpu.VMEM((D, CELLS), BF),
            pltpu.VMEM((D, CELLS), F32),
            pltpu.VMEM((D, CELLS), F32),
            pltpu.VMEM((HEADS, 1, CELLS), F32),
            pltpu.VMEM((HEADS, 1, CELLS), F32),
            pltpu.VMEM((HEADS, 1, CELLS), F32),
            pltpu.VMEM((2 * D, 4 * ROWS), BF),
            pltpu.VMEM((2 * D, D), F32),
            pltpu.VMEM((CELLS, D), BF),
            pltpu.VMEM((CELLS, D), BF),
            pltpu.VMEM((4, CELLS, D), BF),
            pltpu.VMEM((2, 4, TILE, D), BF),
            pltpu.VMEM((2, 4, TILE, D), BF),
            pltpu.VMEM((blocks, BLK, D), BF),
            pltpu.VMEM((D, D), BF),
            pltpu.VMEM((D, D), BF),
            pltpu.VMEM((CELLS, D), BF),
            pltpu.VMEM((blocks, BLK, D), BF),
            pltpu.VMEM((CELLS, D), BF),
            pltpu.SemaphoreType.DMA((5,)),
            pltpu.SemaphoreType.DMA((3,)),
            lon_sem, lon_sem, far_sem, far_sem, lon_sem, lon_sem, far_sem, far_sem, halo_sem, halo_sem,
            *sums,
        ],
        compiler_params=pltpu.CompilerParams(
            collective_id=0, has_side_effects=True, vmem_limit_bytes=62 * 2**20
        ),
        name="encoder_step",
    )(
        destinations.reshape(1, blocks), valid_counts, grid_tokens.reshape(CELLS, D),
        cotangent.reshape(CELLS, D), stencil_taps, obs_tokens, w_query, w_key, w_value, w_out,
    )
    matrix = jax.ShapeDtypeStruct((D, D), F32)
    encoded, grad_obs, grad_grid, *sums = pl.pallas_call(
        write_kernel,
        out_shape=(
            tile, jax.ShapeDtypeStruct((blocks, BLK, D), BF), tile, matrix, matrix, matrix, matrix,
            jax.ShapeDtypeStruct((5, D), F32),
        ),
        in_specs=[anywhere] * 5 + [vmem],
        out_specs=(anywhere,) * 7 + (vmem,),
        scratch_shapes=[
            pltpu.VMEM((CELLS, D), BF), pltpu.VMEM((blocks, BLK, D), BF), pltpu.VMEM((CELLS, D), BF),
            pltpu.VMEM((3, 2, SIDE, SIDE, SIDE, 16, 128), BF), pltpu.VMEM((2, SIDE, SIDE, SIDE, 16, 128), BF),
            pltpu.VMEM((4, D, D), F32), pltpu.SemaphoreType.DMA((10,)), pltpu.SemaphoreType.DMA((10,)),
        ],
        compiler_params=pltpu.CompilerParams(vmem_limit_bytes=62 * 2**20),
        name="write_results",
    )(*results)
    return (encoded.reshape(tile_shape), grad_grid.reshape(tile_shape), grad_obs, *sums)


def solution(mesh):
    in_specs = (
        P("lat", "lon", None),
        P(("lat", "lon"), None, None),
        P(("lat", "lon"), None),
        P(("lat", "lon"), None),
        P(),
        P(),
        P(),
        P(),
        P(),
        P("lat", "lon", None),
    )
    out_specs = (
        P("lat", "lon", None),
        P("lat", "lon", None),
        P(("lat", "lon"), None, None),
        P(),
        P(),
        P(),
        P(),
        P(),
    )
    return jax.shard_map(
        on_device, mesh=mesh, in_specs=in_specs, out_specs=out_specs, check_vma=False
    )
```
